128 devices in a mesh: dev: 128 (over y, x, z, core).
Axes of the slice: x: 4, y: 4, z: 4, core: 2. Of those that a mesh axis runs over, the one named last changes fastest.
Arguments:
- tokens: bfloat16 [131072, 384], P('dev'), may hold values from -6 to 6
- cond: bfloat16 [512, 384], P('dev'), may hold values from -6 to 6
- params: bfloat16 [2659584], P('dev'), may hold values from -4 to 4, as said below
- d_out: bfloat16 [131072, 384], P('dev'), may hold values from -6 to 6
Outputs:
- output: bfloat16 [131072, 384], P('dev')
- d_tokens: float32 [131072, 384], P('dev')
- d_cond: float32 [512, 384], P('dev')
- d_params: float32 [2659584], P('dev')
The draws below stay inside these ranges and needn't reach their ends.
Inputs may be any that keep to these rules, and one draw needn't show every extreme that they name: `params`: the weights and biases of the block in the layout of the steps, then padding.
All inputs are finite; a program needn't handle non-finite values.
Results may differ from the reference program's by a relative error of at most 0.0085.
The reference program's roundings to bfloat16 on the way count: a program that leaves them out, or rounds other values in their place, can miss the bound.
Values may be sent and summed in bfloat16 or wider, within the bound.
A program may use at most 128 MiB of HBM per device.

```python
import math
import jax
import jax.numpy as jnp
from jax import lax

D = 384
FF = 1536
HEADS = 6
SEQ = 256
HEAD_DIM = 64
LAT = 512
TOKENS = 131072
PARAMS = 2659584
PADDED = 2659584


def draw_params(key, part):
    key = jax.random.fold_in(key, 7)
    pieces = [(D * 6 * D, D ** (-0.5)), (6 * D, 0.5), (D * 3 * D, D ** (-0.5)), (2 * D, 0.5), (D * D, (D / 8.0) ** (-0.5)), (D, 0.5), (D * FF, D ** (-0.5)), (FF, 0.5), (FF * D, FF ** (-0.5)), (D, 0.5), (PADDED - PARAMS, 1.0)]
    scales = jnp.concatenate([jnp.full((amount,), factor, jnp.float32) for amount, factor in pieces])
    base = jnp.clip(jax.random.normal(key, (PADDED,), jnp.float32), -4.0, 4.0)
    return (base * scales).astype(jnp.bfloat16)


def levels(rng, shape, split, smallest, high):
    factor_of, own = 1.0, jax.random.fold_in(rng, 6)
    for dim, blocks in split:
        draws = jnp.exp(jax.random.uniform(jax.random.fold_in(own, dim), (blocks,), jnp.float32, smallest / len(split), high / len(split)))
        factor_of = factor_of * jnp.repeat(draws, shape[dim] // blocks).reshape([-1 if axis == dim else 1 for axis in range(len(shape))])
    return factor_of


def gaussian(own_key, shape, deviation, reach, shards=(), dtype=jnp.bfloat16):
    array = jax.random.normal(own_key, shape, jnp.float32) * deviation
    if len(shards) > 0:
        array = levels(own_key, shape, shards, -0.22, 0.18) * array
    return jnp.clip(array, min=-reach, max=reach).astype(dtype)


def setup_inputs(seed: int = 0) -> dict:
    key_list = jax.random.split(jax.random.key(seed), 5)
    return {
        "tokens": gaussian(key_list[0], (TOKENS, D), 1.0, 6.0, ((0, 128),)),
        "cond": gaussian(key_list[1], (LAT, D), 1.0, 6.0, ((0, 128),)),
        "params": draw_params(jax.random.fold_in(key_list[4], 71), 0),
        "d_out": gaussian(key_list[3], (TOKENS, D), 1.0, 6.0, ((0, 128),)),
    }


@jax.custom_vjp
def low(v):
    return lax.optimization_barrier(v.astype(jnp.bfloat16)).astype(jnp.float32)

@jax.custom_vjp
def low_back(v):
    return v

def low_keep(v):
    return (low(v), None)

def low_pass(kept, grad):
    return (grad,)

def back_keep(v):
    return (v, None)

def back_low(kept, grad):
    return (low(grad),)
low.defvjp(low_keep, low_pass)
low_back.defvjp(back_keep, back_low)

def unpack(flat):
    layout = [(D, 6 * D), (6 * D,), (D, 3 * D), (2 * D,), (D, D), (D,), (D, FF), (FF,), (FF, D), (D,)]
    pieces = []
    offset = 0
    for extent in layout:
        amount = math.prod(extent)
        pieces.append(flat[offset:offset + amount].reshape(extent))
        offset = offset + amount
    return pieces

def normalize(values):
    centered = values - lax.optimization_barrier(jnp.mean(values, axis=-1, keepdims=True))
    inverse = lax.rsqrt(lax.optimization_barrier(jnp.mean(centered * centered, axis=-1, keepdims=True)) + 1e-06)
    return centered * inverse

def matmul(left, right):
    return jnp.einsum('gsd,de->gse', left, right, precision=lax.Precision.HIGHEST)

def layer(flat, inputs, conds):
    w_ada, b_ada, w_qkv, b_qv, w_proj, b_proj, w_up, b_up, w_down, b_down = unpack(flat)
    group = inputs.shape[0]
    silu_low = low(jax.nn.silu(conds))
    modulation = low_back(jnp.dot(silu_low, w_ada, precision=lax.Precision.HIGHEST) + b_ada)
    parts = [modulation[:, None, number * D:(number + 1) * D] for number in range(6)]
    shift_attn, scale_attn, gate_attn, shift_mlp, scale_mlp, gate_mlp = parts
    normed_one = normalize(inputs)
    attn_in = low(normed_one * (1.0 + scale_attn) + shift_attn)
    bias_qkv = jnp.concatenate([b_qv[:D], jnp.zeros((D,), jnp.float32), b_qv[D:]])
    projected = low(low_back(matmul(attn_in, w_qkv) + bias_qkv))
    projected = projected.reshape(group, SEQ, 3, HEADS, HEAD_DIM)
    queries, key_rows, value_rows = (projected[:, :, 0], projected[:, :, 1], projected[:, :, 2])
    scores = low_back(jnp.einsum('gqhd,gkhd->ghqk', queries, key_rows, precision=lax.Precision.HIGHEST) * 0.125)
    probs = low(jax.nn.softmax(scores, axis=-1))
    mixed = jnp.einsum('ghqk,gkhd->gqhd', probs, value_rows, precision=lax.Precision.HIGHEST).reshape(group, SEQ, D)
    mixed = low(low_back(mixed))
    branch = low_back(matmul(mixed, w_proj) + b_proj)
    resid = inputs + gate_attn * branch
    normed_two = normalize(resid)
    mlp_in = low(normed_two * (1.0 + scale_mlp) + shift_mlp)
    pre_act = low_back(matmul(mlp_in, w_up) + b_up)
    hidden = low(jax.nn.gelu(pre_act, approximate=True))
    mlp_out = low_back(matmul(hidden, w_down) + b_down)
    return resid + gate_mlp * mlp_out

def reference(tokens, cond, params, d_out):
    group = math.gcd(LAT, 16)
    blocks = LAT // group
    flat = params.astype(jnp.float32)
    inputs = tokens.astype(jnp.float32).reshape(LAT, SEQ, D)
    conds = cond.astype(jnp.float32)
    cotangent = d_out.astype(jnp.float32).reshape(LAT, SEQ, D)

    def forward(flat_in, inputs_in, conds_in):
        stepper = jax.checkpoint(layer)
        outcome = lax.map(lambda block_pair: stepper(flat_in, block_pair[0], block_pair[1]), (inputs_in.reshape(blocks, group, SEQ, D), conds_in.reshape(blocks, group, D)))
        return outcome.reshape(LAT, SEQ, D)
    result, pullback = jax.vjp(forward, flat, inputs, conds)
    grad_flat, grad_inputs, grad_conds = pullback(cotangent)
    return (result.astype(jnp.bfloat16).reshape(TOKENS, D), grad_inputs.reshape(TOKENS, D), grad_conds, grad_flat)
```

```python
import functools

import jax
import jax.numpy as jnp
from jax import lax
from jax.experimental import pallas as pl
from jax.experimental.pallas import tpu as pltpu
from jax.sharding import PartitionSpec as P

D = 384
FF = 1536
HEADS = 6
SEQ = 256
LATENTS = 4
ROWS = LATENTS * SEQ
SHARD = 20778
DEVICES = 128
BLOCK = 176
PARTS = (64, 64, 48)
FIRST = (0, 64, 128)
FLAT_ROWS = 20784

ADA, BADA = 0, 6912
QKV, BQV = 6930, 10386
PROJ, BPROJ = 10392, 11544
UP, BUP = 11547, 16155
DOWN, BDOWN = 16167, 20775

MESH = pl.DeviceIdType.MESH
BF16 = jnp.bfloat16
F32 = jnp.float32

ORDERS = ((2, 1, 0), (1, 0, 2), (0, 2, 1))


def coordinates():
    me = lax.axis_index("dev")
    return (
        lax.rem(lax.div(me, 32), 4),
        lax.rem(lax.div(me, 8), 4),
        lax.rem(lax.div(me, 2), 4),
        lax.rem(me, 2),
    )


def device_at(y, x, z, core):
    return (((y * 4 + x) * 4 + z) * 2 + core,)


def along(place, axis, step):
    moved = list(place)
    moved[axis] = lax.rem(place[axis] + step + 4, 4)
    return moved


def slot_of(part, index):
    place = (
        lax.rem(lax.div(index, 32), 4),
        lax.rem(lax.div(index, 8), 4),
        lax.rem(lax.div(index, 2), 4),
    )
    first, second, third = ORDERS[part]
    return ((lax.rem(index, 2) * 4 + place[third]) * 4 + place[second]) * 4 + place[first]


def shift_parts():
    offset = lax.rem(lax.axis_index("dev") * SHARD, 1024)
    return lax.div(offset, 128), lax.rem(offset, 128)


def one_hot(shape, difference, dtype):
    rows = lax.broadcasted_iota(jnp.int32, shape, 0)
    columns = lax.broadcasted_iota(jnp.int32, shape, 1)
    return jnp.where(columns - rows == difference, 1.0, 0.0).astype(dtype)


def greet(place):
    barrier = pltpu.get_barrier_semaphore()
    partners = [along(place, axis, step) for axis in range(3) for step in (1, 2, 3)]
    partners.append([place[0], place[1], place[2], 1 - place[3]])
    for partner in partners:
        pl.semaphore_signal(barrier, inc=1, device_id=device_at(*partner), device_id_type=MESH)
    pl.semaphore_wait(barrier, len(partners))


def remote(source, target, send, recv, device):
    return pltpu.make_async_remote_copy(
        src_ref=source,
        dst_ref=target,
        send_sem=send,
        recv_sem=recv,
        device_id=device_at(*device),
        device_id_type=MESH,
    )


def gather_kernel(x_ref, first_ref, second_ref, third_ref, send, recv, core_send, core_recv):
    outs = (first_ref, second_ref, third_ref)
    place = coordinates()
    core = place[3]
    sign = 1 - 2 * core
    sibling = [place[0], place[1], place[2], 1 - core]
    rows, lanes = shift_parts()
    x = x_ref[...]
    low = jnp.dot(x, one_hot((128, 128), lanes, BF16), preferred_element_type=F32).astype(BF16)
    high = jnp.dot(x, one_hot((128, 128), lanes - 128, BF16), preferred_element_type=F32).astype(BF16)
    square = (BLOCK, BLOCK)
    aligned = jnp.dot(one_hot(square, -rows, BF16), low, preferred_element_type=F32) + jnp.dot(
        one_hot(square, -rows - 1, BF16), high, preferred_element_type=F32
    )
    aligned = aligned.astype(BF16)
    for part, out in enumerate(outs):
        first, second, third = ORDERS[part]
        out[core, place[third], place[second], place[first]] = aligned[
            FIRST[part] : FIRST[part] + PARTS[part]
        ]
    greet(place)

    def block(part, stage, value):
        out = outs[part]
        first, second, third = ORDERS[part]
        if stage == 0:
            return out.at[core, place[third], place[second], value]
        if stage == 1:
            return out.at[core, place[third], value]
        return out.at[core, value]

    started = []

    def push(part, stage, kind, value, device):
        ref = block(part, stage, value)
        copy = remote(ref, ref, send.at[part, stage, kind], recv.at[part, stage, kind], device)
        copy.start()
        started.append(copy)

    def arrived(part, stage, kind, value):
        ref = block(part, stage, value)
        remote(
            ref, ref, send.at[part, stage, kind], recv.at[part, stage, kind], sibling
        ).wait_recv()

    crossed = []

    def cross(part, kind, value):
        ref = block(part, 2, value)
        copy = remote(ref, ref, core_send.at[part, kind], core_recv.at[part, kind], sibling)
        copy.start()
        started.append(copy)
        mine = outs[part].at[1 - core, value]
        crossed.append(
            remote(mine, mine, core_send.at[part, kind], core_recv.at[part, kind], sibling)
        )

    for stage in range(3):
        spots = []
        for part in range(3):
            axis = ORDERS[part][stage]
            ahead, behind = along(place, axis, sign), along(place, axis, -sign)
            across = along(place, axis, 2)
            spots.append((axis, ahead, behind, across))
            push(part, stage, 0, place[axis], ahead)
            push(part, stage, 1, place[axis], behind)
            if stage < 2:
                push(part, stage, 2, place[axis], across)
        if stage == 2:
            for part in range(3):
                cross(part, 0, place[spots[part][0]])
        for part in range(3):
            axis, ahead, behind, across = spots[part]
            arrived(part, stage, 0, behind[axis])
            if stage == 2:
                push(part, stage, 2, behind[axis], ahead)
                cross(part, 1, behind[axis])
        for part in range(3):
            axis, ahead, behind, across = spots[part]
            arrived(part, stage, 1, ahead[axis])
            if stage == 2:
                cross(part, 2, ahead[axis])
        for part in range(3):
            axis, ahead, behind, across = spots[part]
            arrived(part, stage, 2, across[axis])
            if stage == 2:
                cross(part, 3, across[axis])
    for copy in crossed:
        copy.wait_recv()
    for copy in started:
        copy.wait_send()


def gather(piece):
    return pl.pallas_call(
        gather_kernel,
        out_shape=[jax.ShapeDtypeStruct((2, 4, 4, 4, rows, 128), BF16) for rows in PARTS],
        in_specs=[pl.BlockSpec(memory_space=pltpu.VMEM)],
        out_specs=[pl.BlockSpec(memory_space=pltpu.VMEM)] * 3,
        scratch_shapes=[
            pltpu.SemaphoreType.DMA((3, 3, 3)),
            pltpu.SemaphoreType.DMA((3, 3, 3)),
            pltpu.SemaphoreType.DMA((3, 4)),
            pltpu.SemaphoreType.DMA((3, 4)),
        ],
        compiler_params=pltpu.CompilerParams(
            collective_id=0, has_side_effects=True, vmem_limit_bytes=32 * 1024 * 1024
        ),
        name="gather",
    )(piece)


def scatter_kernel(
    a_ref, b_ref, c_ref, out_ref,
    own_a, own_b, own_c, sib_a, sib_b, sib_c,
    one_a, one_b, one_c, two_a, two_b, two_c, three_a, three_b, three_c,
    total, load, core_send, core_recv, send, recv,
):
    ins = (a_ref, b_ref, c_ref)
    own = (own_a, own_b, own_c)
    sib = (sib_a, sib_b, sib_c)
    lands = ((one_a, one_b, one_c), (two_a, two_b, two_c), (three_a, three_b, three_c))
    place = coordinates()
    core = place[3]
    sign = 1 - 2 * core
    sibling = [place[0], place[1], place[2], 1 - core]
    loads = []
    for part in range(3):
        copy = pltpu.make_async_copy(ins[part].at[core], own[part], load.at[part])
        copy.start()
        loads.append(copy)
    greet(place)
    started = []
    spots = []
    for part in range(3):
        axis = ORDERS[part][2]
        spots.append(
            (axis, along(place, axis, 2), along(place, axis, -sign), along(place, axis, sign))
        )
    for kind in range(4):
        for part in range(3):
            axis = spots[part][0]
            value = place[axis] if kind == 3 else spots[part][(1, 3, 2)[kind]][axis]
            copy = remote(
                ins[part].at[1 - core, value],
                sib[part].at[value],
                core_send.at[part, kind],
                core_recv.at[part, kind],
                sibling,
            )
            copy.start()
            started.append(copy)
    for copy in loads:
        copy.wait()

    def push(part, stage, kind, source, device):
        copy = remote(
            source,
            lands[stage][part].at[kind],
            send.at[part, stage, kind],
            recv.at[part, stage, kind],
            device,
        )
        copy.start()
        started.append(copy)

    def arrived(part, stage, kind):
        ref = lands[stage][part].at[kind]
        remote(
            ref, ref, send.at[part, stage, kind], recv.at[part, stage, kind], sibling
        ).wait_recv()

    def add(target, *others):
        shape = target.shape
        if len(shape) == 2:
            value = target[...].astype(F32)
            for other in others:
                value = value + other[...].astype(F32)
            target[...] = value.astype(BF16)
            return

        def body(step, _):
            if len(shape) == 4:
                here = (lax.div(step, shape[1]), lax.rem(step, shape[1]))
            else:
                here = (step,)
            value = target[here].astype(F32)
            for other in others:
                value = value + other[here].astype(F32)
            target[here] = value.astype(BF16)
            return 0

        count = shape[0] * shape[1] if len(shape) == 4 else shape[0]
        lax.fori_loop(0, count, body, 0)

    for kind in range(4):
        for part in range(3):
            axis = spots[part][0]
            value = place[axis] if kind == 3 else spots[part][1 + kind][axis]
            ref = sib[part].at[value]
            remote(
                ref, ref, core_send.at[part, kind], core_recv.at[part, kind], sibling
            ).wait_recv()
            add(own[part].at[value], sib[part].at[value])
            if kind == 0:
                push(part, 0, 0, own[part].at[value], spots[part][3])
            if kind == 1:
                push(part, 0, 1, own[part].at[value], spots[part][2])
            if kind == 2:
                arrived(part, 0, 0)
                add(own[part].at[value], lands[0][part].at[0])
                push(part, 0, 2, own[part].at[value], spots[part][3])
    held = []
    for part in range(3):
        ref = own[part].at[place[spots[part][0]]]
        arrived(part, 0, 1)
        arrived(part, 0, 2)
        add(ref, lands[0][part].at[1], lands[0][part].at[2])
        held.append(ref)
        axis = ORDERS[part][1]
        for kind in range(3):
            far = along(place, axis, kind + 1)
            push(part, 1, kind, ref.at[far[axis]], far)
    for part in range(3):
        axis = ORDERS[part][1]
        ref = held[part].at[place[axis]]
        for kind in range(3):
            arrived(part, 1, kind)
        add(ref, *[lands[1][part].at[kind] for kind in range(3)])
        held[part] = ref
        axis = ORDERS[part][0]
        for kind in range(3):
            far = along(place, axis, kind + 1)
            push(part, 2, kind, ref.at[far[axis]], far)
    for part in range(3):
        axis = ORDERS[part][0]
        value = held[part][place[axis]].astype(F32)
        for kind in range(3):
            arrived(part, 2, kind)
            value = value + lands[2][part][kind].astype(F32)
        total[FIRST[part] : FIRST[part] + PARTS[part], :] = value
    for copy in started:
        copy.wait_send()
    rows, lanes = shift_parts()
    summed = total[...]

    def product(left, right):
        return jnp.dot(
            left, right, preferred_element_type=F32, precision=lax.Precision.HIGHEST
        )

    low = product(summed, one_hot((128, 128), -lanes, F32))
    high = product(summed, one_hot((128, 128), 128 - lanes, F32))
    square = (BLOCK, BLOCK)
    out_ref[...] = product(one_hot(square, rows, F32), low) + product(
        one_hot(square, rows + 1, F32), high
    )


def scatter(pieces):
    scratch = [pltpu.VMEM((4, 4, 4, rows, 128), BF16) for rows in PARTS] * 2
    scratch += [pltpu.VMEM((3, 4, 4, rows, 128), BF16) for rows in PARTS]
    scratch += [pltpu.VMEM((3, 4, rows, 128), BF16) for rows in PARTS]
    scratch += [pltpu.VMEM((3, rows, 128), BF16) for rows in PARTS]
    scratch += [
        pltpu.VMEM((BLOCK, 128), F32),
        pltpu.SemaphoreType.DMA((3,)),
        pltpu.SemaphoreType.DMA((3, 4)),
        pltpu.SemaphoreType.DMA((3, 4)),
        pltpu.SemaphoreType.DMA((3, 3, 3)),
        pltpu.SemaphoreType.DMA((3, 3, 3)),
    ]
    return pl.pallas_call(
        scatter_kernel,
        out_shape=jax.ShapeDtypeStruct((BLOCK, 128), F32),
        in_specs=[pl.BlockSpec(memory_space=pl.ANY)] * 3,
        out_specs=pl.BlockSpec(memory_space=pltpu.VMEM),
        scratch_shapes=scratch,
        compiler_params=pltpu.CompilerParams(
            collective_id=1, has_side_effects=True, vmem_limit_bytes=40 * 1024 * 1024
        ),
        name="scatter",
    )(*pieces)


def dot(left, right):
    return jnp.dot(left, right, preferred_element_type=F32)


def dot_nt(left, right):
    return lax.dot_general(left, right, (((1,), (1,)), ((), ())), preferred_element_type=F32)


def dot_tn(left, right):
    return lax.dot_general(left, right, (((0,), (0,)), ((), ())), preferred_element_type=F32)


def normalize(values):
    centered = values - jnp.mean(values, axis=-1, keepdims=True)
    inverse = lax.rsqrt(jnp.mean(centered * centered, axis=-1, keepdims=True) + 1e-06)
    return centered * inverse, inverse


def norm_back(grad_norm, normed, inverse):
    return inverse * (
        grad_norm
        - jnp.mean(grad_norm, axis=-1, keepdims=True)
        - normed * jnp.mean(grad_norm * normed, axis=-1, keepdims=True)
    )


def column_sums(values):
    return jnp.sum(values, axis=0, keepdims=True)


def block_kernel(
    tokens_ref, cond_ref, grad_ref, in_a, in_b, in_c,
    out_ref, d_tokens_ref, d_cond_ref, slots_a, slots_b, slots_c,
    flat, w_ada, w_qkv, w_proj, w_up, w_down, bias,
    silu, mod, d_mod, h1, inverse1, qkv, probs, attn_t, mixed_t, branch, resid,
    mlp_t, hidden, slope, d_mlp, d_pre, d_branch, d_resid, d_mixed, d_qkv, load,
):
    slots = (slots_a, slots_b, slots_c)
    loads = [
        pltpu.make_async_copy(source, target, load.at[number])
        for number, (source, target) in enumerate(zip((in_a, in_b, in_c), slots))
    ]
    for copy in loads:
        copy.start()
    flat[0:8, :] = jnp.zeros((8, 128), F32)
    for copy in loads:
        copy.wait()

    def unpack(index, _):
        start = pl.multiple_of(lax.div(index * SHARD, 1024) * 8, 8)
        for part in range(3):
            value = slots[part][slot_of(part, index)].astype(F32)
            if part == 0:
                flat[pl.ds(start, 8), :] += value[:8]
                flat[pl.ds(start + 8, PARTS[0] - 8), :] = value[8:]
            else:
                flat[pl.ds(start + FIRST[part], PARTS[part]), :] = value
        return 0

    lax.fori_loop(0, DEVICES, unpack, 0)

    def take_matrix(target, base, height, width):
        for column in range(width):
            target[:, column * 128 : (column + 1) * 128] = flat[
                pl.ds(base + column, height, stride=width), :
            ].astype(BF16)

    def take_row(base, width, offset):
        for column in range(width):
            bias[0:1, offset + column * 128 : offset + (column + 1) * 128] = flat[
                base + column : base + column + 1, :
            ]

    def put_row(base, value):
        for column in range(value.shape[1] // 128):
            flat[base + column : base + column + 1, :] = value[
                :, column * 128 : (column + 1) * 128
            ]

    def put_block(base, width, column, value):
        for number in range(value.shape[1] // 128):
            flat[pl.ds(base + column + number, value.shape[0], stride=width), :] = value[
                :, number * 128 : (number + 1) * 128
            ]

    take_matrix(w_ada, ADA, D, 18)
    take_matrix(w_qkv, QKV, D, 9)
    take_matrix(w_proj, PROJ, D, 3)
    take_matrix(w_up, UP, D, 12)
    take_matrix(w_down, DOWN, FF, 3)
    take_row(BADA, 18, 0)
    take_row(BQV, 3, 2304)
    bias[0:1, 2688:3072] = jnp.zeros((1, D), F32)
    take_row(BQV + 3, 3, 3072)
    take_row(BPROJ, 3, 3456)
    take_row(BUP, 12, 3840)
    take_row(BDOWN, 3, 5376)

    cond = cond_ref[...].astype(F32)
    silu[...] = jnp.zeros_like(silu)
    silu[0:LATENTS, :] = cond / (1.0 + jnp.exp(-cond))
    silu_low = silu[...].astype(BF16)
    mod[...] = dot(silu_low, w_ada[...]) + bias[0:1, 0:2304]
    d_mod[...] = jnp.zeros_like(d_mod)

    lane = lax.broadcasted_iota(jnp.int32, (SEQ, 128), 1)
    half = (lane < 64, lane >= 64)

    def masked(value, head):
        return jnp.where(half[head], value, jnp.zeros_like(value))

    def forward_attention(latent, _):
        tokens = pl.ds(pl.multiple_of(latent * SEQ, SEQ), SEQ)
        x = tokens_ref[tokens, :].astype(F32)
        shift = mod[pl.ds(latent, 1), 0:D]
        scale = mod[pl.ds(latent, 1), D : 2 * D]
        gate = mod[pl.ds(latent, 1), 2 * D : 3 * D]
        normed, inverse = normalize(x)
        h1[tokens, :] = normed
        inverse1[tokens, :] = inverse
        attn_in = (normed * (1.0 + scale) + shift).astype(BF16)
        attn_t[:, tokens] = attn_in.T
        projected = (dot(attn_in, w_qkv[...]) + bias[0:1, 2304:3456]).astype(BF16)
        qkv[tokens, :] = projected
        for pair in range(3):
            q = projected[:, pair * 128 : (pair + 1) * 128] * jnp.asarray(0.125, BF16)
            k = projected[:, D + pair * 128 : D + (pair + 1) * 128]
            v_t = projected[:, 2 * D + pair * 128 : 2 * D + (pair + 1) * 128].T
            mixed = []
            for head in range(2):
                scores = dot_nt(masked(k, head), q)
                top = jnp.max(scores, axis=0, keepdims=True)
                powers = jnp.exp(scores - top)
                weights = (powers * (1.0 / column_sums(powers))).astype(BF16)
                probs[latent * HEADS + pair * 2 + head] = weights
                mixed.append(dot(v_t[head * 64 : (head + 1) * 64], weights))
            mixed_t[pair * 128 : (pair + 1) * 128, tokens] = jnp.concatenate(
                mixed, axis=0
            ).astype(BF16)
        reached = dot_tn(mixed_t[:, tokens], w_proj[...]) + bias[0:1, 3456:3840]
        branch[tokens, :] = reached
        resid[tokens, :] = x + gate * reached
        return 0

    lax.fori_loop(0, LATENTS, forward_attention, 0)

    chunk = 512

    def mlp(latent, sums):
        sum_down, sum_up, sum_proj = sums
        tokens = pl.ds(pl.multiple_of(latent * SEQ, SEQ), SEQ)
        row = pl.ds(latent, 1)
        gate1 = mod[row, 2 * D : 3 * D]
        shift = mod[row, 3 * D : 4 * D]
        scale = mod[row, 4 * D : 5 * D]
        gate = mod[row, 5 * D : 6 * D]
        kept = resid[tokens, :]
        normed, inverse = normalize(kept)
        mlp_in = (normed * (1.0 + scale) + shift).astype(BF16)
        mlp_t[:, tokens] = mlp_in.T
        for start in range(0, FF, chunk):
            here = slice(start, start + chunk)
            u = dot(mlp_in, w_up[:, here]) + bias[0:1, 3840 + start : 3840 + start + chunk]
            square = u * u
            inner = u * (0.7978845608028654 + (0.7978845608028654 * 0.044715) * square)
            tangent = jnp.tanh(inner)
            above = 0.5 + 0.5 * tangent
            hidden[tokens, here] = (u * above).astype(BF16)
            rise = 0.7978845608028654 + (3 * 0.7978845608028654 * 0.044715) * square
            slope[:, here] = above + (0.5 * u) * (1.0 - tangent * tangent) * rise
        mlp_out = dot(hidden[tokens, :], w_down[...]) + bias[0:1, 5376:5760]
        out_ref[tokens, :] = (kept + gate * mlp_out).astype(BF16)
        grad = grad_ref[tokens, :].astype(F32)
        d_mod[row, 5 * D : 6 * D] = column_sums(grad * mlp_out)
        grad_mlp = (grad * gate).astype(BF16)
        d_mlp[tokens, :] = grad_mlp
        sum_down = sum_down + column_sums(grad_mlp.astype(F32))
        ups = []
        for start in range(0, FF, chunk):
            here = slice(start, start + chunk)
            value = (slope[:, here] * dot_nt(grad_mlp, w_down[here, :])).astype(BF16)
            d_pre[tokens, here] = value
            ups.append(column_sums(value.astype(F32)))
        sum_up = sum_up + jnp.concatenate(ups, axis=1)
        d_in = dot_nt(d_pre[tokens, :], w_up[...])
        d_mod[row, 4 * D : 5 * D] = column_sums(d_in * normed)
        d_mod[row, 3 * D : 4 * D] = column_sums(d_in)
        back = grad + norm_back(d_in * (1.0 + scale), normed, inverse)
        d_resid[tokens, :] = back
        d_mod[row, 2 * D : 3 * D] = column_sums(back * branch[tokens, :])
        low = (back * gate1).astype(BF16)
        d_branch[tokens, :] = low
        sum_proj = sum_proj + column_sums(low.astype(F32))
        d_mixed[tokens, :] = dot_nt(low, w_proj[...]).astype(BF16)
        return sum_down, sum_up, sum_proj

    zeros = jnp.zeros((1, D), F32)
    sum_down, sum_up, sum_proj = lax.fori_loop(
        0, LATENTS, mlp, (zeros, jnp.zeros((1, FF), F32), zeros)
    )
    put_row(BDOWN, sum_down)
    put_row(BUP, sum_up)
    put_row(BPROJ, sum_proj)
    for start in range(0, FF, 256):
        here = slice(start, start + 256)
        put_block(UP, 12, start // 128, dot(mlp_t[...], d_pre[:, here]))
        put_block(DOWN + start * 3, 3, 0, dot_tn(hidden[:, here], d_mlp[...]))
    put_block(PROJ, 3, 0, dot(mixed_t[...], d_branch[...]))

    def backward_attention(latent, sums):
        tokens = pl.ds(pl.multiple_of(latent * SEQ, SEQ), SEQ)
        row = pl.ds(latent, 1)
        scale = mod[row, D : 2 * D]
        projected = qkv[tokens, :]
        d_out = d_mixed[tokens, :]
        for pair in range(3):
            q = projected[:, pair * 128 : (pair + 1) * 128] * jnp.asarray(0.125, BF16)
            k_t = projected[:, D + pair * 128 : D + (pair + 1) * 128].T
            v = projected[:, 2 * D + pair * 128 : 2 * D + (pair + 1) * 128]
            above = d_out[:, pair * 128 : (pair + 1) * 128]
            grad_q, grad_k, grad_v = [], 0.0, 0.0
            for head in range(2):
                mine = masked(above, head)
                weights = probs[latent * HEADS + pair * 2 + head]
                grad_v = grad_v + dot(weights, mine)
                wide = weights.astype(F32)
                product = dot_nt(v, mine) * wide
                scores = (product - wide * column_sums(product)).astype(BF16)
                grad_k = grad_k + dot(scores, masked(q, head))
                grad_q.append(dot(k_t[head * 64 : (head + 1) * 64], scores))
            here = slice(pair * 128, (pair + 1) * 128)
            turned = (jnp.concatenate(grad_q, axis=0) * 0.125).astype(BF16)
            d_qkv[tokens, here] = turned.T
            d_qkv[tokens, D + pair * 128 : D + (pair + 1) * 128] = grad_k.astype(BF16)
            d_qkv[tokens, 2 * D + pair * 128 : 2 * D + (pair + 1) * 128] = grad_v.astype(BF16)
        low = d_qkv[tokens, :]
        normed = h1[tokens, :]
        d_in = dot_nt(low, w_qkv[...])
        d_mod[row, D : 2 * D] = column_sums(d_in * normed)
        d_mod[row, 0:D] = column_sums(d_in)
        d_tokens_ref[tokens, :] = d_resid[tokens, :] + norm_back(
            d_in * (1.0 + scale), normed, inverse1[tokens, :]
        )
        return sums + column_sums(low.astype(F32))

    sum_qkv = lax.fori_loop(0, LATENTS, backward_attention, jnp.zeros((1, 3 * D), F32))
    put_row(BQV, sum_qkv[:, :D])
    put_row(BQV + 3, sum_qkv[:, 2 * D :])
    for start in range(0, 3 * D, D):
        put_block(QKV, 9, start // 128, dot(attn_t[...], d_qkv[:, start : start + D]))
    d_mod_low = d_mod[...].astype(BF16)
    put_row(BADA, column_sums(d_mod_low.astype(F32)))
    for start in range(0, 6 * D, D):
        put_block(ADA, 18, start // 128, dot_tn(silu_low, d_mod_low[:, start : start + D]))
    d_silu = dot_nt(d_mod_low, w_ada[...])[0:LATENTS]
    gate = 1.0 / (1.0 + jnp.exp(-cond))
    d_cond_ref[...] = d_silu * (gate * (1.0 + cond * (1.0 - gate)))

    def pack(index, _):
        start = pl.multiple_of(lax.div(index * SHARD, 1024) * 8, 8)
        for part in range(3):
            slots[part][slot_of(part, index)] = flat[
                pl.ds(start + FIRST[part], PARTS[part]), :
            ].astype(BF16)
        return 0

    lax.fori_loop(0, DEVICES, pack, 0)


def transformer_block(tokens, cond, d_out, gathered):
    vmem = pl.BlockSpec(memory_space=pltpu.VMEM)
    scratch = [
        ((FLAT_ROWS, 128), F32),
        ((D, 6 * D), BF16),
        ((D, 3 * D), BF16),
        ((D, D), BF16),
        ((D, FF), BF16),
        ((FF, D), BF16),
        ((8, 5760), F32),
        ((16, D), F32),
        ((16, 6 * D), F32),
        ((16, 6 * D), F32),
        ((ROWS, D), F32),
        ((ROWS, 1), F32),
        ((ROWS, 3 * D), BF16),
        ((LATENTS * HEADS, SEQ, SEQ), BF16),
        ((D, ROWS), BF16),
        ((D, ROWS), BF16),
        ((ROWS, D), F32),
        ((ROWS, D), F32),
        ((D, ROWS), BF16),
        ((ROWS, FF), BF16),
        ((SEQ, FF), F32),
        ((ROWS, D), BF16),
        ((ROWS, FF), BF16),
        ((ROWS, D), BF16),
        ((ROWS, D), F32),
        ((ROWS, D), BF16),
        ((ROWS, 3 * D), BF16),
    ]
    return pl.pallas_call(
        block_kernel,
        out_shape=[
            jax.ShapeDtypeStruct((ROWS, D), BF16),
            jax.ShapeDtypeStruct((ROWS, D), F32),
            jax.ShapeDtypeStruct((LATENTS, D), F32),
        ]
        + [jax.ShapeDtypeStruct((DEVICES, rows, 128), BF16) for rows in PARTS],
        in_specs=[vmem] * 3 + [pl.BlockSpec(memory_space=pl.ANY)] * 3,
        out_specs=[vmem] * 6,
        scratch_shapes=[pltpu.VMEM(shape, dtype) for shape, dtype in scratch]
        + [pltpu.SemaphoreType.DMA((3,))],
        compiler_params=pltpu.CompilerParams(vmem_limit_bytes=63 * 1024 * 1024),
        name="block",
    )(tokens, cond, d_out, *gathered)


def local(tokens, cond, params, d_out):
    piece = jnp.pad(params, (0, BLOCK * 128 - SHARD)).reshape(BLOCK, 128)
    gathered = gather(piece)
    gathered = [part.reshape(DEVICES, rows, 128) for part, rows in zip(gathered, PARTS)]
    out, d_tokens, d_cond, *slots = transformer_block(tokens, cond, d_out, gathered)
    slots = [part.reshape(2, 4, 4, 4, rows, 128) for part, rows in zip(slots, PARTS)]
    summed = scatter(slots)
    return out, d_tokens, d_cond, summed.reshape(-1)[:SHARD]


def solution(mesh):
    placed = (P("dev", None), P("dev", None), P("dev"), P("dev", None))
    return jax.shard_map(
        local,
        mesh=mesh,
        in_specs=placed,
        out_specs=(P("dev", None), P("dev", None), P("dev", None), P("dev")),
        check_vma=False,
    )
```

```python
import functools

import jax
import jax.numpy as jnp
from jax import lax
from jax.experimental import pallas as pl
from jax.experimental.pallas import tpu as pltpu
from jax.sharding import PartitionSpec as P

D = 384
FF = 1536
HEADS = 6
SEQ = 256
LATENTS = 4
ROWS = LATENTS * SEQ
SHARD = 20778
DEVICES = 128
BLOCK = 176
PARTS = (64, 64, 48)
FIRST = (0, 64, 128)
FLAT_ROWS = 20784

ADA, BADA = 0, 6912
QKV, BQV = 6930, 10386
PROJ, BPROJ = 10392, 11544
UP, BUP = 11547, 16155
DOWN, BDOWN = 16167, 20775

MESH = pl.DeviceIdType.MESH
BF16 = jnp.bfloat16
F32 = jnp.float32

ORDERS = ((2, 1, 0), (1, 0, 2), (0, 2, 1))


def coordinates():
    me = lax.axis_index("dev")
    return (
        lax.rem(lax.div(me, 32), 4),
        lax.rem(lax.div(me, 8), 4),
        lax.rem(lax.div(me, 2), 4),
        lax.rem(me, 2),
    )


def device_at(y, x, z, core):
    return (((y * 4 + x) * 4 + z) * 2 + core,)


def along(place, axis, step):
    moved = list(place)
    moved[axis] = lax.rem(place[axis] + step + 4, 4)
    return moved


def slot_at(part, index):
    place = (
        lax.rem(lax.div(index, 32), 4),
        lax.rem(lax.div(index, 8), 4),
        lax.rem(lax.div(index, 2), 4),
    )
    first, second, third = ORDERS[part]
    return lax.rem(index, 2), place[third], place[second], place[first]


def shift_parts():
    offset = lax.rem(lax.axis_index("dev") * SHARD, 1024)
    return lax.div(offset, 128), lax.rem(offset, 128)


def one_hot(shape, difference, dtype):
    rows = lax.broadcasted_iota(jnp.int32, shape, 0)
    columns = lax.broadcasted_iota(jnp.int32, shape, 1)
    return jnp.where(columns - rows == difference, 1.0, 0.0).astype(dtype)


def greet(place):
    barrier = pltpu.get_barrier_semaphore()
    partners = [along(place, axis, step) for axis in range(3) for step in (1, 2, 3)]
    partners.append([place[0], place[1], place[2], 1 - place[3]])
    for partner in partners:
        pl.semaphore_signal(barrier, inc=1, device_id=device_at(*partner), device_id_type=MESH)
    pl.semaphore_wait(barrier, len(partners))


def remote(source, target, send, recv, device):
    return pltpu.make_async_remote_copy(
        src_ref=source,
        dst_ref=target,
        send_sem=send,
        recv_sem=recv,
        device_id=device_at(*device),
        device_id_type=MESH,
    )


def dot(left, right):
    return jnp.dot(left, right, preferred_element_type=F32)


def dot_nt(left, right):
    return lax.dot_general(left, right, (((1,), (1,)), ((), ())), preferred_element_type=F32)


def dot_tn(left, right):
    return lax.dot_general(left, right, (((0,), (0,)), ((), ())), preferred_element_type=F32)


def normalize(values):
    centered = values - jnp.mean(values, axis=-1, keepdims=True)
    inverse = lax.rsqrt(jnp.mean(centered * centered, axis=-1, keepdims=True) + 1e-06)
    return centered * inverse, inverse


def norm_back(grad_norm, normed, inverse):
    return inverse * (
        grad_norm
        - jnp.mean(grad_norm, axis=-1, keepdims=True)
        - normed * jnp.mean(grad_norm * normed, axis=-1, keepdims=True)
    )


def column_sums(values):
    return jnp.sum(values, axis=0, keepdims=True)


def whole_kernel(
    piece_ref, cond_ref, tokens_hbm, grad_hbm,
    out_hbm, d_tokens_hbm, d_cond_ref, summed_ref,
    slots_a, slots_b, slots_c, sib_a, sib_b, sib_c,
    one_a, one_b, one_c, two_a, two_b, two_c, three_a, three_b, three_c, total,
    tokens_ref, grad_ref, out_ref,
    flat, w_ada, w_qkv, w_proj, w_up, w_down, bias,
    silu, mod, d_mod, h1, inverse1, qkv, probs, attn_t, mixed_t, branch, resid,
    mlp_t, hidden, slope, d_mlp, d_pre, d_branch, d_mixed, d_qkv,
    load, store, gather_send, gather_recv, meet_send, meet_recv,
    core_send, core_recv, send, recv,
):
    slots = (slots_a, slots_b, slots_c)
    sib = (sib_a, sib_b, sib_c)
    lands = ((one_a, one_b, one_c), (two_a, two_b, two_c), (three_a, three_b, three_c))
    place = coordinates()
    core = place[3]
    sign = 1 - 2 * core
    sibling = [place[0], place[1], place[2], 1 - core]
    load_tokens = pltpu.make_async_copy(tokens_hbm, tokens_ref, load.at[0])
    load_grad = pltpu.make_async_copy(grad_hbm, grad_ref, load.at[1])
    load_tokens.start()
    load_grad.start()

    rows, lanes = shift_parts()
    x = piece_ref[...]
    low = dot(x, one_hot((128, 128), lanes, BF16)).astype(BF16)
    high = dot(x, one_hot((128, 128), lanes - 128, BF16)).astype(BF16)
    square = (BLOCK, BLOCK)
    aligned = dot(one_hot(square, -rows, BF16), low) + dot(one_hot(square, -rows - 1, BF16), high)
    aligned = aligned.astype(BF16)
    for part, slot in enumerate(slots):
        first, second, third = ORDERS[part]
        slot[core, place[third], place[second], place[first]] = aligned[
            FIRST[part] : FIRST[part] + PARTS[part]
        ]
    greet(place)

    def block(part, stage, value):
        slot = slots[part]
        first, second, third = ORDERS[part]
        if stage == 0:
            return slot.at[core, place[third], place[second], value]
        if stage == 1:
            return slot.at[core, place[third], value]
        return slot.at[core, value]

    started = []

    def push(part, stage, kind, value, device):
        ref = block(part, stage, value)
        copy = remote(
            ref, ref, gather_send.at[part, stage, kind], gather_recv.at[part, stage, kind], device
        )
        copy.start()
        started.append(copy)

    def arrived(part, stage, kind, value):
        ref = block(part, stage, value)
        remote(
            ref,
            ref,
            gather_send.at[part, stage, kind],
            gather_recv.at[part, stage, kind],
            sibling,
        ).wait_recv()

    crossed = []

    def cross(part, kind, value):
        ref = block(part, 2, value)
        copy = remote(ref, ref, meet_send.at[part, kind], meet_recv.at[part, kind], sibling)
        copy.start()
        started.append(copy)
        mine = slots[part].at[1 - core, value]
        crossed.append(
            remote(mine, mine, meet_send.at[part, kind], meet_recv.at[part, kind], sibling)
        )

    for stage in range(3):
        spots = []
        for part in range(3):
            axis = ORDERS[part][stage]
            ahead, behind = along(place, axis, sign), along(place, axis, -sign)
            across = along(place, axis, 2)
            spots.append((axis, ahead, behind, across))
            push(part, stage, 0, place[axis], ahead)
            push(part, stage, 1, place[axis], behind)
            if stage < 2:
                push(part, stage, 2, place[axis], across)
        if stage == 2:
            for part in range(3):
                cross(part, 0, place[spots[part][0]])
        for part in range(3):
            axis, ahead, behind, across = spots[part]
            arrived(part, stage, 0, behind[axis])
            if stage == 2:
                push(part, stage, 2, behind[axis], ahead)
                cross(part, 1, behind[axis])
        for part in range(3):
            axis, ahead, behind, across = spots[part]
            arrived(part, stage, 1, ahead[axis])
            if stage == 2:
                cross(part, 2, ahead[axis])
        for part in range(3):
            axis, ahead, behind, across = spots[part]
            arrived(part, stage, 2, across[axis])
            if stage == 2:
                cross(part, 3, across[axis])
    for copy in crossed:
        copy.wait_recv()
    for copy in started:
        copy.wait_send()

    def first_row(index):
        return pl.multiple_of(lax.div(index * SHARD, 1024) * 8, 8)

    def unpack(index, _):
        start = first_row(index)
        before = lax.max(index - 1, 0)
        tail = slots[2][slot_at(2, before)][32:48].astype(F32)
        tail = jnp.where(start - first_row(before) == 160, tail[:8], tail[8:])
        tail = jnp.where(index == 0, jnp.zeros_like(tail), tail)
        for part in range(3):
            value = slots[part][slot_at(part, index)].astype(F32)
            if part == 0:
                flat[pl.ds(start, 8), :] = value[:8] + tail
                flat[pl.ds(start + 8, PARTS[0] - 8), :] = value[8:]
            else:
                flat[pl.ds(start + FIRST[part], PARTS[part]), :] = value
        return 0

    lax.fori_loop(0, DEVICES, unpack, 0, unroll=4)

    def take_matrix(target, base, height, width):
        for column in range(width):
            target[:, column * 128 : (column + 1) * 128] = flat[
                pl.ds(base + column, height, stride=width), :
            ].astype(BF16)

    def take_row(base, width, offset):
        for column in range(width):
            bias[0:1, offset + column * 128 : offset + (column + 1) * 128] = flat[
                base + column : base + column + 1, :
            ]

    def put_row(base, value):
        for column in range(value.shape[1] // 128):
            flat[base + column : base + column + 1, :] = value[
                :, column * 128 : (column + 1) * 128
            ]

    def put_block(base, width, column, value):
        for number in range(value.shape[1] // 128):
            flat[pl.ds(base + column + number, value.shape[0], stride=width), :] = value[
                :, number * 128 : (number + 1) * 128
            ]

    take_matrix(w_ada, ADA, D, 18)
    take_matrix(w_qkv, QKV, D, 9)
    take_matrix(w_proj, PROJ, D, 3)
    take_matrix(w_up, UP, D, 12)
    take_matrix(w_down, DOWN, FF, 3)
    take_row(BADA, 18, 0)
    take_row(BQV, 3, 2304)
    bias[0:1, 2688:3072] = jnp.zeros((1, D), F32)
    take_row(BQV + 3, 3, 3072)
    take_row(BPROJ, 3, 3456)
    take_row(BUP, 12, 3840)
    take_row(BDOWN, 3, 5376)

    cond = cond_ref[...].astype(F32)
    silu[...] = jnp.zeros_like(silu)
    silu[0:LATENTS, :] = cond / (1.0 + jnp.exp(-cond))
    silu_low = silu[...].astype(BF16)
    mod[...] = dot(silu_low, w_ada[...]) + bias[0:1, 0:2304]
    d_mod[...] = jnp.zeros_like(d_mod)

    lane = lax.broadcasted_iota(jnp.int32, (SEQ, 128), 1)
    half = (lane < 64, lane >= 64)

    def masked(value, head):
        return jnp.where(half[head], value, jnp.zeros_like(value))

    load_tokens.wait()

    def forward_attention(latent, _):
        tokens = pl.ds(pl.multiple_of(latent * SEQ, SEQ), SEQ)
        x = tokens_ref[tokens, :].astype(F32)
        shift = mod[pl.ds(latent, 1), 0:D]
        scale = mod[pl.ds(latent, 1), D : 2 * D]
        gate = mod[pl.ds(latent, 1), 2 * D : 3 * D]
        normed, inverse = normalize(x)
        h1[tokens, :] = normed
        inverse1[tokens, :] = inverse
        attn_in = (normed * (1.0 + scale) + shift).astype(BF16)
        attn_t[:, tokens] = attn_in.T
        projected = (dot(attn_in, w_qkv[...]) + bias[0:1, 2304:3456]).astype(BF16)
        qkv[tokens, :] = projected
        for pair in range(3):
            q = projected[:, pair * 128 : (pair + 1) * 128] * jnp.asarray(0.125, BF16)
            k = projected[:, D + pair * 128 : D + (pair + 1) * 128]
            v_t = projected[:, 2 * D + pair * 128 : 2 * D + (pair + 1) * 128].T
            mixed = []
            for head in range(2):
                scores = dot_nt(masked(k, head), q)
                top = jnp.max(scores, axis=0, keepdims=True)
                powers = jnp.exp(scores - top)
                weights = (powers * (1.0 / column_sums(powers))).astype(BF16)
                probs[latent * HEADS + pair * 2 + head] = weights
                mixed.append(dot(v_t[head * 64 : (head + 1) * 64], weights))
            mixed_t[pair * 128 : (pair + 1) * 128, tokens] = jnp.concatenate(
                mixed, axis=0
            ).astype(BF16)
        reached = dot_tn(mixed_t[:, tokens], w_proj[...]) + bias[0:1, 3456:3840]
        branch[tokens, :] = reached
        resid[tokens, :] = x + gate * reached
        return 0

    lax.fori_loop(0, LATENTS, forward_attention, 0)

    chunk = 512
    load_grad.wait()

    def mlp(latent, sums):
        sum_down, sum_up, sum_proj = sums
        tokens = pl.ds(pl.multiple_of(latent * SEQ, SEQ), SEQ)
        row = pl.ds(latent, 1)
        gate1 = mod[row, 2 * D : 3 * D]
        shift = mod[row, 3 * D : 4 * D]
        scale = mod[row, 4 * D : 5 * D]
        gate = mod[row, 5 * D : 6 * D]
        kept = resid[tokens, :]
        normed, inverse = normalize(kept)
        mlp_in = (normed * (1.0 + scale) + shift).astype(BF16)
        mlp_t[:, tokens] = mlp_in.T
        for start in range(0, FF, chunk):
            here = slice(start, start + chunk)
            u = dot(mlp_in, w_up[:, here]) + bias[0:1, 3840 + start : 3840 + start + chunk]
            square = u * u
            inner = u * (0.7978845608028654 + (0.7978845608028654 * 0.044715) * square)
            tangent = jnp.tanh(inner)
            above = 0.5 + 0.5 * tangent
            hidden[tokens, here] = (u * above).astype(BF16)
            rise = 0.7978845608028654 + (3 * 0.7978845608028654 * 0.044715) * square
            slope[:, here] = above + (0.5 * u) * (1.0 - tangent * tangent) * rise
        mlp_out = dot(hidden[tokens, :], w_down[...]) + bias[0:1, 5376:5760]
        out_ref[tokens, :] = (kept + gate * mlp_out).astype(BF16)
        pltpu.make_async_copy(
            out_ref.at[tokens, :], out_hbm.at[tokens, :], store.at[0, latent]
        ).start()
        grad = grad_ref[tokens, :].astype(F32)
        d_mod[row, 5 * D : 6 * D] = column_sums(grad * mlp_out)
        grad_mlp = (grad * gate).astype(BF16)
        d_mlp[tokens, :] = grad_mlp
        sum_down = sum_down + column_sums(grad_mlp.astype(F32))
        ups = []
        for start in range(0, FF, chunk):
            here = slice(start, start + chunk)
            value = (slope[:, here] * dot_nt(grad_mlp, w_down[here, :])).astype(BF16)
            d_pre[tokens, here] = value
            ups.append(column_sums(value.astype(F32)))
        sum_up = sum_up + jnp.concatenate(ups, axis=1)
        d_in = dot_nt(d_pre[tokens, :], w_up[...])
        d_mod[row, 4 * D : 5 * D] = column_sums(d_in * normed)
        d_mod[row, 3 * D : 4 * D] = column_sums(d_in)
        back = grad + norm_back(d_in * (1.0 + scale), normed, inverse)
        resid[tokens, :] = back
        d_mod[row, 2 * D : 3 * D] = column_sums(back * branch[tokens, :])
        low = (back * gate1).astype(BF16)
        d_branch[tokens, :] = low
        sum_proj = sum_proj + column_sums(low.astype(F32))
        d_mixed[tokens, :] = dot_nt(low, w_proj[...]).astype(BF16)
        return sum_down, sum_up, sum_proj

    zeros = jnp.zeros((1, D), F32)
    sum_down, sum_up, sum_proj = lax.fori_loop(
        0, LATENTS, mlp, (zeros, jnp.zeros((1, FF), F32), zeros)
    )
    put_row(BDOWN, sum_down)
    put_row(BUP, sum_up)
    put_row(BPROJ, sum_proj)
    for start in range(0, FF, 256):
        here = slice(start, start + 256)
        put_block(UP, 12, start // 128, dot(mlp_t[...], d_pre[:, here]))
        put_block(DOWN + start * 3, 3, 0, dot_tn(hidden[:, here], d_mlp[...]))
    put_block(PROJ, 3, 0, dot(mixed_t[...], d_branch[...]))

    def backward_attention(latent, sums):
        tokens = pl.ds(pl.multiple_of(latent * SEQ, SEQ), SEQ)
        row = pl.ds(latent, 1)
        scale = mod[row, D : 2 * D]
        projected = qkv[tokens, :]
        d_out = d_mixed[tokens, :]
        for pair in range(3):
            q = projected[:, pair * 128 : (pair + 1) * 128] * jnp.asarray(0.125, BF16)
            k_t = projected[:, D + pair * 128 : D + (pair + 1) * 128].T
            v = projected[:, 2 * D + pair * 128 : 2 * D + (pair + 1) * 128]
            above = d_out[:, pair * 128 : (pair + 1) * 128]
            grad_q, grad_k, grad_v = [], 0.0, 0.0
            for head in range(2):
                mine = masked(above, head)
                weights = probs[latent * HEADS + pair * 2 + head]
                grad_v = grad_v + dot(weights, mine)
                wide = weights.astype(F32)
                product = dot_nt(v, mine) * wide
                scores = (product - wide * column_sums(product)).astype(BF16)
                grad_k = grad_k + dot(scores, masked(q, head))
                grad_q.append(dot(k_t[head * 64 : (head + 1) * 64], scores))
            here = slice(pair * 128, (pair + 1) * 128)
            turned = (jnp.concatenate(grad_q, axis=0) * 0.125).astype(BF16)
            d_qkv[tokens, here] = turned.T
            d_qkv[tokens, D + pair * 128 : D + (pair + 1) * 128] = grad_k.astype(BF16)
            d_qkv[tokens, 2 * D + pair * 128 : 2 * D + (pair + 1) * 128] = grad_v.astype(BF16)
        low = d_qkv[tokens, :]
        normed = h1[tokens, :]
        d_in = dot_nt(low, w_qkv[...])
        d_mod[row, D : 2 * D] = column_sums(d_in * normed)
        d_mod[row, 0:D] = column_sums(d_in)
        h1[tokens, :] = resid[tokens, :] + norm_back(
            d_in * (1.0 + scale), normed, inverse1[tokens, :]
        )
        pltpu.make_async_copy(
            h1.at[tokens, :], d_tokens_hbm.at[tokens, :], store.at[1, latent]
        ).start()
        return sums + column_sums(low.astype(F32))

    sum_qkv = lax.fori_loop(0, LATENTS, backward_attention, jnp.zeros((1, 3 * D), F32))
    put_row(BQV, sum_qkv[:, :D])
    put_row(BQV + 3, sum_qkv[:, 2 * D :])
    for start in range(0, 3 * D, D):
        put_block(QKV, 9, start // 128, dot(attn_t[...], d_qkv[:, start : start + D]))
    d_mod_low = d_mod[...].astype(BF16)
    put_row(BADA, column_sums(d_mod_low.astype(F32)))
    for start in range(0, 6 * D, D):
        put_block(ADA, 18, start // 128, dot_tn(silu_low, d_mod_low[:, start : start + D]))
    d_silu = dot_nt(d_mod_low, w_ada[...])[0:LATENTS]
    gate = 1.0 / (1.0 + jnp.exp(-cond))
    d_cond_ref[...] = d_silu * (gate * (1.0 + cond * (1.0 - gate)))

    def slot_row(part, c, b, a, which):
        spot = [0, 0, 0]
        first, second, third = ORDERS[part]
        spot[third], spot[second], spot[first] = c, b, a
        start = first_row(device_at(*spot, which)[0])
        return pl.ds(pl.multiple_of(start + FIRST[part], 8), PARTS[part])

    def pack(part, value):
        def body(step, _):
            b, a = lax.div(step, 4), lax.rem(step, 4)
            slots[part][1 - core, value, b, a] = flat[
                slot_row(part, value, b, a, 1 - core), :
            ].astype(BF16)
            return 0

        lax.fori_loop(0, 16, body, 0, unroll=4)

    def meet(part, value):
        def body(step, _):
            b, a = lax.div(step, 4), lax.rem(step, 4)
            mine = flat[slot_row(part, value, b, a, core), :]
            slots[part][core, value, b, a] = (mine + sib[part][value, b, a].astype(F32)).astype(
                BF16
            )
            return 0

        lax.fori_loop(0, 16, body, 0, unroll=4)

    started = []
    spots = []
    for part in range(3):
        axis = ORDERS[part][2]
        spots.append(
            (axis, along(place, axis, 2), along(place, axis, -sign), along(place, axis, sign))
        )
    for kind in range(4):
        for part in range(3):
            axis = spots[part][0]
            value = place[axis] if kind == 3 else spots[part][(1, 3, 2)[kind]][axis]
            pack(part, value)
            copy = remote(
                slots[part].at[1 - core, value],
                sib[part].at[value],
                core_send.at[part, kind],
                core_recv.at[part, kind],
                sibling,
            )
            copy.start()
            started.append(copy)

    def send_sum(part, stage, kind, source, device):
        copy = remote(
            source,
            lands[stage][part].at[kind],
            send.at[part, stage, kind],
            recv.at[part, stage, kind],
            device,
        )
        copy.start()
        started.append(copy)

    def sum_arrived(part, stage, kind):
        ref = lands[stage][part].at[kind]
        remote(
            ref, ref, send.at[part, stage, kind], recv.at[part, stage, kind], sibling
        ).wait_recv()

    def add(target, *others):
        shape = target.shape

        def body(step, _):
            if len(shape) == 4:
                here = (lax.div(step, shape[1]), lax.rem(step, shape[1]))
            else:
                here = (step,)
            value = target[here].astype(F32)
            for other in others:
                value = value + other[here].astype(F32)
            target[here] = value.astype(BF16)
            return 0

        count = shape[0] * shape[1] if len(shape) == 4 else shape[0]
        lax.fori_loop(0, count, body, 0, unroll=4)

    for kind in range(4):
        for part in range(3):
            axis = spots[part][0]
            value = place[axis] if kind == 3 else spots[part][1 + kind][axis]
            ref = sib[part].at[value]
            mine = slots[part].at[core, value]
            remote(
                ref, ref, core_send.at[part, kind], core_recv.at[part, kind], sibling
            ).wait_recv()
            meet(part, value)
            if kind == 0:
                send_sum(part, 0, 0, mine, spots[part][3])
            if kind == 1:
                send_sum(part, 0, 1, mine, spots[part][2])
            if kind == 2:
                sum_arrived(part, 0, 0)
                add(mine, lands[0][part].at[0])
                send_sum(part, 0, 2, mine, spots[part][3])
    held = []
    for part in range(3):
        ref = slots[part].at[core, place[spots[part][0]]]
        sum_arrived(part, 0, 1)
        sum_arrived(part, 0, 2)
        add(ref, lands[0][part].at[1], lands[0][part].at[2])
        held.append(ref)
        axis = ORDERS[part][1]
        for kind in range(3):
            far = along(place, axis, kind + 1)
            send_sum(part, 1, kind, ref.at[far[axis]], far)
    for part in range(3):
        axis = ORDERS[part][1]
        ref = held[part].at[place[axis]]
        for kind in range(3):
            sum_arrived(part, 1, kind)
        add(ref, *[lands[1][part].at[kind] for kind in range(3)])
        held[part] = ref
        axis = ORDERS[part][0]
        for kind in range(3):
            far = along(place, axis, kind + 1)
            send_sum(part, 2, kind, ref.at[far[axis]], far)
    for part in range(3):
        axis = ORDERS[part][0]
        value = held[part][place[axis]].astype(F32)
        for kind in range(3):
            sum_arrived(part, 2, kind)
            value = value + lands[2][part][kind].astype(F32)
        total[FIRST[part] : FIRST[part] + PARTS[part], :] = value
    for copy in started:
        copy.wait_send()
    for latent in range(LATENTS):
        tokens = pl.ds(latent * SEQ, SEQ)
        pltpu.make_async_copy(
            out_ref.at[tokens, :], out_hbm.at[tokens, :], store.at[0, latent]
        ).wait()
        pltpu.make_async_copy(
            h1.at[tokens, :], d_tokens_hbm.at[tokens, :], store.at[1, latent]
        ).wait()
    summed = total[...]

    def product(left, right):
        return jnp.dot(left, right, preferred_element_type=F32, precision=lax.Precision.HIGHEST)

    low = product(summed, one_hot((128, 128), -lanes, F32))
    high = product(summed, one_hot((128, 128), 128 - lanes, F32))
    summed_ref[...] = product(one_hot(square, rows, F32), low) + product(
        one_hot(square, rows + 1, F32), high
    )


def transformer_block(piece, cond, tokens, d_out):
    vmem = pl.BlockSpec(memory_space=pltpu.VMEM)
    hbm = pl.BlockSpec(memory_space=pl.ANY)
    scratch = [((2, 4, 4, 4, rows, 128), BF16) for rows in PARTS]
    scratch += [((4, 4, 4, rows, 128), BF16) for rows in PARTS]
    scratch += [((3, 4, 4, rows, 128), BF16) for rows in PARTS]
    scratch += [((3, 4, rows, 128), BF16) for rows in PARTS]
    scratch += [((3, rows, 128), BF16) for rows in PARTS]
    scratch += [
        ((BLOCK, 128), F32),
        ((ROWS, D), BF16),
        ((ROWS, D), BF16),
        ((ROWS, D), BF16),
        ((FLAT_ROWS, 128), F32),
        ((D, 6 * D), BF16),
        ((D, 3 * D), BF16),
        ((D, D), BF16),
        ((D, FF), BF16),
        ((FF, D), BF16),
        ((8, 5760), F32),
        ((16, D), F32),
        ((16, 6 * D), F32),
        ((16, 6 * D), F32),
        ((ROWS, D), F32),
        ((ROWS, 1), F32),
        ((ROWS, 3 * D), BF16),
        ((LATENTS * HEADS, SEQ, SEQ), BF16),
        ((D, ROWS), BF16),
        ((D, ROWS), BF16),
        ((ROWS, D), F32),
        ((ROWS, D), F32),
        ((D, ROWS), BF16),
        ((ROWS, FF), BF16),
        ((SEQ, FF), F32),
        ((ROWS, D), BF16),
        ((ROWS, FF), BF16),
        ((ROWS, D), BF16),
        ((ROWS, D), BF16),
        ((ROWS, 3 * D), BF16),
    ]
    sems = [(2,), (2, 4), (3, 3, 3), (3, 3, 3), (3, 4), (3, 4), (3, 4), (3, 4), (3, 3, 3), (3, 3, 3)]
    return pl.pallas_call(
        whole_kernel,
        out_shape=[
            jax.ShapeDtypeStruct((ROWS, D), BF16),
            jax.ShapeDtypeStruct((ROWS, D), F32),
            jax.ShapeDtypeStruct((LATENTS, D), F32),
            jax.ShapeDtypeStruct((BLOCK, 128), F32),
        ],
        in_specs=[vmem, vmem, hbm, hbm],
        out_specs=[hbm, hbm, vmem, vmem],
        scratch_shapes=[pltpu.VMEM(shape, dtype) for shape, dtype in scratch]
        + [pltpu.SemaphoreType.DMA(shape) for shape in sems],
        compiler_params=pltpu.CompilerParams(
            collective_id=0, has_side_effects=True, vmem_limit_bytes=63 * 1024 * 1024
        ),
        name="block",
    )(piece, cond, tokens, d_out)


def local(tokens, cond, params, d_out):
    piece = jnp.pad(params, (0, BLOCK * 128 - SHARD)).reshape(BLOCK, 128)
    out, d_tokens, d_cond, summed = transformer_block(piece, cond, tokens, d_out)
    return out, d_tokens, d_cond, summed.reshape(-1)[:SHARD]


def solution(mesh):
    placed = (P("dev", None), P("dev", None), P("dev"), P("dev", None))
    return jax.shard_map(
        local,
        mesh=mesh,
        in_specs=placed,
        out_specs=(P("dev", None), P("dev", None), P("dev", None), P("dev")),
        check_vma=False,
    )
```

```python
import functools

import jax
import jax.numpy as jnp
from jax import lax
from jax.experimental import pallas as pl
from jax.experimental.pallas import tpu as pltpu
from jax.sharding import PartitionSpec as P

D = 384
FF = 1536
HEADS = 6
SEQ = 256
LATENTS = 4
ROWS = LATENTS * SEQ
SHARD = 20778
DEVICES = 128
BLOCK = 176
PARTS = (48, 64, 64)
FIRST = (0, 48, 112)
FLAT_ROWS = 20784

ADA, BADA = 0, 6912
QKV, BQV = 6930, 10386
PROJ, BPROJ = 10392, 11544
UP, BUP = 11547, 16155
DOWN, BDOWN = 16167, 20775

HALF = DEVICES // 2

MESH = pl.DeviceIdType.MESH
BF16 = jnp.bfloat16
F32 = jnp.float32

ORDERS = ((2, 1, 0), (1, 0, 2), (0, 2, 1))


def coordinates():
    me = lax.axis_index("dev")
    return (
        lax.rem(lax.div(me, 32), 4),
        lax.rem(lax.div(me, 8), 4),
        lax.rem(lax.div(me, 2), 4),
        lax.rem(me, 2),
    )


def device_at(y, x, z, core):
    return (((y * 4 + x) * 4 + z) * 2 + core,)


def along(place, axis, step):
    moved = list(place)
    moved[axis] = lax.rem(place[axis] + step + 4, 4)
    return moved


def when(condition, action):
    if condition is None:
        action()
    else:
        pl.when(condition)(action)


def shift_parts():
    offset = lax.rem(lax.axis_index("dev") * SHARD, 1024)
    return lax.div(offset, 128), lax.rem(offset, 128)


def one_hot(shape, difference, dtype):
    rows = lax.broadcasted_iota(jnp.int32, shape, 0)
    columns = lax.broadcasted_iota(jnp.int32, shape, 1)
    return jnp.where(columns - rows == difference, 1.0, 0.0).astype(dtype)


def greet(place):
    barrier = pltpu.get_barrier_semaphore()
    partners = [along(place, axis, step) for axis in range(3) for step in (1, 2, 3)]
    partners.append([place[0], place[1], place[2], 1 - place[3]])
    for partner in partners:
        pl.semaphore_signal(barrier, inc=1, device_id=device_at(*partner), device_id_type=MESH)
    pl.semaphore_wait(barrier, len(partners))


def remote(source, target, send, recv, device):
    return pltpu.make_async_remote_copy(
        src_ref=source,
        dst_ref=target,
        send_sem=send,
        recv_sem=recv,
        device_id=device_at(*device),
        device_id_type=MESH,
    )


def dot(left, right):
    return jnp.dot(left, right, preferred_element_type=F32)


def dot_nt(left, right):
    return lax.dot_general(left, right, (((1,), (1,)), ((), ())), preferred_element_type=F32)


def dot_tn(left, right):
    return lax.dot_general(left, right, (((0,), (0,)), ((), ())), preferred_element_type=F32)


def normalize(values):
    centered = values - jnp.mean(values, axis=-1, keepdims=True)
    inverse = lax.rsqrt(jnp.mean(centered * centered, axis=-1, keepdims=True) + 1e-06)
    return centered * inverse, inverse


def norm_back(grad_norm, normed, inverse):
    return inverse * (
        grad_norm
        - jnp.mean(grad_norm, axis=-1, keepdims=True)
        - normed * jnp.mean(grad_norm * normed, axis=-1, keepdims=True)
    )


def column_sums(values):
    return jnp.sum(values, axis=0, keepdims=True)


def whole_kernel(
    piece_ref, cond_ref, tokens_hbm, grad_hbm,
    out_hbm, d_tokens_hbm, d_cond_ref, summed_ref,
    *scratch,
):
    scratch = list(scratch)

    def take(count):
        taken = scratch[:count]
        del scratch[:count]
        return taken

    slots = (take(3), take(3))
    sib = (take(3), take(3))
    lands = tuple([take(3) for _ in range(3)] for _ in range(2))
    (
        total, tokens_ref, grad_ref, out_ref,
        flat, w_ada, w_qkv, w_proj, w_up, w_down, bias,
        silu, mod, d_mod, h1, inverse1, qkv, probs, attn_t, mixed_f, mixed_t, resid,
        mlp_t, hidden, slope, d_mlp, d_pre, d_branch, d_mixed, d_qkv,
        load, store, gather_send, gather_recv, meet_send, meet_recv,
        core_send, core_recv, send, recv,
    ) = scratch
    place = coordinates()
    core = place[3]
    sibling = [place[0], place[1], place[2], 1 - core]
    owner = (place[0] < 2, place[0] >= 2)
    load_tokens = pltpu.make_async_copy(tokens_hbm, tokens_ref, load.at[0])
    load_grad = pltpu.make_async_copy(grad_hbm, grad_ref, load.at[1])
    load_tokens.start()
    load_grad.start()

    def in_half(half, y):
        return lax.div(y, 2) == half

    def spot(axis, value):
        return lax.rem(value, 2) if axis == 0 else value

    def base(half, part, stage):
        ref = slots[half][part].at[core]
        for axis in (ORDERS[part][2], ORDERS[part][1])[: 2 - stage]:
            ref = ref.at[spot(axis, place[axis])]
        return ref

    def block(half, part, stage, value):
        return base(half, part, stage).at[spot(ORDERS[part][stage], value)]

    rows, lanes = shift_parts()
    x = piece_ref[...]
    low = dot(x, one_hot((128, 128), lanes, BF16)).astype(BF16)
    high = dot(x, one_hot((128, 128), lanes - 128, BF16)).astype(BF16)
    square = (BLOCK, BLOCK)
    aligned = dot(one_hot(square, -rows, BF16), low) + dot(one_hot(square, -rows - 1, BF16), high)
    aligned = aligned.astype(BF16)

    for half in range(2):

        def lay(half=half):
            for part in range(3):
                block(half, part, 0, place[ORDERS[part][0]])[...] = aligned[
                    FIRST[part] : FIRST[part] + PARTS[part]
                ]

        when(owner[half], lay)
    greet(place)

    gathers = ([], [])

    def gather_push(half, part, stage, kind):
        axis = ORDERS[part][stage]
        ref = block(half, part, stage, place[axis])
        return remote(
            ref,
            ref,
            gather_send.at[half, part, stage, kind - 1],
            gather_recv.at[half, part, stage, kind - 1],
            along(place, axis, kind),
        )

    def cross_push(half, part, kind):
        axis = ORDERS[part][2]
        ref = block(half, part, 2, along(place, axis, -kind)[axis])
        return remote(
            ref, ref, meet_send.at[half, part, kind], meet_recv.at[half, part, kind], sibling
        )

    def launch(kept, condition, make):
        when(condition, lambda: make().start())
        kept.append((condition, make))

    def wait_sent(kept):
        for condition, make in kept:
            when(condition, lambda make=make: make().wait_send())

    def gather_start(half, stage):
        for part in range(3):
            turn = ORDERS[part].index(0)
            condition = owner[half] if stage <= turn else None
            for kind in (2, 1, 3):
                launch(
                    gathers[half],
                    condition,
                    functools.partial(gather_push, half, part, stage, kind),
                )
        if stage == 2:
            for part in range(3):
                condition = owner[half] if ORDERS[part][2] == 0 else None
                launch(gathers[half], condition, functools.partial(cross_push, half, part, 0))

    def arrival(half, part, stage, kind):
        turn = ORDERS[part].index(0)
        if stage == turn:
            return in_half(half, along(place, 0, -kind)[0])
        return owner[half] if stage < turn else None

    def gather_wait(half, stage):
        for kind in (1, 3, 2):
            for part in range(3):
                condition = arrival(half, part, stage, kind)

                def wait(part=part, kind=kind):
                    axis = ORDERS[part][stage]
                    ref = block(half, part, stage, along(place, axis, -kind)[axis])
                    remote(
                        ref,
                        ref,
                        gather_send.at[half, part, stage, kind - 1],
                        gather_recv.at[half, part, stage, kind - 1],
                        sibling,
                    ).wait_recv()

                when(condition, wait)
                if stage == 2:
                    launch(
                        gathers[half], condition, functools.partial(cross_push, half, part, kind)
                    )

    def gather_end(half):
        for kind in range(4):
            for part in range(3):
                axis = ORDERS[part][2]
                if kind == 0:
                    condition = owner[half] if axis == 0 else None
                else:
                    condition = arrival(half, part, 2, kind)

                def wait(part=part, kind=kind, axis=axis):
                    value = spot(axis, along(place, axis, -kind)[axis])
                    ref = slots[half][part].at[1 - core, value]
                    remote(
                        ref,
                        ref,
                        meet_send.at[half, part, kind],
                        meet_recv.at[half, part, kind],
                        sibling,
                    ).wait_recv()

                when(condition, wait)
        wait_sent(gathers[half])

    def first_row(index):
        return pl.multiple_of(lax.div(index * SHARD, 1024) * 8, 8)

    def slot_at(part, index):
        where = (
            lax.rem(lax.div(index, 32), 2),
            lax.rem(lax.div(index, 8), 4),
            lax.rem(lax.div(index, 2), 4),
        )
        first, second, third = ORDERS[part]
        return lax.rem(index, 2), where[third], where[second], where[first]

    def piece_tail(half, index):
        here = slots[half][2][slot_at(2, index)][48:64].astype(F32)
        return jnp.where(first_row(index + 1) - first_row(index) == 160, here[:8], here[8:])

    def unpack_one(half, index, tail):
        where = first_row(index)
        for part in range(3):
            value = slots[half][part][slot_at(part, index)].astype(F32)
            if part == 0:
                flat[pl.ds(where, 8), :] = value[:8] + tail
                flat[pl.ds(where + 8, PARTS[0] - 8), :] = value[8:]
            else:
                flat[pl.ds(where + FIRST[part], PARTS[part]), :] = value

    def unpack(half):
        tail = jnp.zeros((8, 128), F32) if half == 0 else piece_tail(0, HALF - 1)
        unpack_one(half, half * HALF, tail)

        def body(index, _):
            unpack_one(half, index, piece_tail(half, index - 1))
            return 0

        lax.fori_loop(half * HALF + 1, (half + 1) * HALF, body, 0, unroll=3)

    gather_start(0, 0)
    gather_start(1, 0)
    gather_wait(0, 0)
    gather_start(0, 1)
    gather_wait(0, 1)
    gather_start(0, 2)
    gather_wait(1, 0)
    gather_start(1, 1)
    gather_wait(0, 2)
    gather_end(0)
    gather_wait(1, 1)
    gather_start(1, 2)
    unpack(0)

    def take_matrix(target, base, height, width):
        for column in range(width):
            target[:, column * 128 : (column + 1) * 128] = flat[
                pl.ds(base + column, height, stride=width), :
            ].astype(BF16)

    def take_row(base, width, offset):
        for column in range(width):
            bias[0:1, offset + column * 128 : offset + (column + 1) * 128] = flat[
                base + column : base + column + 1, :
            ]

    def put_row(base, value):
        for column in range(value.shape[1] // 128):
            flat[base + column : base + column + 1, :] = value[
                :, column * 128 : (column + 1) * 128
            ]

    def put_block(base, width, column, value):
        for number in range(value.shape[1] // 128):
            flat[pl.ds(base + column + number, value.shape[0], stride=width), :] = value[
                :, number * 128 : (number + 1) * 128
            ]

    take_matrix(w_ada, ADA, D, 18)
    take_matrix(w_qkv, QKV, D, 9)
    take_row(BADA, 18, 0)
    take_row(BQV, 3, 2304)
    bias[0:1, 2688:3456] = jnp.zeros((1, 2 * D), F32)

    cond = cond_ref[...].astype(F32)
    silu[...] = jnp.zeros_like(silu)
    silu[0:LATENTS, :] = cond / (1.0 + jnp.exp(-cond))
    silu_low = silu[...].astype(BF16)
    mod[...] = dot(silu_low, w_ada[...]) + bias[0:1, 0:2304]
    d_mod[...] = jnp.zeros_like(d_mod)

    lane = lax.broadcasted_iota(jnp.int32, (SEQ, 128), 1)
    half = (lane < 64, lane >= 64)

    def masked(value, head):
        return jnp.where(half[head], value, jnp.zeros_like(value))

    load_tokens.wait()

    def forward_attention(latent, _):
        tokens = pl.ds(pl.multiple_of(latent * SEQ, SEQ), SEQ)
        x = tokens_ref[tokens, :].astype(F32)
        shift = mod[pl.ds(latent, 1), 0:D]
        scale = mod[pl.ds(latent, 1), D : 2 * D]
        normed, inverse = normalize(x)
        h1[tokens, :] = normed
        inverse1[tokens, :] = inverse
        attn_in = (normed * (1.0 + scale) + shift).astype(BF16)
        attn_t[:, tokens] = attn_in.T
        projected = (dot(attn_in, w_qkv[...]) + bias[0:1, 2304:3456]).astype(BF16)
        qkv[tokens, :] = projected
        for pair in range(3):
            q = projected[:, pair * 128 : (pair + 1) * 128] * jnp.asarray(0.125, BF16)
            k = projected[:, D + pair * 128 : D + (pair + 1) * 128]
            v_t = projected[:, 2 * D + pair * 128 : 2 * D + (pair + 1) * 128].T
            mixed = []
            for head in range(2):
                scores = dot_nt(masked(k, head), q)
                top = jnp.max(scores, axis=0, keepdims=True)
                powers = jnp.exp(scores - top)
                weights = (powers * (1.0 / column_sums(powers))).astype(BF16)
                probs[latent * HEADS + pair * 2 + head] = weights
                mixed.append(dot(v_t[head * 64 : (head + 1) * 64], weights))
            mixed_f[pair * 128 : (pair + 1) * 128, tokens] = jnp.concatenate(mixed, axis=0)
        return 0

    lax.fori_loop(0, 2, forward_attention, 0)
    gather_wait(1, 2)
    lax.fori_loop(2, LATENTS, forward_attention, 0)
    gather_end(1)
    unpack(1)
    take_matrix(w_proj, PROJ, D, 3)
    take_matrix(w_up, UP, D, 12)
    take_matrix(w_down, DOWN, FF, 3)
    take_row(BQV + 3, 3, 3072)
    take_row(BPROJ, 3, 3456)
    take_row(BUP, 12, 3840)
    take_row(BDOWN, 3, 5376)
    bias_v = jnp.broadcast_to(bias[0:1, 3072:3456], (8, D)).T[:, 0:1]

    chunk = 512
    load_grad.wait()

    def mlp(latent, sums):
        sum_down, sum_up, sum_proj, sum_v = sums
        tokens = pl.ds(pl.multiple_of(latent * SEQ, SEQ), SEQ)
        row = pl.ds(latent, 1)
        gate1 = mod[row, 2 * D : 3 * D]
        shift = mod[row, 3 * D : 4 * D]
        scale = mod[row, 4 * D : 5 * D]
        gate = mod[row, 5 * D : 6 * D]
        mixed = (mixed_f[:, tokens] + bias_v).astype(BF16)
        mixed_t[:, tokens] = mixed
        reached = dot_tn(mixed, w_proj[...]) + bias[0:1, 3456:3840]
        kept = tokens_ref[tokens, :].astype(F32) + gate1 * reached
        normed, inverse = normalize(kept)
        mlp_in = (normed * (1.0 + scale) + shift).astype(BF16)
        mlp_t[:, tokens] = mlp_in.T
        for start in range(0, FF, chunk):
            here = slice(start, start + chunk)
            u = dot(mlp_in, w_up[:, here]) + bias[0:1, 3840 + start : 3840 + start + chunk]
            square = u * u
            inner = u * (0.7978845608028654 + (0.7978845608028654 * 0.044715) * square)
            tangent = jnp.tanh(inner)
            above = 0.5 + 0.5 * tangent
            hidden[tokens, here] = (u * above).astype(BF16)
            rise = 0.7978845608028654 + (3 * 0.7978845608028654 * 0.044715) * square
            slope[:, here] = above + (0.5 * u) * (1.0 - tangent * tangent) * rise
        mlp_out = dot(hidden[tokens, :], w_down[...]) + bias[0:1, 5376:5760]
        out_ref[tokens, :] = (kept + gate * mlp_out).astype(BF16)
        pltpu.make_async_copy(
            out_ref.at[tokens, :], out_hbm.at[tokens, :], store.at[0, latent]
        ).start()
        grad = grad_ref[tokens, :].astype(F32)
        d_mod[row, 5 * D : 6 * D] = column_sums(grad * mlp_out)
        grad_mlp = (grad * gate).astype(BF16)
        d_mlp[tokens, :] = grad_mlp
        sum_down = sum_down + column_sums(grad_mlp.astype(F32))
        ups = []
        for start in range(0, FF, chunk):
            here = slice(start, start + chunk)
            value = (slope[:, here] * dot_nt(grad_mlp, w_down[here, :])).astype(BF16)
            d_pre[tokens, here] = value
            ups.append(column_sums(value.astype(F32)))
        sum_up = sum_up + jnp.concatenate(ups, axis=1)
        d_in = dot_nt(d_pre[tokens, :], w_up[...])
        d_mod[row, 4 * D : 5 * D] = column_sums(d_in * normed)
        d_mod[row, 3 * D : 4 * D] = column_sums(d_in)
        back = grad + norm_back(d_in * (1.0 + scale), normed, inverse)
        resid[tokens, :] = back
        d_mod[row, 2 * D : 3 * D] = column_sums(back * reached)
        low = (back * gate1).astype(BF16)
        d_branch[tokens, :] = low
        sum_proj = sum_proj + column_sums(low.astype(F32))
        mixed_grad = dot_nt(low, w_proj[...]).astype(BF16)
        d_mixed[tokens, :] = mixed_grad
        sum_v = sum_v + column_sums(mixed_grad.astype(F32))
        return sum_down, sum_up, sum_proj, sum_v

    zeros = jnp.zeros((1, D), F32)
    sum_down, sum_up, sum_proj, sum_v = lax.fori_loop(
        0, LATENTS, mlp, (zeros, jnp.zeros((1, FF), F32), zeros, zeros)
    )
    put_row(BQV + 3, sum_v)
    put_row(BDOWN, sum_down)
    put_row(BUP, sum_up)
    put_row(BPROJ, sum_proj)
    for start in range(0, FF, 256):
        here = slice(start, start + 256)
        put_block(UP, 12, start // 128, dot(mlp_t[...], d_pre[:, here]))
        put_block(DOWN + start * 3, 3, 0, dot_tn(hidden[:, here], d_mlp[...]))
    put_block(PROJ, 3, 0, dot(mixed_t[...], d_branch[...]))

    def slot_rows(half, part, c, b, a, which):
        where = [0, 0, 0]
        first, second, third = ORDERS[part]
        where[third], where[second], where[first] = c, b, a
        where[0] = where[0] + 2 * half
        return pl.ds(
            pl.multiple_of(first_row(device_at(*where, which)[0]) + FIRST[part], 8), PARTS[part]
        )

    def each_slot(part, action):
        first, second, _ = ORDERS[part]
        wide = 2 if first == 0 else 4
        count = wide * (2 if second == 0 else 4)

        def body(step, _):
            action(lax.div(step, wide), lax.rem(step, wide))
            return 0

        lax.fori_loop(0, count, body, 0, unroll=4)

    reduces = []

    def meet_push(half, part, kind):
        axis = ORDERS[part][2]
        value = kind if axis == 0 else along(place, axis, kind)[axis]
        return remote(
            slots[half][part].at[1 - core, value],
            sib[half][part].at[value],
            core_send.at[half, part, kind],
            core_recv.at[half, part, kind],
            sibling,
        )

    def meet_kinds(part):
        return (0, 1) if ORDERS[part][2] == 0 else (2, 1, 3, 0)

    def meet_start(half):
        for turn in range(4):
            for part in range(3):
                kinds = meet_kinds(part)
                if turn >= len(kinds):
                    continue
                kind = kinds[turn]
                axis = ORDERS[part][2]
                value = kind if axis == 0 else along(place, axis, kind)[axis]

                def pack(b, a, part=part, value=value):
                    slots[half][part][1 - core, value, b, a] = flat[
                        slot_rows(half, part, value, b, a, 1 - core), :
                    ].astype(BF16)

                each_slot(part, pack)
                launch(reduces, None, functools.partial(meet_push, half, part, kind))

    def sum_push(half, part, stage, kind):
        axis = ORDERS[part][stage]
        far = along(place, axis, kind)
        return remote(
            block(half, part, stage, far[axis]),
            lands[half][stage][part].at[kind - 1],
            send.at[half, part, stage, kind - 1],
            recv.at[half, part, stage, kind - 1],
            far,
        )

    def sum_start(half, part, stage, kind):
        turn = ORDERS[part].index(0)
        if stage == turn:
            condition = in_half(half, along(place, 0, kind)[0])
        else:
            condition = owner[half] if stage < turn else None
        launch(reduces, condition, functools.partial(sum_push, half, part, stage, kind))

    def meet_end(half):
        for turn in range(4):
            for part in range(3):
                kinds = meet_kinds(part)
                if turn >= len(kinds):
                    continue
                kind = kinds[turn]
                axis = ORDERS[part][2]
                value = kind if axis == 0 else along(place, axis, kind)[axis]
                meet_push(half, part, kind).wait_recv()

                def meet(b, a, part=part, value=value):
                    mine = flat[slot_rows(half, part, value, b, a, core), :]
                    other = sib[half][part][value, b, a].astype(F32)
                    slots[half][part][core, value, b, a] = (mine + other).astype(BF16)

                each_slot(part, meet)
                if axis != 0:
                    if kind != 0:
                        sum_start(half, part, 2, kind)
                elif turn == 1:
                    for kind in (2, 1, 3):
                        sum_start(half, part, 2, kind)

    def reduce_start(half, stage):
        for part in range(3):
            for kind in (2, 1, 3):
                sum_start(half, part, stage, kind)

    def reduce_wait(half, stage):
        for part in range(3):
            turn = ORDERS[part].index(0)

            def finish(part=part):
                for kind in (1, 3, 2):
                    sum_push(half, part, stage, kind).wait_recv()
                target = block(half, part, stage, place[ORDERS[part][stage]])
                others = [lands[half][stage][part].at[kind] for kind in range(3)]
                shape = target.shape
                if stage == 0:
                    value = target[...].astype(F32)
                    for other in others:
                        value = value + other[...].astype(F32)
                    total[FIRST[part] : FIRST[part] + PARTS[part], :] = value
                    return

                def body(step, _):
                    here = (lax.div(step, shape[1]), lax.rem(step, shape[1]))
                    here = here if stage == 2 else (step,)
                    value = target[here].astype(F32)
                    for other in others:
                        value = value + other[here].astype(F32)
                    target[here] = value.astype(BF16)
                    return 0

                count = shape[0] * shape[1] if stage == 2 else shape[0]
                lax.fori_loop(0, count, body, 0, unroll=min(count, 4))

            when(owner[half] if stage <= turn else None, finish)

    meet_start(1)

    def backward_attention(latent, sums):
        tokens = pl.ds(pl.multiple_of(latent * SEQ, SEQ), SEQ)
        row = pl.ds(latent, 1)
        scale = mod[row, D : 2 * D]
        projected = qkv[tokens, :]
        d_out = d_mixed[tokens, :]
        for pair in range(3):
            q = projected[:, pair * 128 : (pair + 1) * 128] * jnp.asarray(0.125, BF16)
            k_t = projected[:, D + pair * 128 : D + (pair + 1) * 128].T
            v = projected[:, 2 * D + pair * 128 : 2 * D + (pair + 1) * 128]
            above = d_out[:, pair * 128 : (pair + 1) * 128]
            grad_q, grad_k, grad_v = [], 0.0, 0.0
            for head in range(2):
                mine = masked(above, head)
                weights = probs[latent * HEADS + pair * 2 + head]
                grad_v = grad_v + dot(weights, mine)
                wide = weights.astype(F32)
                product = dot_nt(v, mine) * wide
                scores = (product - wide * column_sums(product)).astype(BF16)
                grad_k = grad_k + dot(scores, masked(q, head))
                grad_q.append(dot(k_t[head * 64 : (head + 1) * 64], scores))
            here = slice(pair * 128, (pair + 1) * 128)
            turned = (jnp.concatenate(grad_q, axis=0) * 0.125).astype(BF16)
            d_qkv[tokens, here] = turned.T
            d_qkv[tokens, D + pair * 128 : D + (pair + 1) * 128] = grad_k.astype(BF16)
            d_qkv[tokens, 2 * D + pair * 128 : 2 * D + (pair + 1) * 128] = grad_v.astype(BF16)
        low = d_qkv[tokens, :]
        normed = h1[tokens, :]
        d_in = dot_nt(low, w_qkv[...])
        d_mod[row, D : 2 * D] = column_sums(d_in * normed)
        d_mod[row, 0:D] = column_sums(d_in)
        h1[tokens, :] = resid[tokens, :] + norm_back(
            d_in * (1.0 + scale), normed, inverse1[tokens, :]
        )
        pltpu.make_async_copy(
            h1.at[tokens, :], d_tokens_hbm.at[tokens, :], store.at[1, latent]
        ).start()
        return sums + column_sums(low[:, :D].astype(F32))

    sum_q = lax.fori_loop(0, 2, backward_attention, zeros)
    meet_end(1)
    sum_q = lax.fori_loop(2, LATENTS, backward_attention, sum_q)
    put_row(BQV, sum_q)
    reduce_wait(1, 2)
    reduce_start(1, 1)
    for start in range(0, 3 * D, D):
        put_block(QKV, 9, start // 128, dot(attn_t[...], d_qkv[:, start : start + D]))
    d_mod_low = d_mod[...].astype(BF16)
    put_row(BADA, column_sums(d_mod_low.astype(F32)))
    for start in range(0, 6 * D, D):
        put_block(ADA, 18, start // 128, dot_tn(silu_low, d_mod_low[:, start : start + D]))
    d_silu = dot_nt(d_mod_low, w_ada[...])[0:LATENTS]
    gate = 1.0 / (1.0 + jnp.exp(-cond))
    d_cond_ref[...] = d_silu * (gate * (1.0 + cond * (1.0 - gate)))

    meet_start(0)
    reduce_wait(1, 1)
    reduce_start(1, 0)
    meet_end(0)
    reduce_wait(0, 2)
    reduce_start(0, 1)
    reduce_wait(1, 0)
    reduce_wait(0, 1)
    reduce_start(0, 0)
    reduce_wait(0, 0)
    wait_sent(reduces)
    for latent in range(LATENTS):
        tokens = pl.ds(latent * SEQ, SEQ)
        pltpu.make_async_copy(
            out_ref.at[tokens, :], out_hbm.at[tokens, :], store.at[0, latent]
        ).wait()
        pltpu.make_async_copy(
            h1.at[tokens, :], d_tokens_hbm.at[tokens, :], store.at[1, latent]
        ).wait()
    summed = total[...]

    def product(left, right):
        return jnp.dot(left, right, preferred_element_type=F32, precision=lax.Precision.HIGHEST)

    low = product(summed, one_hot((128, 128), -lanes, F32))
    high = product(summed, one_hot((128, 128), 128 - lanes, F32))
    summed_ref[...] = product(one_hot(square, rows, F32), low) + product(
        one_hot(square, rows + 1, F32), high
    )


def sizes(part, stage):
    return tuple(2 if axis == 0 else 4 for axis in reversed(ORDERS[part][:stage]))


def transformer_block(piece, cond, tokens, d_out):
    vmem = pl.BlockSpec(memory_space=pltpu.VMEM)
    hbm = pl.BlockSpec(memory_space=pl.ANY)
    scratch = []
    for lead in ((2,), ()):
        for _ in range(2):
            for part in range(3):
                scratch.append((lead + sizes(part, 3) + (PARTS[part], 128), BF16))
    for _ in range(2):
        for stage in range(3):
            for part in range(3):
                scratch.append(((3,) + sizes(part, stage) + (PARTS[part], 128), BF16))
    scratch += [
        ((BLOCK, 128), F32),
        ((ROWS, D), BF16),
        ((ROWS, D), BF16),
        ((ROWS, D), BF16),
        ((FLAT_ROWS, 128), F32),
        ((D, 6 * D), BF16),
        ((D, 3 * D), BF16),
        ((D, D), BF16),
        ((D, FF), BF16),
        ((FF, D), BF16),
        ((8, 5760), F32),
        ((16, D), F32),
        ((16, 6 * D), F32),
        ((16, 6 * D), F32),
        ((ROWS, D), F32),
        ((ROWS, 1), F32),
        ((ROWS, 3 * D), BF16),
        ((LATENTS * HEADS, SEQ, SEQ), BF16),
        ((D, ROWS), BF16),
        ((D, ROWS), F32),
        ((D, ROWS), BF16),
        ((ROWS, D), F32),
        ((D, ROWS), BF16),
        ((ROWS, FF), BF16),
        ((SEQ, FF), F32),
        ((ROWS, D), BF16),
        ((ROWS, FF), BF16),
        ((ROWS, D), BF16),
        ((ROWS, D), BF16),
        ((ROWS, 3 * D), BF16),
    ]
    sems = [(2,), (2, 4)]
    sems += [(2, 3, 3, 3)] * 2 + [(2, 3, 4)] * 4 + [(2, 3, 3, 3)] * 2
    return pl.pallas_call(
        whole_kernel,
        out_shape=[
            jax.ShapeDtypeStruct((ROWS, D), BF16),
            jax.ShapeDtypeStruct((ROWS, D), F32),
            jax.ShapeDtypeStruct((LATENTS, D), F32),
            jax.ShapeDtypeStruct((BLOCK, 128), F32),
        ],
        in_specs=[vmem, vmem, hbm, hbm],
        out_specs=[hbm, hbm, vmem, vmem],
        scratch_shapes=[pltpu.VMEM(shape, dtype) for shape, dtype in scratch]
        + [pltpu.SemaphoreType.DMA(shape) for shape in sems],
        compiler_params=pltpu.CompilerParams(
            collective_id=0, has_side_effects=True, vmem_limit_bytes=63 * 1024 * 1024
        ),
        name="block",
    )(piece, cond, tokens, d_out)


def local(tokens, cond, params, d_out):
    piece = jnp.pad(params, (0, BLOCK * 128 - SHARD)).reshape(BLOCK, 128)
    out, d_tokens, d_cond, summed = transformer_block(piece, cond, tokens, d_out)
    return out, d_tokens, d_cond, summed.reshape(-1)[:SHARD]


def solution(mesh):
    placed = (P("dev", None), P("dev", None), P("dev"), P("dev", None))
    return jax.shard_map(
        local,
        mesh=mesh,
        in_specs=placed,
        out_specs=(P("dev", None), P("dev", None), P("dev", None), P("dev")),
        check_vma=False,
    )
```

```python
import functools

import jax
import jax.numpy as jnp
from jax import lax
from jax.experimental import pallas as pl
from jax.experimental.pallas import tpu as pltpu
from jax.sharding import PartitionSpec as P

D = 384
FF = 1536
HEADS = 6
SEQ = 256
LATENTS = 4
ROWS = LATENTS * SEQ
SHARD = 20778
DEVICES = 128
BLOCK = 176
PARTS = (64, 64, 48)
FIRST = (0, 64, 128)
FLAT_ROWS = 20784

ADA, BADA = 0, 6912
QKV, BQV = 6930, 10386
PROJ, BPROJ = 10392, 11544
UP, BUP = 11547, 16155
DOWN, BDOWN = 16167, 20775

HALF = DEVICES // 2

MESH = pl.DeviceIdType.MESH
BF16 = jnp.bfloat16
F32 = jnp.float32

ORDERS = ((2, 1, 0), (1, 0, 2), (2, 0, 1))


def coordinates():
    me = lax.axis_index("dev")
    return (
        lax.rem(lax.div(me, 32), 4),
        lax.rem(lax.div(me, 8), 4),
        lax.rem(lax.div(me, 2), 4),
        lax.rem(me, 2),
    )


def device_at(y, x, z, core):
    return (((y * 4 + x) * 4 + z) * 2 + core,)


def along(place, axis, step):
    moved = list(place)
    moved[axis] = lax.rem(place[axis] + step + 4, 4)
    return moved


def when(condition, action):
    if condition is None:
        action()
    else:
        pl.when(condition)(action)


def shift_parts():
    offset = lax.rem(lax.axis_index("dev") * SHARD, 1024)
    return lax.div(offset, 128), lax.rem(offset, 128)


def one_hot(shape, difference, dtype):
    rows = lax.broadcasted_iota(jnp.int32, shape, 0)
    columns = lax.broadcasted_iota(jnp.int32, shape, 1)
    return jnp.where(columns - rows == difference, 1.0, 0.0).astype(dtype)


def greet(place):
    barrier = pltpu.get_barrier_semaphore()
    partners = [along(place, axis, step) for axis in range(3) for step in (1, 2, 3)]
    partners.append([place[0], place[1], place[2], 1 - place[3]])
    for partner in partners:
        pl.semaphore_signal(barrier, inc=1, device_id=device_at(*partner), device_id_type=MESH)
    pl.semaphore_wait(barrier, len(partners))


def remote(source, target, send, recv, device):
    return pltpu.make_async_remote_copy(
        src_ref=source,
        dst_ref=target,
        send_sem=send,
        recv_sem=recv,
        device_id=device_at(*device),
        device_id_type=MESH,
    )


def dot(left, right):
    return jnp.dot(left, right, preferred_element_type=F32)


def dot_nt(left, right):
    return lax.dot_general(left, right, (((1,), (1,)), ((), ())), preferred_element_type=F32)


def dot_tn(left, right):
    return lax.dot_general(left, right, (((0,), (0,)), ((), ())), preferred_element_type=F32)


def normalize(values):
    centered = values - jnp.mean(values, axis=-1, keepdims=True)
    inverse = lax.rsqrt(jnp.mean(centered * centered, axis=-1, keepdims=True) + 1e-06)
    return centered * inverse, inverse


def norm_back(grad_norm, normed, inverse):
    return inverse * (
        grad_norm
        - jnp.mean(grad_norm, axis=-1, keepdims=True)
        - normed * jnp.mean(grad_norm * normed, axis=-1, keepdims=True)
    )


def column_sums(values):
    return jnp.sum(values, axis=0, keepdims=True)


def whole_kernel(
    piece_ref, cond_ref, tokens_hbm, grad_hbm,
    out_hbm, d_tokens_hbm, d_cond_ref, summed_ref,
    *scratch,
):
    scratch = list(scratch)

    def take(count):
        taken = scratch[:count]
        del scratch[:count]
        return taken

    slots = take(3)
    sib = take(3)
    lands = [take(3) for _ in range(3)]
    (
        total, tokens_ref, grad_ref, out_ref,
        flat, w_ada, w_qkv, w_proj, w_up, w_down, bias,
        silu, mod, d_mod, h1, inverse1, qkv, probs, attn_t, mixed_f, mixed_t, resid,
        mlp_t, hidden, slope, d_mlp, d_pre, d_branch, d_mixed, d_qkv,
        load, store, gather_send, gather_recv, last_send, last_recv, meet_send, meet_recv,
        core_send, core_recv, far_send, far_recv, send, recv,
    ) = scratch
    place = coordinates()
    core = place[3]
    sibling = [place[0], place[1], place[2], 1 - core]
    load_tokens = pltpu.make_async_copy(tokens_hbm, tokens_ref, load.at[0])
    load_grad = pltpu.make_async_copy(grad_hbm, grad_ref, load.at[1])
    load_tokens.start()
    load_grad.start()

    def in_half(half, y):
        return lax.div(y, 2) == half

    def base(part, stage):
        ref = slots[part].at[core]
        for axis in (ORDERS[part][2], ORDERS[part][1])[: 2 - stage]:
            ref = ref.at[place[axis]]
        return ref

    def block(part, stage, value):
        return base(part, stage).at[value]

    def half_block(half, part, which, value):
        ref = slots[part].at[which, value]
        return ref if part == 0 else ref.at[2 * half : 2 * half + 2]

    rows, lanes = shift_parts()
    x = piece_ref[...]
    low = dot(x, one_hot((128, 128), lanes, BF16)).astype(BF16)
    high = dot(x, one_hot((128, 128), lanes - 128, BF16)).astype(BF16)
    square = (BLOCK, BLOCK)
    aligned = dot(one_hot(square, -rows, BF16), low) + dot(one_hot(square, -rows - 1, BF16), high)
    aligned = aligned.astype(BF16)

    for part in range(3):
        block(part, 0, place[ORDERS[part][0]])[...] = aligned[
            FIRST[part] : FIRST[part] + PARTS[part]
        ]
    greet(place)

    gathers = ([], [])

    def launch(kept, condition, make):
        when(condition, lambda: make().start())
        kept.append((condition, make))

    def wait_sent(kept):
        for condition, make in kept:
            when(condition, lambda make=make: make().wait_send())

    def near(part, stage, kind, from_me):
        axis = ORDERS[part][stage]
        value = place[axis] if from_me else along(place, axis, -kind)[axis]
        ref = block(part, stage, value)
        sems = (gather_send.at[part, stage, kind - 1], gather_recv.at[part, stage, kind - 1])
        return remote(ref, ref, *sems, along(place, axis, kind))

    def gather_stage(stage):
        for part in range(3):
            for kind in (2, 1, 3):
                launch(gathers[0], None, functools.partial(near, part, stage, kind, True))
        for kind in (1, 3, 2):
            for part in range(3):
                near(part, stage, kind, False).wait_recv()

    def last(half, part, kind, from_me):
        axis = ORDERS[part][2]
        value = place[axis] if from_me else along(place, axis, -kind)[axis]
        ref = half_block(half, part, core, value)
        sems = (last_send.at[half, part, kind - 1], last_recv.at[half, part, kind - 1])
        return remote(ref, ref, *sems, along(place, axis, kind))

    def cross(half, part, kind, which):
        axis = ORDERS[part][2]
        ref = half_block(half, part, which, along(place, axis, -kind)[axis])
        return remote(
            ref, ref, meet_send.at[half, part, kind], meet_recv.at[half, part, kind], sibling
        )

    def arrival(half, part, kind):
        return in_half(half, along(place, 0, -kind)[0]) if part == 0 else None

    def gather_start(half):
        for kind in (2, 1, 3):
            for part in range(3):
                launch(
                    gathers[half],
                    arrival(half, part, 0),
                    functools.partial(last, half, part, kind, True),
                )
        for part in range(3):
            launch(
                gathers[half],
                arrival(half, part, 0),
                functools.partial(cross, half, part, 0, core),
            )

    def gather_wait(half):
        for kind in (1, 3, 2):
            for part in range(3):
                condition = arrival(half, part, kind)
                when(
                    condition,
                    lambda part=part, kind=kind: last(half, part, kind, False).wait_recv(),
                )
                launch(
                    gathers[half],
                    condition,
                    functools.partial(cross, half, part, kind, core),
                )

    def gather_end(half):
        for kind in range(4):
            for part in range(3):
                when(
                    arrival(half, part, kind),
                    lambda part=part, kind=kind: cross(half, part, kind, 1 - core).wait_recv(),
                )
        wait_sent(gathers[half])

    def first_row(index):
        return pl.multiple_of(lax.div(index * SHARD, 1024) * 8, 8)

    def slot_at(part, index):
        where = (
            lax.rem(lax.div(index, 32), 4),
            lax.rem(lax.div(index, 8), 4),
            lax.rem(lax.div(index, 2), 4),
        )
        first, second, third = ORDERS[part]
        return lax.rem(index, 2), where[third], where[second], where[first]

    def piece_tail(index):
        here = slots[2][slot_at(2, index)][32:48].astype(F32)
        return jnp.where(first_row(index + 1) - first_row(index) == 160, here[:8], here[8:])

    def unpack_one(index, tail):
        where = first_row(index)
        for part in range(3):
            value = slots[part][slot_at(part, index)].astype(F32)
            if part == 0:
                flat[pl.ds(where, 8), :] = value[:8] + tail
                flat[pl.ds(where + 8, PARTS[0] - 8), :] = value[8:]
            else:
                flat[pl.ds(where + FIRST[part], PARTS[part]), :] = value

    def unpack(half):
        tail = jnp.zeros((8, 128), F32) if half == 0 else piece_tail(HALF - 1)
        unpack_one(half * HALF, tail)

        def body(index, _):
            unpack_one(index, piece_tail(index - 1))
            return 0

        lax.fori_loop(half * HALF + 1, (half + 1) * HALF, body, 0, unroll=3)

    gather_stage(0)
    gather_stage(1)
    gather_start(0)
    gather_wait(0)
    gather_end(0)
    gather_start(1)
    unpack(0)

    def take_matrix(target, base, height, width):
        for column in range(width):
            target[:, column * 128 : (column + 1) * 128] = flat[
                pl.ds(base + column, height, stride=width), :
            ].astype(BF16)

    def take_row(base, width, offset):
        for column in range(width):
            bias[0:1, offset + column * 128 : offset + (column + 1) * 128] = flat[
                base + column : base + column + 1, :
            ]

    def put_row(base, value):
        for column in range(value.shape[1] // 128):
            flat[base + column : base + column + 1, :] = value[
                :, column * 128 : (column + 1) * 128
            ]

    def put_block(base, width, column, value):
        for number in range(value.shape[1] // 128):
            flat[pl.ds(base + column + number, value.shape[0], stride=width), :] = value[
                :, number * 128 : (number + 1) * 128
            ]

    take_matrix(w_ada, ADA, D, 18)
    take_matrix(w_qkv, QKV, D, 9)
    take_row(BADA, 18, 0)
    take_row(BQV, 3, 2304)
    bias[0:1, 2688:3456] = jnp.zeros((1, 2 * D), F32)

    cond = cond_ref[...].astype(F32)
    silu[...] = jnp.zeros_like(silu)
    silu[0:LATENTS, :] = cond / (1.0 + jnp.exp(-cond))
    silu_low = silu[...].astype(BF16)
    mod[...] = dot(silu_low, w_ada[...]) + bias[0:1, 0:2304]
    d_mod[...] = jnp.zeros_like(d_mod)

    lane = lax.broadcasted_iota(jnp.int32, (SEQ, 128), 1)
    half = (lane < 64, lane >= 64)

    def masked(value, head):
        return jnp.where(half[head], value, jnp.zeros_like(value))

    load_tokens.wait()

    def forward_attention(latent, _):
        tokens = pl.ds(pl.multiple_of(latent * SEQ, SEQ), SEQ)
        x = tokens_ref[tokens, :].astype(F32)
        shift = mod[pl.ds(latent, 1), 0:D]
        scale = mod[pl.ds(latent, 1), D : 2 * D]
        normed, inverse = normalize(x)
        h1[tokens, :] = normed
        inverse1[tokens, :] = inverse
        attn_in = (normed * (1.0 + scale) + shift).astype(BF16)
        attn_t[:, tokens] = attn_in.T
        projected = (dot(attn_in, w_qkv[...]) + bias[0:1, 2304:3456]).astype(BF16)
        qkv[tokens, :] = projected
        for pair in range(3):
            q = projected[:, pair * 128 : (pair + 1) * 128] * jnp.asarray(0.125, BF16)
            k = projected[:, D + pair * 128 : D + (pair + 1) * 128]
            v_t = projected[:, 2 * D + pair * 128 : 2 * D + (pair + 1) * 128].T
            mixed = []
            for head in range(2):
                scores = dot_nt(masked(k, head), q)
                top = jnp.max(scores, axis=0, keepdims=True)
                powers = jnp.exp(scores - top)
                weights = (powers * (1.0 / column_sums(powers))).astype(BF16)
                probs[latent * HEADS + pair * 2 + head] = weights
                mixed.append(dot(v_t[head * 64 : (head + 1) * 64], weights))
            mixed_f[pair * 128 : (pair + 1) * 128, tokens] = jnp.concatenate(mixed, axis=0)
        return 0

    lax.fori_loop(0, 2, forward_attention, 0)
    gather_wait(1)
    lax.fori_loop(2, LATENTS, forward_attention, 0)
    gather_end(1)
    unpack(1)
    take_matrix(w_proj, PROJ, D, 3)
    take_matrix(w_up, UP, D, 12)
    take_matrix(w_down, DOWN, FF, 3)
    take_row(BQV + 3, 3, 3072)
    take_row(BPROJ, 3, 3456)
    take_row(BUP, 12, 3840)
    take_row(BDOWN, 3, 5376)
    bias_v = jnp.broadcast_to(bias[0:1, 3072:3456], (8, D)).T[:, 0:1]

    chunk = 512
    load_grad.wait()

    def mlp(latent, sums):
        sum_down, sum_up, sum_proj, sum_v = sums
        tokens = pl.ds(pl.multiple_of(latent * SEQ, SEQ), SEQ)
        row = pl.ds(latent, 1)
        gate1 = mod[row, 2 * D : 3 * D]
        shift = mod[row, 3 * D : 4 * D]
        scale = mod[row, 4 * D : 5 * D]
        gate = mod[row, 5 * D : 6 * D]
        mixed = (mixed_f[:, tokens] + bias_v).astype(BF16)
        mixed_t[:, tokens] = mixed
        reached = dot_tn(mixed, w_proj[...]) + bias[0:1, 3456:3840]
        kept = tokens_ref[tokens, :].astype(F32) + gate1 * reached
        normed, inverse = normalize(kept)
        mlp_in = (normed * (1.0 + scale) + shift).astype(BF16)
        mlp_t[:, tokens] = mlp_in.T
        for start in range(0, FF, chunk):
            here = slice(start, start + chunk)
            u = dot(mlp_in, w_up[:, here]) + bias[0:1, 3840 + start : 3840 + start + chunk]
            square = u * u
            inner = u * (0.7978845608028654 + (0.7978845608028654 * 0.044715) * square)
            tangent = jnp.tanh(inner)
            above = 0.5 + 0.5 * tangent
            hidden[tokens, here] = (u * above).astype(BF16)
            rise = 0.7978845608028654 + (3 * 0.7978845608028654 * 0.044715) * square
            slope[:, here] = above + (0.5 * u) * (1.0 - tangent * tangent) * rise
        mlp_out = dot(hidden[tokens, :], w_down[...]) + bias[0:1, 5376:5760]
        out_ref[tokens, :] = (kept + gate * mlp_out).astype(BF16)
        pltpu.make_async_copy(
            out_ref.at[tokens, :], out_hbm.at[tokens, :], store.at[0, latent]
        ).start()
        grad = grad_ref[tokens, :].astype(F32)
        d_mod[row, 5 * D : 6 * D] = column_sums(grad * mlp_out)
        grad_mlp = (grad * gate).astype(BF16)
        d_mlp[tokens, :] = grad_mlp
        sum_down = sum_down + column_sums(grad_mlp.astype(F32))
        ups = []
        for start in range(0, FF, chunk):
            here = slice(start, start + chunk)
            value = (slope[:, here] * dot_nt(grad_mlp, w_down[here, :])).astype(BF16)
            d_pre[tokens, here] = value
            ups.append(column_sums(value.astype(F32)))
        sum_up = sum_up + jnp.concatenate(ups, axis=1)
        d_in = dot_nt(d_pre[tokens, :], w_up[...])
        d_mod[row, 4 * D : 5 * D] = column_sums(d_in * normed)
        d_mod[row, 3 * D : 4 * D] = column_sums(d_in)
        back = grad + norm_back(d_in * (1.0 + scale), normed, inverse)
        resid[tokens, :] = back
        d_mod[row, 2 * D : 3 * D] = column_sums(back * reached)
        low = (back * gate1).astype(BF16)
        d_branch[tokens, :] = low
        sum_proj = sum_proj + column_sums(low.astype(F32))
        mixed_grad = dot_nt(low, w_proj[...]).astype(BF16)
        d_mixed[tokens, :] = mixed_grad
        sum_v = sum_v + column_sums(mixed_grad.astype(F32))
        return sum_down, sum_up, sum_proj, sum_v

    zeros = jnp.zeros((1, D), F32)
    sum_down, sum_up, sum_proj, sum_v = lax.fori_loop(
        0, LATENTS, mlp, (zeros, jnp.zeros((1, FF), F32), zeros, zeros)
    )
    put_row(BQV + 3, sum_v)
    put_row(BDOWN, sum_down)
    put_row(BUP, sum_up)
    put_row(BPROJ, sum_proj)
    for start in range(0, FF, 256):
        here = slice(start, start + 256)
        put_block(UP, 12, start // 128, dot(mlp_t[...], d_pre[:, here]))
        put_block(DOWN + start * 3, 3, 0, dot_tn(hidden[:, here], d_mlp[...]))
    put_block(PROJ, 3, 0, dot(mixed_t[...], d_branch[...]))

    def slot_rows(part, c, b, a, which):
        where = [0, 0, 0]
        first, second, third = ORDERS[part]
        where[third], where[second], where[first] = c, b, a
        return pl.ds(
            pl.multiple_of(first_row(device_at(*where, which)[0]) + FIRST[part], 8), PARTS[part]
        )

    def each_slot(half, part, action):
        begin, count = (0, 16) if part == 0 else (8 * half, 8)

        def body(step, _):
            action(lax.div(step, 4), lax.rem(step, 4))
            return 0

        lax.fori_loop(begin, begin + count, body, 0, unroll=4)

    reduces = []

    def meet_value(half, part, kind):
        return 2 * half + kind if part == 0 else along(place, ORDERS[part][2], kind)[ORDERS[part][2]]

    def meet_turns():
        return [
            (part, (0, 1) if part == 0 else (2, 1, 3, 0), turn)
            for turn in range(4)
            for part in range(3)
            if turn < (2 if part == 0 else 4)
        ]

    def meet_push(half, part, kind):
        value = meet_value(half, part, kind)
        target = sib[part].at[value]
        return remote(
            half_block(half, part, 1 - core, value),
            target if part == 0 else target.at[2 * half : 2 * half + 2],
            core_send.at[half, part, kind],
            core_recv.at[half, part, kind],
            sibling,
        )

    def meet_start(half):
        for part, kinds, turn in meet_turns():
            value = meet_value(half, part, kinds[turn])

            def pack(b, a, part=part, value=value):
                slots[part][1 - core, value, b, a] = flat[
                    slot_rows(part, value, b, a, 1 - core), :
                ].astype(BF16)

            each_slot(half, part, pack)
            launch(reduces, None, functools.partial(meet_push, half, part, kinds[turn]))

    def far_push(half, part, kind):
        far = along(place, ORDERS[part][2], kind)
        land = lands[2][part].at[kind - 1]
        which = 0 if part == 0 else half
        return remote(
            half_block(half, part, core, far[ORDERS[part][2]]),
            land if part == 0 else land.at[2 * half : 2 * half + 2],
            far_send.at[which, part, kind - 1],
            far_recv.at[which, part, kind - 1],
            far,
        )

    def meet_end(half):
        for part, kinds, turn in meet_turns():
            kind = kinds[turn]
            value = meet_value(half, part, kind)
            meet_push(half, part, kind).wait_recv()

            def meet(b, a, part=part, value=value):
                mine = flat[slot_rows(part, value, b, a, core), :]
                other = sib[part][value, b, a].astype(F32)
                slots[part][core, value, b, a] = (mine + other).astype(BF16)

            each_slot(half, part, meet)
            if part == 0 and turn == 1:
                for kind in (2, 1, 3):
                    launch(
                        reduces,
                        in_half(half, along(place, 0, kind)[0]),
                        functools.partial(far_push, half, 0, kind),
                    )
            if part != 0 and kind != 0:
                launch(reduces, None, functools.partial(far_push, half, part, kind))

    def add(target, others, begin, count):
        def body(step, _):
            here = (lax.div(step, 4), lax.rem(step, 4)) if len(target.shape) == 4 else (step,)
            value = target[here].astype(F32)
            for other in others:
                value = value + other[here].astype(F32)
            target[here] = value.astype(BF16)
            return 0

        lax.fori_loop(begin, begin + count, body, 0, unroll=4)

    def far_wait(half, part):
        for kind in (1, 3, 2):
            far_push(half, part, kind).wait_recv()
        others = [lands[2][part].at[kind] for kind in range(3)]
        begin, count = (0, 16) if part == 0 else (8 * half, 8)
        add(block(part, 2, place[ORDERS[part][2]]), others, begin, count)

    def sum_push(part, stage, kind):
        axis = ORDERS[part][stage]
        far = along(place, axis, kind)
        return remote(
            block(part, stage, far[axis]),
            lands[stage][part].at[kind - 1],
            send.at[part, stage, kind - 1],
            recv.at[part, stage, kind - 1],
            far,
        )

    def reduce_start(part, stage):
        for kind in (2, 1, 3):
            launch(reduces, None, functools.partial(sum_push, part, stage, kind))

    def reduce_wait(part, stage):
        for kind in (1, 3, 2):
            sum_push(part, stage, kind).wait_recv()
        target = block(part, stage, place[ORDERS[part][stage]])
        others = [lands[stage][part].at[kind] for kind in range(3)]
        if stage == 1:
            add(target, others, 0, 4)
            return
        value = target[...].astype(F32)
        for other in others:
            value = value + other[...].astype(F32)
        total[FIRST[part] : FIRST[part] + PARTS[part], :] = value

    meet_start(1)

    def backward_attention(latent, sums):
        tokens = pl.ds(pl.multiple_of(latent * SEQ, SEQ), SEQ)
        row = pl.ds(latent, 1)
        scale = mod[row, D : 2 * D]
        projected = qkv[tokens, :]
        d_out = d_mixed[tokens, :]
        for pair in range(3):
            q = projected[:, pair * 128 : (pair + 1) * 128] * jnp.asarray(0.125, BF16)
            k_t = projected[:, D + pair * 128 : D + (pair + 1) * 128].T
            v = projected[:, 2 * D + pair * 128 : 2 * D + (pair + 1) * 128]
            above = d_out[:, pair * 128 : (pair + 1) * 128]
            grad_q, grad_k, grad_v = [], 0.0, 0.0
            for head in range(2):
                mine = masked(above, head)
                weights = probs[latent * HEADS + pair * 2 + head]
                grad_v = grad_v + dot(weights, mine)
                wide = weights.astype(F32)
                product = dot_nt(v, mine) * wide
                scores = (product - wide * column_sums(product)).astype(BF16)
                grad_k = grad_k + dot(scores, masked(q, head))
                grad_q.append(dot(k_t[head * 64 : (head + 1) * 64], scores))
            here = slice(pair * 128, (pair + 1) * 128)
            turned = (jnp.concatenate(grad_q, axis=0) * 0.125).astype(BF16)
            d_qkv[tokens, here] = turned.T
            d_qkv[tokens, D + pair * 128 : D + (pair + 1) * 128] = grad_k.astype(BF16)
            d_qkv[tokens, 2 * D + pair * 128 : 2 * D + (pair + 1) * 128] = grad_v.astype(BF16)
        low = d_qkv[tokens, :]
        normed = h1[tokens, :]
        d_in = dot_nt(low, w_qkv[...])
        d_mod[row, D : 2 * D] = column_sums(d_in * normed)
        d_mod[row, 0:D] = column_sums(d_in)
        h1[tokens, :] = resid[tokens, :] + norm_back(
            d_in * (1.0 + scale), normed, inverse1[tokens, :]
        )
        pltpu.make_async_copy(
            h1.at[tokens, :], d_tokens_hbm.at[tokens, :], store.at[1, latent]
        ).start()
        return sums + column_sums(low[:, :D].astype(F32))

    sum_q = lax.fori_loop(0, 2, backward_attention, zeros)
    meet_end(1)
    sum_q = lax.fori_loop(2, LATENTS, backward_attention, sum_q)
    put_row(BQV, sum_q)
    far_wait(1, 1)
    far_wait(1, 2)
    for start in range(0, 3 * D, D):
        put_block(QKV, 9, start // 128, dot(attn_t[...], d_qkv[:, start : start + D]))
    d_mod_low = d_mod[...].astype(BF16)
    put_row(BADA, column_sums(d_mod_low.astype(F32)))
    for start in range(0, 6 * D, D):
        put_block(ADA, 18, start // 128, dot_tn(silu_low, d_mod_low[:, start : start + D]))
    d_silu = dot_nt(d_mod_low, w_ada[...])[0:LATENTS]
    gate = 1.0 / (1.0 + jnp.exp(-cond))
    d_cond_ref[...] = d_silu * (gate * (1.0 + cond * (1.0 - gate)))

    meet_start(0)
    meet_end(0)
    for part in range(3):
        far_wait(0, part)
        reduce_start(part, 1)
    for part in range(3):
        reduce_wait(part, 1)
        reduce_start(part, 0)
    for part in range(3):
        reduce_wait(part, 0)
    wait_sent(reduces)
    for latent in range(LATENTS):
        tokens = pl.ds(latent * SEQ, SEQ)
        pltpu.make_async_copy(
            out_ref.at[tokens, :], out_hbm.at[tokens, :], store.at[0, latent]
        ).wait()
        pltpu.make_async_copy(
            h1.at[tokens, :], d_tokens_hbm.at[tokens, :], store.at[1, latent]
        ).wait()
    summed = total[...]

    def product(left, right):
        return jnp.dot(left, right, preferred_element_type=F32, precision=lax.Precision.HIGHEST)

    low = product(summed, one_hot((128, 128), -lanes, F32))
    high = product(summed, one_hot((128, 128), 128 - lanes, F32))
    summed_ref[...] = product(one_hot(square, rows, F32), low) + product(
        one_hot(square, rows + 1, F32), high
    )


def transformer_block(piece, cond, tokens, d_out):
    vmem = pl.BlockSpec(memory_space=pltpu.VMEM)
    hbm = pl.BlockSpec(memory_space=pl.ANY)
    scratch = [((2, 4, 4, 4, rows, 128), BF16) for rows in PARTS]
    scratch += [((4, 4, 4, rows, 128), BF16) for rows in PARTS]
    for lead in ((3,), (3, 4), (3, 4, 4)):
        scratch += [(lead + (rows, 128), BF16) for rows in PARTS]
    scratch += [
        ((BLOCK, 128), F32),
        ((ROWS, D), BF16),
        ((ROWS, D), BF16),
        ((ROWS, D), BF16),
        ((FLAT_ROWS, 128), F32),
        ((D, 6 * D), BF16),
        ((D, 3 * D), BF16),
        ((D, D), BF16),
        ((D, FF), BF16),
        ((FF, D), BF16),
        ((8, 5760), F32),
        ((16, D), F32),
        ((16, 6 * D), F32),
        ((16, 6 * D), F32),
        ((ROWS, D), F32),
        ((ROWS, 1), F32),
        ((ROWS, 3 * D), BF16),
        ((LATENTS * HEADS, SEQ, SEQ), BF16),
        ((D, ROWS), BF16),
        ((D, ROWS), F32),
        ((D, ROWS), BF16),
        ((ROWS, D), F32),
        ((D, ROWS), BF16),
        ((ROWS, FF), BF16),
        ((SEQ, FF), F32),
        ((ROWS, D), BF16),
        ((ROWS, FF), BF16),
        ((ROWS, D), BF16),
        ((ROWS, D), BF16),
        ((ROWS, 3 * D), BF16),
    ]
    sems = [(2,), (2, 4)]
    sems += [(3, 2, 3)] * 2 + [(2, 3, 3)] * 2 + [(2, 3, 4)] * 4 + [(2, 3, 3)] * 2 + [(3, 2, 3)] * 2
    return pl.pallas_call(
        whole_kernel,
        out_shape=[
            jax.ShapeDtypeStruct((ROWS, D), BF16),
            jax.ShapeDtypeStruct((ROWS, D), F32),
            jax.ShapeDtypeStruct((LATENTS, D), F32),
            jax.ShapeDtypeStruct((BLOCK, 128), F32),
        ],
        in_specs=[vmem, vmem, hbm, hbm],
        out_specs=[hbm, hbm, vmem, vmem],
        scratch_shapes=[pltpu.VMEM(shape, dtype) for shape, dtype in scratch]
        + [pltpu.SemaphoreType.DMA(shape) for shape in sems],
        compiler_params=pltpu.CompilerParams(
            collective_id=0, has_side_effects=True, vmem_limit_bytes=63 * 1024 * 1024
        ),
        name="block",
    )(piece, cond, tokens, d_out)


def local(tokens, cond, params, d_out):
    piece = jnp.pad(params, (0, BLOCK * 128 - SHARD)).reshape(BLOCK, 128)
    out, d_tokens, d_cond, summed = transformer_block(piece, cond, tokens, d_out)
    return out, d_tokens, d_cond, summed.reshape(-1)[:SHARD]


def solution(mesh):
    placed = (P("dev", None), P("dev", None), P("dev"), P("dev", None))
    return jax.shard_map(
        local,
        mesh=mesh,
        in_specs=placed,
        out_specs=(P("dev", None), P("dev", None), P("dev", None), P("dev")),
        check_vma=False,
    )
```

```python
import functools

import jax
import jax.numpy as jnp
from jax import lax
from jax.experimental import pallas as pl
from jax.experimental.pallas import tpu as pltpu
from jax.sharding import PartitionSpec as P

D = 384
FF = 1536
HEADS = 6
SEQ = 256
LATENTS = 4
ROWS = LATENTS * SEQ
SHARD = 20778
DEVICES = 128
BLOCK = 176
PARTS = (64, 64, 48)
FIRST = (0, 64, 128)
FLAT_ROWS = 20784

ADA, BADA = 0, 6912
QKV, BQV = 6930, 10386
PROJ, BPROJ = 10392, 11544
UP, BUP = 11547, 16155
DOWN, BDOWN = 16167, 20775

MESH = pl.DeviceIdType.MESH
BF16 = jnp.bfloat16
F32 = jnp.float32

ORDERS = ((2, 1, 0), (1, 0, 2), (0, 2, 1))


def coordinates():
    me = lax.axis_index("dev")
    return (
        lax.rem(lax.div(me, 32), 4),
        lax.rem(lax.div(me, 8), 4),
        lax.rem(lax.div(me, 2), 4),
        lax.rem(me, 2),
    )


def device_at(y, x, z, core):
    return (((y * 4 + x) * 4 + z) * 2 + core,)


def along(place, axis, step):
    moved = list(place)
    moved[axis] = lax.rem(place[axis] + step + 4, 4)
    return moved


def slot_at(part, index):
    place = (
        lax.rem(lax.div(index, 32), 4),
        lax.rem(lax.div(index, 8), 4),
        lax.rem(lax.div(index, 2), 4),
    )
    first, second, third = ORDERS[part]
    return lax.rem(index, 2), place[third], place[second], place[first]


def shift_parts():
    offset = lax.rem(lax.axis_index("dev") * SHARD, 1024)
    return lax.div(offset, 128), lax.rem(offset, 128)


def one_hot(shape, difference, dtype):
    rows = lax.broadcasted_iota(jnp.int32, shape, 0)
    columns = lax.broadcasted_iota(jnp.int32, shape, 1)
    return jnp.where(columns - rows == difference, 1.0, 0.0).astype(dtype)


def greet(place):
    barrier = pltpu.get_barrier_semaphore()
    partners = [along(place, axis, step) for axis in range(3) for step in (1, 2, 3)]
    partners.append([place[0], place[1], place[2], 1 - place[3]])
    for partner in partners:
        pl.semaphore_signal(barrier, inc=1, device_id=device_at(*partner), device_id_type=MESH)
    pl.semaphore_wait(barrier, len(partners))


def remote(source, target, send, recv, device):
    return pltpu.make_async_remote_copy(
        src_ref=source,
        dst_ref=target,
        send_sem=send,
        recv_sem=recv,
        device_id=device_at(*device),
        device_id_type=MESH,
    )


def dot(left, right):
    return jnp.dot(left, right, preferred_element_type=F32)


def dot_nt(left, right):
    return lax.dot_general(left, right, (((1,), (1,)), ((), ())), preferred_element_type=F32)


def dot_tn(left, right):
    return lax.dot_general(left, right, (((0,), (0,)), ((), ())), preferred_element_type=F32)


def normalize(values):
    centered = values - jnp.mean(values, axis=-1, keepdims=True)
    inverse = lax.rsqrt(jnp.mean(centered * centered, axis=-1, keepdims=True) + 1e-06)
    return centered * inverse, inverse


def norm_back(grad_norm, normed, inverse):
    return inverse * (
        grad_norm
        - jnp.mean(grad_norm, axis=-1, keepdims=True)
        - normed * jnp.mean(grad_norm * normed, axis=-1, keepdims=True)
    )


def column_sums(values):
    return jnp.sum(values, axis=0, keepdims=True)


def whole_kernel(
    piece_ref, cond_ref, tokens_hbm, grad_hbm,
    out_hbm, d_tokens_hbm, d_cond_ref, summed_ref,
    slots_a, slots_b, slots_c, sib_a, sib_b, sib_c,
    one_a, one_b, one_c, two_a, two_b, two_c, three_a, three_b, three_c, total,
    tokens_ref, grad_ref, out_ref,
    flat, w_ada, w_qkv, w_proj, w_up, w_down, bias,
    silu, mod, d_mod, h1, inverse1, qkv, probs, attn_t, mixed_t, branch, resid,
    mlp_t, hidden, slope, d_mlp, d_pre, d_branch, d_mixed, d_qkv,
    load, store, gather_send, gather_recv, meet_send, meet_recv,
    core_send, core_recv, send, recv,
):
    slots = (slots_a, slots_b, slots_c)
    sib = (sib_a, sib_b, sib_c)
    lands = ((one_a, one_b, one_c), (two_a, two_b, two_c), (three_a, three_b, three_c))
    place = coordinates()
    core = place[3]
    sign = 1 - 2 * core
    sibling = [place[0], place[1], place[2], 1 - core]
    load_tokens = pltpu.make_async_copy(tokens_hbm, tokens_ref, load.at[0])
    load_grad = pltpu.make_async_copy(grad_hbm, grad_ref, load.at[1])
    load_tokens.start()
    load_grad.start()

    rows, lanes = shift_parts()
    x = piece_ref[...]
    low = dot(x, one_hot((128, 128), lanes, BF16)).astype(BF16)
    high = dot(x, one_hot((128, 128), lanes - 128, BF16)).astype(BF16)
    square = (BLOCK, BLOCK)
    aligned = dot(one_hot(square, -rows, BF16), low) + dot(one_hot(square, -rows - 1, BF16), high)
    aligned = aligned.astype(BF16)
    for part, slot in enumerate(slots):
        first, second, third = ORDERS[part]
        slot[core, place[third], place[second], place[first]] = aligned[
            FIRST[part] : FIRST[part] + PARTS[part]
        ]
    greet(place)

    def block(part, stage, value):
        slot = slots[part]
        first, second, third = ORDERS[part]
        if stage == 0:
            return slot.at[core, place[third], place[second], value]
        if stage == 1:
            return slot.at[core, place[third], value]
        return slot.at[core, value]

    started = []

    def push(part, stage, kind, value, device):
        ref = block(part, stage, value)
        copy = remote(
            ref, ref, gather_send.at[part, stage, kind], gather_recv.at[part, stage, kind], device
        )
        copy.start()
        started.append(copy)

    def arrived(part, stage, kind, value):
        ref = block(part, stage, value)
        remote(
            ref,
            ref,
            gather_send.at[part, stage, kind],
            gather_recv.at[part, stage, kind],
            sibling,
        ).wait_recv()

    crossed = []

    def cross(part, kind, value):
        ref = block(part, 2, value)
        copy = remote(ref, ref, meet_send.at[part, kind], meet_recv.at[part, kind], sibling)
        copy.start()
        started.append(copy)
        mine = slots[part].at[1 - core, value]
        crossed.append(
            remote(mine, mine, meet_send.at[part, kind], meet_recv.at[part, kind], sibling)
        )

    for stage in range(3):
        spots = []
        for part in range(3):
            axis = ORDERS[part][stage]
            ahead, behind = along(place, axis, sign), along(place, axis, -sign)
            across = along(place, axis, 2)
            spots.append((axis, ahead, behind, across))
            push(part, stage, 0, place[axis], ahead)
            push(part, stage, 1, place[axis], behind)
            if stage < 2:
                push(part, stage, 2, place[axis], across)
        if stage == 2:
            for part in range(3):
                cross(part, 0, place[spots[part][0]])
        for part in range(3):
            axis, ahead, behind, across = spots[part]
            arrived(part, stage, 0, behind[axis])
            if stage == 2:
                push(part, stage, 2, behind[axis], ahead)
                cross(part, 1, behind[axis])
        for part in range(3):
            axis, ahead, behind, across = spots[part]
            arrived(part, stage, 1, ahead[axis])
            if stage == 2:
                cross(part, 2, ahead[axis])
        for part in range(3):
            axis, ahead, behind, across = spots[part]
            arrived(part, stage, 2, across[axis])
            if stage == 2:
                cross(part, 3, across[axis])
    for copy in crossed:
        copy.wait_recv()
    for copy in started:
        copy.wait_send()

    def first_row(index):
        return pl.multiple_of(lax.div(index * SHARD, 1024) * 8, 8)

    def unpack(index, _):
        start = first_row(index)
        before = lax.max(index - 1, 0)
        tail = slots[2][slot_at(2, before)][32:48].astype(F32)
        tail = jnp.where(start - first_row(before) == 160, tail[:8], tail[8:])
        tail = jnp.where(index == 0, jnp.zeros_like(tail), tail)
        for part in range(3):
            value = slots[part][slot_at(part, index)].astype(F32)
            if part == 0:
                flat[pl.ds(start, 8), :] = value[:8] + tail
                flat[pl.ds(start + 8, PARTS[0] - 8), :] = value[8:]
            else:
                flat[pl.ds(start + FIRST[part], PARTS[part]), :] = value
        return 0

    lax.fori_loop(0, DEVICES, unpack, 0, unroll=4)

    def take_matrix(target, base, height, width):
        for column in range(width):
            target[:, column * 128 : (column + 1) * 128] = flat[
                pl.ds(base + column, height, stride=width), :
            ].astype(BF16)

    def take_row(base, width, offset):
        for column in range(width):
            bias[0:1, offset + column * 128 : offset + (column + 1) * 128] = flat[
                base + column : base + column + 1, :
            ]

    def put_row(base, value):
        for column in range(value.shape[1] // 128):
            flat[base + column : base + column + 1, :] = value[
                :, column * 128 : (column + 1) * 128
            ]

    def put_block(base, width, column, value):
        for number in range(value.shape[1] // 128):
            flat[pl.ds(base + column + number, value.shape[0], stride=width), :] = value[
                :, number * 128 : (number + 1) * 128
            ]

    take_matrix(w_ada, ADA, D, 18)
    take_matrix(w_qkv, QKV, D, 9)
    take_matrix(w_proj, PROJ, D, 3)
    take_matrix(w_up, UP, D, 12)
    take_matrix(w_down, DOWN, FF, 3)
    take_row(BADA, 18, 0)
    take_row(BQV, 3, 2304)
    bias[0:1, 2688:3072] = jnp.zeros((1, D), F32)
    take_row(BQV + 3, 3, 3072)
    take_row(BPROJ, 3, 3456)
    take_row(BUP, 12, 3840)
    take_row(BDOWN, 3, 5376)

    cond = cond_ref[...].astype(F32)
    silu[...] = jnp.zeros_like(silu)
    silu[0:LATENTS, :] = cond / (1.0 + jnp.exp(-cond))
    silu_low = silu[...].astype(BF16)
    mod[...] = dot(silu_low, w_ada[...]) + bias[0:1, 0:2304]
    d_mod[...] = jnp.zeros_like(d_mod)

    lane = lax.broadcasted_iota(jnp.int32, (SEQ, 128), 1)
    half = (lane < 64, lane >= 64)

    def masked(value, head):
        return jnp.where(half[head], value, jnp.zeros_like(value))

    load_tokens.wait()

    def forward_attention(latent, _):
        tokens = pl.ds(latent * SEQ, SEQ) if isinstance(latent, int) else pl.ds(pl.multiple_of(latent * SEQ, SEQ), SEQ)
        x = tokens_ref[tokens, :].astype(F32)
        shift = mod[pl.ds(latent, 1), 0:D]
        scale = mod[pl.ds(latent, 1), D : 2 * D]
        gate = mod[pl.ds(latent, 1), 2 * D : 3 * D]
        normed, inverse = normalize(x)
        h1[tokens, :] = normed
        inverse1[tokens, :] = inverse
        attn_in = (normed * (1.0 + scale) + shift).astype(BF16)
        attn_t[:, tokens] = attn_in.T
        projected = (dot(attn_in, w_qkv[...]) + bias[0:1, 2304:3456]).astype(BF16)
        qkv[tokens, :] = projected

        def tail(pair, weights):
            v_t = projected[:, 2 * D + pair * 128 : 2 * D + (pair + 1) * 128].T
            zz = jnp.zeros((64, SEQ), BF16)
            spread = jnp.concatenate([jnp.concatenate([v_t[:64], zz], axis=0), jnp.concatenate([zz, v_t[64:]], axis=0)], axis=1)
            mixed_t[pair * 128 : (pair + 1) * 128, tokens] = dot(spread, jnp.concatenate(weights, axis=0)).astype(BF16)

        def soft(pair, scores):
            top = jnp.max(scores, axis=0, keepdims=True)
            powers = jnp.exp(scores - top)
            low = (powers * (1.0 / column_sums(powers))).astype(BF16)
            both = [low[:, :SEQ], low[:, SEQ:]]
            for head in range(2):
                probs[latent * HEADS + pair * 2 + head] = both[head]
            return both

        def score(pair):
            q = projected[:, pair * 128 : (pair + 1) * 128] * jnp.asarray(0.125, BF16)
            k = projected[:, D + pair * 128 : D + (pair + 1) * 128]
            return dot_nt(k, jnp.concatenate([masked(q, 0), masked(q, 1)], axis=0))

        scores = [score(pair) for pair in range(3)]
        weights = [soft(pair, scores[pair]) for pair in range(3)]
        for pair in range(3):
            tail(pair, weights[pair])
        reached = dot_tn(mixed_t[:, tokens], w_proj[...]) + bias[0:1, 3456:3840]
        branch[tokens, :] = reached
        resid[tokens, :] = x + gate * reached
        return 0

    for latent in range(LATENTS):
        forward_attention(latent, 0)

    chunk = 512
    load_grad.wait()

    def mlp(latent, sums):
        sum_down, sum_up, sum_proj = sums
        tokens = pl.ds(latent * SEQ, SEQ) if isinstance(latent, int) else pl.ds(pl.multiple_of(latent * SEQ, SEQ), SEQ)
        row = pl.ds(latent, 1)
        gate1 = mod[row, 2 * D : 3 * D]
        shift = mod[row, 3 * D : 4 * D]
        scale = mod[row, 4 * D : 5 * D]
        gate = mod[row, 5 * D : 6 * D]
        kept = resid[tokens, :]
        normed, inverse = normalize(kept)
        mlp_in = (normed * (1.0 + scale) + shift).astype(BF16)
        mlp_t[:, tokens] = mlp_in.T
        for start in range(0, FF, chunk):
            here = slice(start, start + chunk)
            u = dot(mlp_in, w_up[:, here]) + bias[0:1, 3840 + start : 3840 + start + chunk]
            square = u * u
            inner = u * (0.7978845608028654 + (0.7978845608028654 * 0.044715) * square)
            tangent = jnp.tanh(inner)
            above = 0.5 + 0.5 * tangent
            hidden[tokens, here] = (u * above).astype(BF16)
            rise = 0.7978845608028654 + (3 * 0.7978845608028654 * 0.044715) * square
            slope[:, here] = above + (0.5 * u) * (1.0 - tangent * tangent) * rise
        mlp_out = dot(hidden[tokens, :], w_down[...]) + bias[0:1, 5376:5760]
        out_ref[tokens, :] = (kept + gate * mlp_out).astype(BF16)
        pltpu.make_async_copy(
            out_ref.at[tokens, :], out_hbm.at[tokens, :], store.at[0, latent]
        ).start()
        grad = grad_ref[tokens, :].astype(F32)
        d_mod[row, 5 * D : 6 * D] = column_sums(grad * mlp_out)
        grad_mlp = (grad * gate).astype(BF16)
        d_mlp[tokens, :] = grad_mlp
        sum_down = sum_down + column_sums(grad_mlp.astype(F32))
        ups = []
        for start in range(0, FF, chunk):
            here = slice(start, start + chunk)
            value = (slope[:, here] * dot_nt(grad_mlp, w_down[here, :])).astype(BF16)
            d_pre[tokens, here] = value
            ups.append(column_sums(value.astype(F32)))
        sum_up = sum_up + jnp.concatenate(ups, axis=1)
        d_in = dot_nt(d_pre[tokens, :], w_up[...])
        d_mod[row, 4 * D : 5 * D] = column_sums(d_in * normed)
        d_mod[row, 3 * D : 4 * D] = column_sums(d_in)
        back = grad + norm_back(d_in * (1.0 + scale), normed, inverse)
        resid[tokens, :] = back
        d_mod[row, 2 * D : 3 * D] = column_sums(back * branch[tokens, :])
        low = (back * gate1).astype(BF16)
        d_branch[tokens, :] = low
        sum_proj = sum_proj + column_sums(low.astype(F32))
        d_mixed[tokens, :] = dot_nt(low, w_proj[...]).astype(BF16)
        return sum_down, sum_up, sum_proj

    zeros = jnp.zeros((1, D), F32)
    sums = (zeros, jnp.zeros((1, FF), F32), zeros)
    for latent in range(LATENTS):
        sums = mlp(latent, sums)
    sum_down, sum_up, sum_proj = sums
    put_row(BDOWN, sum_down)
    put_row(BUP, sum_up)
    put_row(BPROJ, sum_proj)
    for start in range(0, FF, 256):
        here = slice(start, start + 256)
        put_block(UP, 12, start // 128, dot(mlp_t[...], d_pre[:, here]))
        put_block(DOWN + start * 3, 3, 0, dot_tn(hidden[:, here], d_mlp[...]))
    put_block(PROJ, 3, 0, dot(mixed_t[...], d_branch[...]))

    def backward_attention(latent, sums):
        tokens = pl.ds(latent * SEQ, SEQ) if isinstance(latent, int) else pl.ds(pl.multiple_of(latent * SEQ, SEQ), SEQ)
        row = pl.ds(latent, 1)
        scale = mod[row, D : 2 * D]
        projected = qkv[tokens, :]
        d_out = d_mixed[tokens, :]

        def columns(number, pair):
            return projected[:, number * D + pair * 128 : number * D + (pair + 1) * 128]

        def split(value):
            return jnp.concatenate([masked(value, 0), masked(value, 1)], axis=0)

        def weights_of(pair):
            return jnp.concatenate([probs[latent * HEADS + pair * 2 + head] for head in range(2)], axis=1)

        spread = [split(d_out[:, pair * 128 : (pair + 1) * 128]) for pair in range(3)]
        first = [dot_nt(columns(2, pair), spread[pair]) for pair in range(3)]
        scores = []
        for pair in range(3):
            wide = weights_of(pair).astype(F32)
            product = first[pair] * wide
            scores.append((product - wide * column_sums(product)).astype(BF16))
        for pair in range(3):
            here = slice(pair * 128, (pair + 1) * 128)
            grad_v = dot(weights_of(pair), spread[pair])
            d_qkv[tokens, 2 * D + pair * 128 : 2 * D + (pair + 1) * 128] = grad_v.astype(BF16)
            q = columns(0, pair) * jnp.asarray(0.125, BF16)
            grad_k = dot(scores[pair], split(q))
            d_qkv[tokens, D + pair * 128 : D + (pair + 1) * 128] = grad_k.astype(BF16)
            k_t = columns(1, pair).T
            zz = jnp.zeros((64, SEQ), BF16)
            lhs = jnp.concatenate([jnp.concatenate([k_t[:64], zz], axis=0), jnp.concatenate([zz, k_t[64:]], axis=0)], axis=1)
            rhs = jnp.concatenate([scores[pair][:, :SEQ], scores[pair][:, SEQ:]], axis=0)
            d_qkv[tokens, here] = (dot(lhs, rhs) * 0.125).astype(BF16).T
        low = d_qkv[tokens, :]
        normed = h1[tokens, :]
        d_in = dot_nt(low, w_qkv[...])
        d_mod[row, D : 2 * D] = column_sums(d_in * normed)
        d_mod[row, 0:D] = column_sums(d_in)
        h1[tokens, :] = resid[tokens, :] + norm_back(
            d_in * (1.0 + scale), normed, inverse1[tokens, :]
        )
        pltpu.make_async_copy(
            h1.at[tokens, :], d_tokens_hbm.at[tokens, :], store.at[1, latent]
        ).start()
        return sums + column_sums(low.astype(F32))

    sum_qkv = jnp.zeros((1, 3 * D), F32)
    for latent in range(LATENTS):
        sum_qkv = backward_attention(latent, sum_qkv)
    put_row(BQV, sum_qkv[:, :D])
    put_row(BQV + 3, sum_qkv[:, 2 * D :])
    for start in range(0, 3 * D, D):
        put_block(QKV, 9, start // 128, dot(attn_t[...], d_qkv[:, start : start + D]))
    d_mod_low = d_mod[...].astype(BF16)
    put_row(BADA, column_sums(d_mod_low.astype(F32)))
    for start in range(0, 6 * D, D):
        put_block(ADA, 18, start // 128, dot_tn(silu_low, d_mod_low[:, start : start + D]))
    d_silu = dot_nt(d_mod_low, w_ada[...])[0:LATENTS]
    gate = 1.0 / (1.0 + jnp.exp(-cond))
    d_cond_ref[...] = d_silu * (gate * (1.0 + cond * (1.0 - gate)))

    def slot_row(part, c, b, a, which):
        spot = [0, 0, 0]
        first, second, third = ORDERS[part]
        spot[third], spot[second], spot[first] = c, b, a
        start = first_row(device_at(*spot, which)[0])
        return pl.ds(pl.multiple_of(start + FIRST[part], 8), PARTS[part])

    def pack(part, value):
        def body(step, _):
            b, a = lax.div(step, 4), lax.rem(step, 4)
            slots[part][1 - core, value, b, a] = flat[
                slot_row(part, value, b, a, 1 - core), :
            ].astype(BF16)
            return 0

        lax.fori_loop(0, 16, body, 0, unroll=4)

    def meet(part, value):
        def body(step, _):
            b, a = lax.div(step, 4), lax.rem(step, 4)
            mine = flat[slot_row(part, value, b, a, core), :]
            slots[part][core, value, b, a] = (mine + sib[part][value, b, a].astype(F32)).astype(
                BF16
            )
            return 0

        lax.fori_loop(0, 16, body, 0, unroll=4)

    started = []
    spots = []
    for part in range(3):
        axis = ORDERS[part][2]
        spots.append(
            (axis, along(place, axis, 2), along(place, axis, -sign), along(place, axis, sign))
        )
    for kind in range(4):
        for part in range(3):
            axis = spots[part][0]
            value = place[axis] if kind == 3 else spots[part][(1, 3, 2)[kind]][axis]
            pack(part, value)
            copy = remote(
                slots[part].at[1 - core, value],
                sib[part].at[value],
                core_send.at[part, kind],
                core_recv.at[part, kind],
                sibling,
            )
            copy.start()
            started.append(copy)

    def send_sum(part, stage, kind, source, device):
        copy = remote(
            source,
            lands[stage][part].at[kind],
            send.at[part, stage, kind],
            recv.at[part, stage, kind],
            device,
        )
        copy.start()
        started.append(copy)

    def sum_arrived(part, stage, kind):
        ref = lands[stage][part].at[kind]
        remote(
            ref, ref, send.at[part, stage, kind], recv.at[part, stage, kind], sibling
        ).wait_recv()

    def add(target, *others):
        shape = target.shape

        def body(step, _):
            if len(shape) == 4:
                here = (lax.div(step, shape[1]), lax.rem(step, shape[1]))
            else:
                here = (step,)
            value = target[here].astype(F32)
            for other in others:
                value = value + other[here].astype(F32)
            target[here] = value.astype(BF16)
            return 0

        count = shape[0] * shape[1] if len(shape) == 4 else shape[0]
        lax.fori_loop(0, count, body, 0, unroll=4)

    for kind in range(4):
        for part in range(3):
            axis = spots[part][0]
            value = place[axis] if kind == 3 else spots[part][1 + kind][axis]
            ref = sib[part].at[value]
            mine = slots[part].at[core, value]
            remote(
                ref, ref, core_send.at[part, kind], core_recv.at[part, kind], sibling
            ).wait_recv()
            meet(part, value)
            if kind == 0:
                send_sum(part, 0, 0, mine, spots[part][3])
            if kind == 1:
                send_sum(part, 0, 1, mine, spots[part][2])
            if kind == 2:
                sum_arrived(part, 0, 0)
                add(mine, lands[0][part].at[0])
                send_sum(part, 0, 2, mine, spots[part][3])
    held = []
    for part in range(3):
        ref = slots[part].at[core, place[spots[part][0]]]
        sum_arrived(part, 0, 1)
        sum_arrived(part, 0, 2)
        add(ref, lands[0][part].at[1], lands[0][part].at[2])
        held.append(ref)
        axis = ORDERS[part][1]
        for kind in range(3):
            far = along(place, axis, kind + 1)
            send_sum(part, 1, kind, ref.at[far[axis]], far)
    for part in range(3):
        axis = ORDERS[part][1]
        ref = held[part].at[place[axis]]
        for kind in range(3):
            sum_arrived(part, 1, kind)
        add(ref, *[lands[1][part].at[kind] for kind in range(3)])
        held[part] = ref
        axis = ORDERS[part][0]
        for kind in range(3):
            far = along(place, axis, kind + 1)
            send_sum(part, 2, kind, ref.at[far[axis]], far)
    for part in range(3):
        axis = ORDERS[part][0]
        value = held[part][place[axis]].astype(F32)
        for kind in range(3):
            sum_arrived(part, 2, kind)
            value = value + lands[2][part][kind].astype(F32)
        total[FIRST[part] : FIRST[part] + PARTS[part], :] = value
    for copy in started:
        copy.wait_send()
    for latent in range(LATENTS):
        tokens = pl.ds(latent * SEQ, SEQ)
        pltpu.make_async_copy(
            out_ref.at[tokens, :], out_hbm.at[tokens, :], store.at[0, latent]
        ).wait()
        pltpu.make_async_copy(
            h1.at[tokens, :], d_tokens_hbm.at[tokens, :], store.at[1, latent]
        ).wait()
    summed = total[...]

    def product(left, right):
        return jnp.dot(left, right, preferred_element_type=F32, precision=lax.Precision.HIGHEST)

    low = product(summed, one_hot((128, 128), -lanes, F32))
    high = product(summed, one_hot((128, 128), 128 - lanes, F32))
    summed_ref[...] = product(one_hot(square, rows, F32), low) + product(
        one_hot(square, rows + 1, F32), high
    )


def transformer_block(piece, cond, tokens, d_out):
    vmem = pl.BlockSpec(memory_space=pltpu.VMEM)
    hbm = pl.BlockSpec(memory_space=pl.ANY)
    scratch = [((2, 4, 4, 4, rows, 128), BF16) for rows in PARTS]
    scratch += [((4, 4, 4, rows, 128), BF16) for rows in PARTS]
    scratch += [((3, 4, 4, rows, 128), BF16) for rows in PARTS]
    scratch += [((3, 4, rows, 128), BF16) for rows in PARTS]
    scratch += [((3, rows, 128), BF16) for rows in PARTS]
    scratch += [
        ((BLOCK, 128), F32),
        ((ROWS, D), BF16),
        ((ROWS, D), BF16),
        ((ROWS, D), BF16),
        ((FLAT_ROWS, 128), F32),
        ((D, 6 * D), BF16),
        ((D, 3 * D), BF16),
        ((D, D), BF16),
        ((D, FF), BF16),
        ((FF, D), BF16),
        ((8, 5760), F32),
        ((16, D), F32),
        ((16, 6 * D), F32),
        ((16, 6 * D), F32),
        ((ROWS, D), F32),
        ((ROWS, 1), F32),
        ((ROWS, 3 * D), BF16),
        ((LATENTS * HEADS, SEQ, SEQ), BF16),
        ((D, ROWS), BF16),
        ((D, ROWS), BF16),
        ((ROWS, D), F32),
        ((ROWS, D), F32),
        ((D, ROWS), BF16),
        ((ROWS, FF), BF16),
        ((SEQ, FF), F32),
        ((ROWS, D), BF16),
        ((ROWS, FF), BF16),
        ((ROWS, D), BF16),
        ((ROWS, D), BF16),
        ((ROWS, 3 * D), BF16),
    ]
    sems = [(2,), (2, 4), (3, 3, 3), (3, 3, 3), (3, 4), (3, 4), (3, 4), (3, 4), (3, 3, 3), (3, 3, 3)]
    return pl.pallas_call(
        whole_kernel,
        out_shape=[
            jax.ShapeDtypeStruct((ROWS, D), BF16),
            jax.ShapeDtypeStruct((ROWS, D), F32),
            jax.ShapeDtypeStruct((LATENTS, D), F32),
            jax.ShapeDtypeStruct((BLOCK, 128), F32),
        ],
        in_specs=[vmem, vmem, hbm, hbm],
        out_specs=[hbm, hbm, vmem, vmem],
        scratch_shapes=[pltpu.VMEM(shape, dtype) for shape, dtype in scratch]
        + [pltpu.SemaphoreType.DMA(shape) for shape in sems],
        compiler_params=pltpu.CompilerParams(
            collective_id=0, has_side_effects=True, vmem_limit_bytes=63 * 1024 * 1024
        ),
        name="block",
    )(piece, cond, tokens, d_out)


def local(tokens, cond, params, d_out):
    piece = jnp.pad(params, (0, BLOCK * 128 - SHARD)).reshape(BLOCK, 128)
    out, d_tokens, d_cond, summed = transformer_block(piece, cond, tokens, d_out)
    return out, d_tokens, d_cond, summed.reshape(-1)[:SHARD]


def solution(mesh):
    placed = (P("dev", None), P("dev", None), P("dev"), P("dev", None))
    return jax.shard_map(
        local,
        mesh=mesh,
        in_specs=placed,
        out_specs=(P("dev", None), P("dev", None), P("dev", None), P("dev")),
        check_vma=False,
    )
```

```python
import functools

import jax
import jax.numpy as jnp
from jax import lax
from jax.experimental import pallas as pl
from jax.experimental.pallas import tpu as pltpu
from jax.sharding import PartitionSpec as P

D = 384
FF = 1536
HEADS = 6
SEQ = 256
LATENTS = 4
ROWS = LATENTS * SEQ
SHARD = 20778
DEVICES = 128
BLOCK = 176
PARTS = (32, 64, 80)
FIRST = (0, 32, 96)
FLAT_ROWS = 20784

ADA, BADA = 0, 6912
QKV, BQV = 6930, 10386
PROJ, BPROJ = 10392, 11544
UP, BUP = 11547, 16155
DOWN, BDOWN = 16167, 20775

HALF = DEVICES // 2

MESH = pl.DeviceIdType.MESH
BF16 = jnp.bfloat16
F32 = jnp.float32

ORDERS = ((2, 1, 0), (1, 0, 2), (2, 0, 1))


def coordinates():
    me = lax.axis_index("dev")
    return (
        lax.rem(lax.div(me, 32), 4),
        lax.rem(lax.div(me, 8), 4),
        lax.rem(lax.div(me, 2), 4),
        lax.rem(me, 2),
    )


def device_at(y, x, z, core):
    return (((y * 4 + x) * 4 + z) * 2 + core,)


def along(place, axis, step):
    moved = list(place)
    moved[axis] = lax.rem(place[axis] + step + 4, 4)
    return moved


def when(condition, action):
    if condition is None:
        action()
    else:
        pl.when(condition)(action)


def shift_parts():
    offset = lax.rem(lax.axis_index("dev") * SHARD, 1024)
    return lax.div(offset, 128), lax.rem(offset, 128)


def one_hot(shape, difference, dtype):
    rows = lax.broadcasted_iota(jnp.int32, shape, 0)
    columns = lax.broadcasted_iota(jnp.int32, shape, 1)
    return jnp.where(columns - rows == difference, 1.0, 0.0).astype(dtype)


def greet(place):
    barrier = pltpu.get_barrier_semaphore()
    partners = [along(place, axis, step) for axis in range(3) for step in (1, 2, 3)]
    partners.append([place[0], place[1], place[2], 1 - place[3]])
    for partner in partners:
        pl.semaphore_signal(barrier, inc=1, device_id=device_at(*partner), device_id_type=MESH)
    pl.semaphore_wait(barrier, len(partners))


def remote(source, target, send, recv, device):
    return pltpu.make_async_remote_copy(
        src_ref=source,
        dst_ref=target,
        send_sem=send,
        recv_sem=recv,
        device_id=device_at(*device),
        device_id_type=MESH,
    )


def dot(left, right):
    return jnp.dot(left, right, preferred_element_type=F32)


def dot_nt(left, right):
    return lax.dot_general(left, right, (((1,), (1,)), ((), ())), preferred_element_type=F32)


def dot_tn(left, right):
    return lax.dot_general(left, right, (((0,), (0,)), ((), ())), preferred_element_type=F32)


def normalize(values):
    centered = values - jnp.mean(values, axis=-1, keepdims=True)
    inverse = lax.rsqrt(jnp.mean(centered * centered, axis=-1, keepdims=True) + 1e-06)
    return centered * inverse, inverse


def norm_back(grad_norm, normed, inverse):
    return inverse * (
        grad_norm
        - jnp.mean(grad_norm, axis=-1, keepdims=True)
        - normed * jnp.mean(grad_norm * normed, axis=-1, keepdims=True)
    )


def column_sums(values):
    return jnp.sum(values, axis=0, keepdims=True)


def whole_kernel(
    piece_ref, cond_ref, tokens_hbm, grad_hbm,
    out_hbm, d_tokens_hbm, d_cond_ref, summed_ref,
    *scratch,
):
    scratch = list(scratch)

    def take(count):
        taken = scratch[:count]
        del scratch[:count]
        return taken

    slots = take(3)
    sib = take(3)
    lands = [take(3) for _ in range(3)]
    (
        total, tokens_ref, grad_ref, out_ref,
        flat, w_ada, w_qkv, w_proj, w_up, w_down, bias,
        silu, mod, d_mod, h1, inverse1, qkv, probs, attn_t, mixed_f, mixed_t, resid,
        mlp_t, hidden, slope, d_mlp, d_pre, d_branch, d_mixed, d_qkv,
        load, store, gather_send, gather_recv, last_send, last_recv, meet_send, meet_recv,
        core_send, core_recv, far_send, far_recv, send, recv,
    ) = scratch
    place = coordinates()
    core = place[3]
    sibling = [place[0], place[1], place[2], 1 - core]
    load_tokens = pltpu.make_async_copy(tokens_hbm, tokens_ref, load.at[0])
    load_grad = pltpu.make_async_copy(grad_hbm, grad_ref, load.at[1])
    load_tokens.start()
    load_grad.start()

    def base(part, stage):
        ref = slots[part].at[core]
        for axis in (ORDERS[part][2], ORDERS[part][1])[: 2 - stage]:
            ref = ref.at[place[axis]]
        return ref

    def block(part, stage, value):
        return base(part, stage).at[value]

    def half_block(half, part, which, value):
        ref = slots[part].at[which, value]
        return ref if part == 0 else ref.at[2 * half : 2 * half + 2]

    rows, lanes = shift_parts()
    x = piece_ref[...]
    low = dot(x, one_hot((128, 128), lanes, BF16)).astype(BF16)
    high = dot(x, one_hot((128, 128), lanes - 128, BF16)).astype(BF16)
    square = (BLOCK, BLOCK)
    aligned = dot(one_hot(square, -rows, BF16), low) + dot(one_hot(square, -rows - 1, BF16), high)
    aligned = aligned.astype(BF16)

    for part in range(3):
        block(part, 0, place[ORDERS[part][0]])[...] = aligned[
            FIRST[part] : FIRST[part] + PARTS[part]
        ]
    greet(place)

    gathers = ([], [])

    def launch(kept, condition, make):
        when(condition, lambda: make().start())
        kept.append((condition, make))

    def wait_sent(kept):
        for condition, make in kept:
            when(condition, lambda make=make: make().wait_send())

    def near(part, stage, kind, from_me):
        axis = ORDERS[part][stage]
        value = place[axis] if from_me else along(place, axis, -kind)[axis]
        ref = block(part, stage, value)
        sems = (gather_send.at[part, stage, kind - 1], gather_recv.at[part, stage, kind - 1])
        return remote(ref, ref, *sems, along(place, axis, kind))

    def gather_stage(stage):
        for part in range(3):
            for kind in (2, 1, 3):
                launch(gathers[0], None, functools.partial(near, part, stage, kind, True))
        for kind in (1, 3, 2):
            for part in range(3):
                near(part, stage, kind, False).wait_recv()

    def last(half, part, kind, from_me):
        axis = ORDERS[part][2]
        value = place[axis] if from_me else along(place, axis, -kind)[axis]
        ref = half_block(half, part, core, value)
        sems = (last_send.at[half, part, kind - 1], last_recv.at[half, part, kind - 1])
        return remote(ref, ref, *sems, along(place, axis, kind))

    def cross(half, part, kind, which):
        axis = ORDERS[part][2]
        ref = half_block(half, part, which, along(place, axis, -kind)[axis])
        return remote(
            ref, ref, meet_send.at[half, part, kind], meet_recv.at[half, part, kind], sibling
        )

    def parts_of(half):
        return (0, 1, 2) if half == 0 else (1, 2)

    def gather_start(half):
        for kind in (2, 1, 3):
            for part in parts_of(half):
                launch(gathers[half], None, functools.partial(last, half, part, kind, True))
        for part in parts_of(half):
            launch(gathers[half], None, functools.partial(cross, half, part, 0, core))

    def gather_wait(half):
        for kind in (1, 3, 2):
            for part in parts_of(half):
                last(half, part, kind, False).wait_recv()
                launch(gathers[half], None, functools.partial(cross, half, part, kind, core))

    def gather_end(half):
        for kind in range(4):
            for part in parts_of(half):
                cross(half, part, kind, 1 - core).wait_recv()
        wait_sent(gathers[half])

    def first_row(index):
        return pl.multiple_of(lax.div(index * SHARD, 1024) * 8, 8)

    def slot_at(part, index):
        where = (
            lax.rem(lax.div(index, 32), 4),
            lax.rem(lax.div(index, 8), 4),
            lax.rem(lax.div(index, 2), 4),
        )
        first, second, third = ORDERS[part]
        return lax.rem(index, 2), where[third], where[second], where[first]

    def piece_tail(index):
        here = slots[2][slot_at(2, index)][64:80].astype(F32)
        return jnp.where(first_row(index + 1) - first_row(index) == 160, here[:8], here[8:])

    def unpack_one(index, tail):
        where = first_row(index)
        for part in range(3):
            value = slots[part][slot_at(part, index)].astype(F32)
            if part == 0:
                flat[pl.ds(where, 8), :] = value[:8] + tail
                flat[pl.ds(where + 8, PARTS[0] - 8), :] = value[8:]
            else:
                flat[pl.ds(where + FIRST[part], PARTS[part]), :] = value

    def unpack(half):
        tail = jnp.zeros((8, 128), F32) if half == 0 else piece_tail(HALF - 1)
        unpack_one(half * HALF, tail)

        def body(index, _):
            unpack_one(index, piece_tail(index - 1))
            return 0

        lax.fori_loop(half * HALF + 1, (half + 1) * HALF, body, 0, unroll=3)

    gather_stage(0)
    gather_stage(1)
    gather_start(0)
    gather_wait(0)
    gather_end(0)
    gather_start(1)
    unpack(0)

    def take_matrix(target, base, height, width):
        for column in range(width):
            target[:, column * 128 : (column + 1) * 128] = flat[
                pl.ds(base + column, height, stride=width), :
            ].astype(BF16)

    def take_row(base, width, offset):
        for column in range(width):
            bias[0:1, offset + column * 128 : offset + (column + 1) * 128] = flat[
                base + column : base + column + 1, :
            ]

    def put_row(base, value):
        for column in range(value.shape[1] // 128):
            flat[base + column : base + column + 1, :] = value[
                :, column * 128 : (column + 1) * 128
            ]

    def put_block(base, width, column, value):
        for number in range(value.shape[1] // 128):
            flat[pl.ds(base + column + number, value.shape[0], stride=width), :] = value[
                :, number * 128 : (number + 1) * 128
            ]

    take_matrix(w_ada, ADA, D, 18)
    take_matrix(w_qkv, QKV, D, 9)
    take_row(BADA, 18, 0)
    take_row(BQV, 3, 2304)
    bias[0:1, 2688:3456] = jnp.zeros((1, 2 * D), F32)

    cond = cond_ref[...].astype(F32)
    silu[...] = jnp.zeros_like(silu)
    silu[0:LATENTS, :] = cond / (1.0 + jnp.exp(-cond))
    silu_low = silu[...].astype(BF16)
    mod[...] = dot(silu_low, w_ada[...]) + bias[0:1, 0:2304]
    d_mod[...] = jnp.zeros_like(d_mod)

    lane = lax.broadcasted_iota(jnp.int32, (SEQ, 128), 1)
    half = (lane < 64, lane >= 64)

    def masked(value, head):
        return jnp.where(half[head], value, jnp.zeros_like(value))

    load_tokens.wait()

    def side_by_side(value):
        blank = jnp.zeros((64, SEQ), BF16)
        first = jnp.concatenate([value[:64], blank], axis=0)
        return jnp.concatenate([first, jnp.concatenate([blank, value[64:]], axis=0)], axis=1)

    def forward_attention(latent, _):
        tokens = pl.ds(latent * SEQ, SEQ)
        x = tokens_ref[tokens, :].astype(F32)
        shift = mod[pl.ds(latent, 1), 0:D]
        scale = mod[pl.ds(latent, 1), D : 2 * D]
        normed, inverse = normalize(x)
        h1[tokens, :] = normed
        inverse1[tokens, :] = inverse
        attn_in = (normed * (1.0 + scale) + shift).astype(BF16)
        attn_t[:, tokens] = attn_in.T
        projected = (dot(attn_in, w_qkv[...]) + bias[0:1, 2304:3456]).astype(BF16)
        qkv[tokens, :] = projected
        def tail(pair, weights):
            v_t = projected[:, 2 * D + pair * 128 : 2 * D + (pair + 1) * 128].T
            spread = side_by_side(v_t)
            mixed_f[pair * 128 : (pair + 1) * 128, tokens] = dot(spread, jnp.concatenate(weights, axis=0))

        def soft(pair, scores):
            top = jnp.max(scores, axis=0, keepdims=True)
            powers = jnp.exp(scores - top)
            low = (powers * (1.0 / column_sums(powers))).astype(BF16)
            both = [low[:, :SEQ], low[:, SEQ:]]
            for head in range(2):
                probs[latent * HEADS + pair * 2 + head] = both[head]
            return both

        def score(pair):
            q = projected[:, pair * 128 : (pair + 1) * 128] * jnp.asarray(0.125, BF16)
            k = projected[:, D + pair * 128 : D + (pair + 1) * 128]
            return dot_nt(k, jnp.concatenate([masked(q, 0), masked(q, 1)], axis=0))

        scores = [score(pair) for pair in range(3)]
        weights = [soft(pair, scores[pair]) for pair in range(3)]
        for pair in range(3):
            tail(pair, weights[pair])
        return 0

    for latent in range(0, 2):
        forward_attention(latent, 0)
    gather_wait(1)
    for latent in range(2, LATENTS):
        forward_attention(latent, 0)
    gather_end(1)
    unpack(1)
    take_matrix(w_proj, PROJ, D, 3)
    take_matrix(w_up, UP, D, 12)
    take_matrix(w_down, DOWN, FF, 3)
    take_row(BQV + 3, 3, 3072)
    take_row(BPROJ, 3, 3456)
    take_row(BUP, 12, 3840)
    take_row(BDOWN, 3, 5376)
    bias_v = jnp.broadcast_to(bias[0:1, 3072:3456], (8, D)).T[:, 0:1]

    chunk = 512
    load_grad.wait()

    def mlp(latent, sums):
        sum_down, sum_up, sum_proj, sum_v = sums
        tokens = pl.ds(latent * SEQ, SEQ)
        row = pl.ds(latent, 1)
        gate1 = mod[row, 2 * D : 3 * D]
        shift = mod[row, 3 * D : 4 * D]
        scale = mod[row, 4 * D : 5 * D]
        gate = mod[row, 5 * D : 6 * D]
        mixed = (mixed_f[:, tokens] + bias_v).astype(BF16)
        mixed_t[:, tokens] = mixed
        reached = dot_tn(mixed, w_proj[...]) + bias[0:1, 3456:3840]
        kept = tokens_ref[tokens, :].astype(F32) + gate1 * reached
        normed, inverse = normalize(kept)
        mlp_in = (normed * (1.0 + scale) + shift).astype(BF16)
        mlp_t[:, tokens] = mlp_in.T
        for start in range(0, FF, chunk):
            here = slice(start, start + chunk)
            u = dot(mlp_in, w_up[:, here]) + bias[0:1, 3840 + start : 3840 + start + chunk]
            square = u * u
            inner = u * (0.7978845608028654 + (0.7978845608028654 * 0.044715) * square)
            tangent = jnp.tanh(inner)
            above = 0.5 + 0.5 * tangent
            hidden[tokens, here] = (u * above).astype(BF16)
            rise = 0.7978845608028654 + (3 * 0.7978845608028654 * 0.044715) * square
            slope[:, here] = above + (0.5 * u) * (1.0 - tangent * tangent) * rise
        mlp_out = dot(hidden[tokens, :], w_down[...]) + bias[0:1, 5376:5760]
        out_ref[tokens, :] = (kept + gate * mlp_out).astype(BF16)
        pltpu.make_async_copy(
            out_ref.at[tokens, :], out_hbm.at[tokens, :], store.at[0, latent]
        ).start()
        grad = grad_ref[tokens, :].astype(F32)
        d_mod[row, 5 * D : 6 * D] = column_sums(grad * mlp_out)
        grad_mlp = (grad * gate).astype(BF16)
        d_mlp[tokens, :] = grad_mlp
        sum_down = sum_down + column_sums(grad_mlp.astype(F32))
        ups = []
        for start in range(0, FF, chunk):
            here = slice(start, start + chunk)
            value = (slope[:, here] * dot_nt(grad_mlp, w_down[here, :])).astype(BF16)
            d_pre[tokens, here] = value
            ups.append(column_sums(value.astype(F32)))
        sum_up = sum_up + jnp.concatenate(ups, axis=1)
        d_in = dot_nt(d_pre[tokens, :], w_up[...])
        d_mod[row, 4 * D : 5 * D] = column_sums(d_in * normed)
        d_mod[row, 3 * D : 4 * D] = column_sums(d_in)
        back = grad + norm_back(d_in * (1.0 + scale), normed, inverse)
        resid[tokens, :] = back
        d_mod[row, 2 * D : 3 * D] = column_sums(back * reached)
        low = (back * gate1).astype(BF16)
        d_branch[tokens, :] = low
        sum_proj = sum_proj + column_sums(low.astype(F32))
        mixed_grad = dot_nt(low, w_proj[...]).astype(BF16)
        d_mixed[tokens, :] = mixed_grad
        sum_v = sum_v + column_sums(mixed_grad.astype(F32))
        return sum_down, sum_up, sum_proj, sum_v

    zeros = jnp.zeros((1, D), F32)
    sums = (zeros, jnp.zeros((1, FF), F32), zeros, zeros)
    for latent in range(LATENTS):
        sums = mlp(latent, sums)
    sum_down, sum_up, sum_proj, sum_v = sums
    put_row(BQV + 3, sum_v)
    put_row(BDOWN, sum_down)
    put_row(BUP, sum_up)
    put_row(BPROJ, sum_proj)
    for start in range(0, FF, 256):
        here = slice(start, start + 256)
        put_block(UP, 12, start // 128, dot(mlp_t[...], d_pre[:, here]))
        put_block(DOWN + start * 3, 3, 0, dot_tn(hidden[:, here], d_mlp[...]))
    put_block(PROJ, 3, 0, dot(mixed_t[...], d_branch[...]))

    def slot_rows(part, c, b, a, which):
        where = [0, 0, 0]
        first, second, third = ORDERS[part]
        where[third], where[second], where[first] = c, b, a
        return pl.ds(
            pl.multiple_of(first_row(device_at(*where, which)[0]) + FIRST[part], 8), PARTS[part]
        )

    def each_slot(half, part, action):
        begin, count = (0, 16) if part == 0 else (8 * half, 8)

        def body(step, _):
            action(lax.div(step, 4), lax.rem(step, 4))
            return 0

        lax.fori_loop(begin, begin + count, body, 0, unroll=4)

    reduces = []

    def meet_value(part, kind):
        return along(place, ORDERS[part][2], kind)[ORDERS[part][2]]

    def meet_turns(half):
        return [(part, kind) for kind in (2, 1, 3, 0) for part in parts_of(half)]

    def meet_push(half, part, kind):
        value = meet_value(part, kind)
        target = sib[part].at[value]
        return remote(
            half_block(half, part, 1 - core, value),
            target if part == 0 else target.at[2 * half : 2 * half + 2],
            core_send.at[half, part, kind],
            core_recv.at[half, part, kind],
            sibling,
        )

    def meet_start(half):
        for part, kind in meet_turns(half):
            value = meet_value(part, kind)

            def pack(b, a, part=part, value=value):
                slots[part][1 - core, value, b, a] = flat[
                    slot_rows(part, value, b, a, 1 - core), :
                ].astype(BF16)

            each_slot(half, part, pack)
            launch(reduces, None, functools.partial(meet_push, half, part, kind))

    def far_push(half, part, kind):
        far = along(place, ORDERS[part][2], kind)
        land = lands[2][part].at[kind - 1]
        return remote(
            half_block(half, part, core, far[ORDERS[part][2]]),
            land if part == 0 else land.at[2 * half : 2 * half + 2],
            far_send.at[half, part, kind - 1],
            far_recv.at[half, part, kind - 1],
            far,
        )

    def meet_end(half):
        for part, kind in meet_turns(half):
            value = meet_value(part, kind)
            meet_push(half, part, kind).wait_recv()

            def meet(b, a, part=part, value=value):
                mine = flat[slot_rows(part, value, b, a, core), :]
                other = sib[part][value, b, a].astype(F32)
                slots[part][core, value, b, a] = (mine + other).astype(BF16)

            each_slot(half, part, meet)
            if kind != 0:
                launch(reduces, None, functools.partial(far_push, half, part, kind))

    def add(target, others, begin, count):
        def body(step, _):
            here = (lax.div(step, 4), lax.rem(step, 4)) if len(target.shape) == 4 else (step,)
            value = target[here].astype(F32)
            for other in others:
                value = value + other[here].astype(F32)
            target[here] = value.astype(BF16)
            return 0

        lax.fori_loop(begin, begin + count, body, 0, unroll=4)

    def far_wait(half, part):
        for kind in (1, 3, 2):
            far_push(half, part, kind).wait_recv()
        others = [lands[2][part].at[kind] for kind in range(3)]
        begin, count = (0, 16) if part == 0 else (8 * half, 8)
        add(block(part, 2, place[ORDERS[part][2]]), others, begin, count)

    def sum_push(part, stage, kind):
        axis = ORDERS[part][stage]
        far = along(place, axis, kind)
        return remote(
            block(part, stage, far[axis]),
            lands[stage][part].at[kind - 1],
            send.at[part, stage, kind - 1],
            recv.at[part, stage, kind - 1],
            far,
        )

    def reduce_start(part, stage):
        for kind in (2, 1, 3):
            launch(reduces, None, functools.partial(sum_push, part, stage, kind))

    def reduce_wait(part, stage):
        for kind in (1, 3, 2):
            sum_push(part, stage, kind).wait_recv()
        target = block(part, stage, place[ORDERS[part][stage]])
        others = [lands[stage][part].at[kind] for kind in range(3)]
        if stage == 1:
            add(target, others, 0, 4)
            return
        value = target[...].astype(F32)
        for other in others:
            value = value + other[...].astype(F32)
        total[FIRST[part] : FIRST[part] + PARTS[part], :] = value

    meet_start(1)

    def backward_attention(latent, sums):
        tokens = pl.ds(latent * SEQ, SEQ)
        row = pl.ds(latent, 1)
        scale = mod[row, D : 2 * D]
        projected = qkv[tokens, :]
        d_out = d_mixed[tokens, :]
        def columns(number, pair):
            return projected[:, number * D + pair * 128 : number * D + (pair + 1) * 128]

        def split(value):
            return jnp.concatenate([masked(value, 0), masked(value, 1)], axis=0)

        def weights_of(pair):
            return jnp.concatenate([probs[latent * HEADS + pair * 2 + head] for head in range(2)], axis=1)

        spread = [split(d_out[:, pair * 128 : (pair + 1) * 128]) for pair in range(3)]
        first = [dot_nt(columns(2, pair), spread[pair]) for pair in range(3)]
        scores = []
        for pair in range(3):
            wide = weights_of(pair).astype(F32)
            product = first[pair] * wide
            scores.append((product - wide * column_sums(product)).astype(BF16))
        for pair in range(3):
            here = slice(pair * 128, (pair + 1) * 128)
            grad_v = dot(weights_of(pair), spread[pair])
            d_qkv[tokens, 2 * D + pair * 128 : 2 * D + (pair + 1) * 128] = grad_v.astype(BF16)
            q = columns(0, pair) * jnp.asarray(0.125, BF16)
            grad_k = dot(scores[pair], split(q))
            d_qkv[tokens, D + pair * 128 : D + (pair + 1) * 128] = grad_k.astype(BF16)
            k_t = columns(1, pair).T
            low = jnp.concatenate([scores[pair][:, :SEQ], scores[pair][:, SEQ:]], axis=0)
            d_qkv[tokens, here] = (dot(side_by_side(k_t), low) * 0.125).astype(BF16).T
        low = d_qkv[tokens, :]
        normed = h1[tokens, :]
        d_in = dot_nt(low, w_qkv[...])
        d_mod[row, D : 2 * D] = column_sums(d_in * normed)
        d_mod[row, 0:D] = column_sums(d_in)
        h1[tokens, :] = resid[tokens, :] + norm_back(
            d_in * (1.0 + scale), normed, inverse1[tokens, :]
        )
        pltpu.make_async_copy(
            h1.at[tokens, :], d_tokens_hbm.at[tokens, :], store.at[1, latent]
        ).start()
        return sums + column_sums(low[:, :D].astype(F32))

    sum_q = zeros
    for latent in range(0, 2):
        sum_q = backward_attention(latent, sum_q)
    meet_end(1)
    for latent in range(2, LATENTS):
        sum_q = backward_attention(latent, sum_q)
    put_row(BQV, sum_q)
    far_wait(1, 1)
    far_wait(1, 2)
    for start in range(0, 3 * D, D):
        put_block(QKV, 9, start // 128, dot(attn_t[...], d_qkv[:, start : start + D]))
    d_mod_low = d_mod[...].astype(BF16)
    put_row(BADA, column_sums(d_mod_low.astype(F32)))
    for start in range(0, 6 * D, D):
        put_block(ADA, 18, start // 128, dot_tn(silu_low, d_mod_low[:, start : start + D]))
    d_silu = dot_nt(d_mod_low, w_ada[...])[0:LATENTS]
    gate = 1.0 / (1.0 + jnp.exp(-cond))
    d_cond_ref[...] = d_silu * (gate * (1.0 + cond * (1.0 - gate)))

    meet_start(0)
    meet_end(0)
    for part in range(3):
        far_wait(0, part)
        reduce_start(part, 1)
    for part in range(3):
        reduce_wait(part, 1)
        reduce_start(part, 0)
    for part in range(3):
        reduce_wait(part, 0)
    wait_sent(reduces)
    for latent in range(LATENTS):
        tokens = pl.ds(latent * SEQ, SEQ)
        pltpu.make_async_copy(
            out_ref.at[tokens, :], out_hbm.at[tokens, :], store.at[0, latent]
        ).wait()
        pltpu.make_async_copy(
            h1.at[tokens, :], d_tokens_hbm.at[tokens, :], store.at[1, latent]
        ).wait()
    summed = total[...]

    def product(left, right):
        return jnp.dot(left, right, preferred_element_type=F32, precision=lax.Precision.HIGHEST)

    low = product(summed, one_hot((128, 128), -lanes, F32))
    high = product(summed, one_hot((128, 128), 128 - lanes, F32))
    summed_ref[...] = product(one_hot(square, rows, F32), low) + product(
        one_hot(square, rows + 1, F32), high
    )


def transformer_block(piece, cond, tokens, d_out):
    vmem = pl.BlockSpec(memory_space=pltpu.VMEM)
    hbm = pl.BlockSpec(memory_space=pl.ANY)
    scratch = [((2, 4, 4, 4, rows, 128), BF16) for rows in PARTS]
    scratch += [((4, 4, 4, rows, 128), BF16) for rows in PARTS]
    for lead in ((3,), (3, 4), (3, 4, 4)):
        scratch += [(lead + (rows, 128), BF16) for rows in PARTS]
    scratch += [
        ((BLOCK, 128), F32),
        ((ROWS, D), BF16),
        ((ROWS, D), BF16),
        ((ROWS, D), BF16),
        ((FLAT_ROWS, 128), F32),
        ((D, 6 * D), BF16),
        ((D, 3 * D), BF16),
        ((D, D), BF16),
        ((D, FF), BF16),
        ((FF, D), BF16),
        ((8, 5760), F32),
        ((16, D), F32),
        ((16, 6 * D), F32),
        ((16, 6 * D), F32),
        ((ROWS, D), F32),
        ((ROWS, 1), F32),
        ((ROWS, 3 * D), BF16),
        ((LATENTS * HEADS, SEQ, SEQ), BF16),
        ((D, ROWS), BF16),
        ((D, ROWS), F32),
        ((D, ROWS), BF16),
        ((ROWS, D), F32),
        ((D, ROWS), BF16),
        ((ROWS, FF), BF16),
        ((SEQ, FF), F32),
        ((ROWS, D), BF16),
        ((ROWS, FF), BF16),
        ((ROWS, D), BF16),
        ((ROWS, D), BF16),
        ((ROWS, 3 * D), BF16),
    ]
    sems = [(2,), (2, 4)]
    sems += [(3, 2, 3)] * 2 + [(2, 3, 3)] * 2 + [(2, 3, 4)] * 4 + [(2, 3, 3)] * 2 + [(3, 2, 3)] * 2
    return pl.pallas_call(
        whole_kernel,
        out_shape=[
            jax.ShapeDtypeStruct((ROWS, D), BF16),
            jax.ShapeDtypeStruct((ROWS, D), F32),
            jax.ShapeDtypeStruct((LATENTS, D), F32),
            jax.ShapeDtypeStruct((BLOCK, 128), F32),
        ],
        in_specs=[vmem, vmem, hbm, hbm],
        out_specs=[hbm, hbm, vmem, vmem],
        scratch_shapes=[pltpu.VMEM(shape, dtype) for shape, dtype in scratch]
        + [pltpu.SemaphoreType.DMA(shape) for shape in sems],
        compiler_params=pltpu.CompilerParams(
            collective_id=0, has_side_effects=True, vmem_limit_bytes=63 * 1024 * 1024
        ),
        name="block",
    )(piece, cond, tokens, d_out)


def local(tokens, cond, params, d_out):
    piece = jnp.pad(params, (0, BLOCK * 128 - SHARD)).reshape(BLOCK, 128)
    out, d_tokens, d_cond, summed = transformer_block(piece, cond, tokens, d_out)
    return out, d_tokens, d_cond, summed.reshape(-1)[:SHARD]


def solution(mesh):
    placed = (P("dev", None), P("dev", None), P("dev"), P("dev", None))
    return jax.shard_map(
        local,
        mesh=mesh,
        in_specs=placed,
        out_specs=(P("dev", None), P("dev", None), P("dev", None), P("dev")),
        check_vma=False,
    )
```

```python
import functools

import jax
import jax.numpy as jnp
from jax import lax
from jax.experimental import pallas as pl
from jax.experimental.pallas import tpu as pltpu
from jax.sharding import PartitionSpec as P

D = 384
FF = 1536
HEADS = 6
SEQ = 256
LATENTS = 4
ROWS = LATENTS * SEQ
SHARD = 20778
DEVICES = 128
BLOCK = 176
PARTS = (64, 64, 48)
FIRST = (0, 64, 128)
FLAT_ROWS = 20784

ADA, BADA = 0, 6912
QKV, BQV = 6930, 10386
PROJ, BPROJ = 10392, 11544
UP, BUP = 11547, 16155
DOWN, BDOWN = 16167, 20775

MESH = pl.DeviceIdType.MESH
BF16 = jnp.bfloat16
F32 = jnp.float32

ORDERS = ((2, 1, 0), (1, 0, 2), (0, 2, 1))


def coordinates():
    me = lax.axis_index("dev")
    return (
        lax.rem(lax.div(me, 32), 4),
        lax.rem(lax.div(me, 8), 4),
        lax.rem(lax.div(me, 2), 4),
        lax.rem(me, 2),
    )


def device_at(y, x, z, core):
    return (((y * 4 + x) * 4 + z) * 2 + core,)


def along(place, axis, step):
    moved = list(place)
    moved[axis] = lax.rem(place[axis] + step + 4, 4)
    return moved


def slot_at(part, index):
    place = (
        lax.rem(lax.div(index, 32), 4),
        lax.rem(lax.div(index, 8), 4),
        lax.rem(lax.div(index, 2), 4),
    )
    first, second, third = ORDERS[part]
    return lax.rem(index, 2), place[third], place[second], place[first]


def shift_parts():
    offset = lax.rem(lax.axis_index("dev") * SHARD, 1024)
    return lax.div(offset, 128), lax.rem(offset, 128)


def one_hot(shape, difference, dtype):
    rows = lax.broadcasted_iota(jnp.int32, shape, 0)
    columns = lax.broadcasted_iota(jnp.int32, shape, 1)
    return jnp.where(columns - rows == difference, 1.0, 0.0).astype(dtype)


def greet(place):
    barrier = pltpu.get_barrier_semaphore()
    partners = [along(place, axis, step) for axis in range(3) for step in (1, 2, 3)]
    partners.append([place[0], place[1], place[2], 1 - place[3]])
    for partner in partners:
        pl.semaphore_signal(barrier, inc=1, device_id=device_at(*partner), device_id_type=MESH)
    pl.semaphore_wait(barrier, len(partners))


def remote(source, target, send, recv, device):
    return pltpu.make_async_remote_copy(
        src_ref=source,
        dst_ref=target,
        send_sem=send,
        recv_sem=recv,
        device_id=device_at(*device),
        device_id_type=MESH,
    )


def dot(left, right):
    return jnp.dot(left, right, preferred_element_type=F32)


def dot_nt(left, right):
    return lax.dot_general(left, right, (((1,), (1,)), ((), ())), preferred_element_type=F32)


def dot_tn(left, right):
    return lax.dot_general(left, right, (((0,), (0,)), ((), ())), preferred_element_type=F32)


def normalize(values):
    centered = values - jnp.mean(values, axis=-1, keepdims=True)
    inverse = lax.rsqrt(jnp.mean(centered * centered, axis=-1, keepdims=True) + 1e-06)
    return centered * inverse, inverse


def norm_back(grad_norm, normed, inverse):
    return inverse * (
        grad_norm
        - jnp.mean(grad_norm, axis=-1, keepdims=True)
        - normed * jnp.mean(grad_norm * normed, axis=-1, keepdims=True)
    )


def column_sums(values):
    return jnp.sum(values, axis=0, keepdims=True)


def whole_kernel(
    piece_ref, cond_ref, tokens_hbm, grad_hbm,
    out_hbm, d_tokens_hbm, d_cond_ref, summed_ref,
    slots_a, slots_b, slots_c, sib_a, sib_b, sib_c,
    one_a, one_b, one_c, two_a, two_b, two_c, three_a, three_b, three_c, total,
    tokens_ref, grad_ref, out_ref,
    flat, w_ada, w_qkv, w_proj, w_up, w_down, bias,
    silu, mod, d_mod, h1, inverse1, qkv, probs, attn_t, mixed_t, branch, resid,
    mlp_t, hidden, slope, d_mlp, d_pre, d_branch, d_mixed,
    load, store, gather_send, gather_recv, meet_send, meet_recv,
    core_send, core_recv, send, recv,
):
    slots = (slots_a, slots_b, slots_c)
    sib = (sib_a, sib_b, sib_c)
    lands = ((one_a, one_b, one_c), (two_a, two_b, two_c), (three_a, three_b, three_c))
    place = coordinates()
    core = place[3]
    sign = 1 - 2 * core
    sibling = [place[0], place[1], place[2], 1 - core]
    load_tokens = pltpu.make_async_copy(tokens_hbm, tokens_ref, load.at[0])
    load_grad = pltpu.make_async_copy(grad_hbm, grad_ref, load.at[1])
    load_tokens.start()
    load_grad.start()

    rows, lanes = shift_parts()
    x = piece_ref[...]
    low = dot(x, one_hot((128, 128), lanes, BF16)).astype(BF16)
    high = dot(x, one_hot((128, 128), lanes - 128, BF16)).astype(BF16)
    square = (BLOCK, BLOCK)
    aligned = dot(one_hot(square, -rows, BF16), low) + dot(one_hot(square, -rows - 1, BF16), high)
    aligned = aligned.astype(BF16)
    for part, slot in enumerate(slots):
        first, second, third = ORDERS[part]
        slot[core, place[third], place[second], place[first]] = aligned[
            FIRST[part] : FIRST[part] + PARTS[part]
        ]
    greet(place)

    def block(part, stage, value):
        slot = slots[part]
        first, second, third = ORDERS[part]
        if stage == 0:
            return slot.at[core, place[third], place[second], value]
        if stage == 1:
            return slot.at[core, place[third], value]
        return slot.at[core, value]

    started = []

    def push(part, stage, kind, value, device):
        ref = block(part, stage, value)
        copy = remote(
            ref, ref, gather_send.at[part, stage, kind], gather_recv.at[part, stage, kind], device
        )
        copy.start()
        started.append(copy)

    def arrived(part, stage, kind, value):
        ref = block(part, stage, value)
        remote(
            ref,
            ref,
            gather_send.at[part, stage, kind],
            gather_recv.at[part, stage, kind],
            sibling,
        ).wait_recv()

    crossed = []

    def cross(part, kind, value):
        ref = block(part, 2, value)
        copy = remote(ref, ref, meet_send.at[part, kind], meet_recv.at[part, kind], sibling)
        copy.start()
        started.append(copy)
        mine = slots[part].at[1 - core, value]
        crossed.append(
            remote(mine, mine, meet_send.at[part, kind], meet_recv.at[part, kind], sibling)
        )

    for stage in range(3):
        spots = []
        for part in range(3):
            axis = ORDERS[part][stage]
            ahead, behind = along(place, axis, sign), along(place, axis, -sign)
            across = along(place, axis, 2)
            spots.append((axis, ahead, behind, across))
            push(part, stage, 0, place[axis], ahead)
            push(part, stage, 1, place[axis], behind)
            if stage < 2:
                push(part, stage, 2, place[axis], across)
        if stage == 2:
            for part in range(3):
                cross(part, 0, place[spots[part][0]])
        for part in range(3):
            axis, ahead, behind, across = spots[part]
            arrived(part, stage, 0, behind[axis])
            if stage == 2:
                push(part, stage, 2, behind[axis], ahead)
                cross(part, 1, behind[axis])
        for part in range(3):
            axis, ahead, behind, across = spots[part]
            arrived(part, stage, 1, ahead[axis])
            if stage == 2:
                cross(part, 2, ahead[axis])
        for part in range(3):
            axis, ahead, behind, across = spots[part]
            arrived(part, stage, 2, across[axis])
            if stage == 2:
                cross(part, 3, across[axis])
    for copy in crossed:
        copy.wait_recv()
    for copy in started:
        copy.wait_send()

    def first_row(index):
        return pl.multiple_of(lax.div(index * SHARD, 1024) * 8, 8)

    def unpack(index, _):
        start = first_row(index)
        before = lax.max(index - 1, 0)
        tail = slots[2][slot_at(2, before)][32:48].astype(F32)
        tail = jnp.where(start - first_row(before) == 160, tail[:8], tail[8:])
        tail = jnp.where(index == 0, jnp.zeros_like(tail), tail)
        for part in range(3):
            value = slots[part][slot_at(part, index)].astype(F32)
            if part == 0:
                flat[pl.ds(start, 8), :] = value[:8] + tail
                flat[pl.ds(start + 8, PARTS[0] - 8), :] = value[8:]
            else:
                flat[pl.ds(start + FIRST[part], PARTS[part]), :] = value
        return 0

    lax.fori_loop(0, DEVICES, unpack, 0, unroll=4)

    def take_matrix(target, base, height, width):
        for column in range(width):
            target[:, column * 128 : (column + 1) * 128] = flat[
                pl.ds(base + column, height, stride=width), :
            ].astype(BF16)

    def take_row(base, width, offset):
        for column in range(width):
            bias[0:1, offset + column * 128 : offset + (column + 1) * 128] = flat[
                base + column : base + column + 1, :
            ]

    def put_row(base, value):
        for column in range(value.shape[1] // 128):
            flat[base + column : base + column + 1, :] = value[
                :, column * 128 : (column + 1) * 128
            ]

    def put_block(base, width, column, value):
        for number in range(value.shape[1] // 128):
            flat[pl.ds(base + column + number, value.shape[0], stride=width), :] = value[
                :, number * 128 : (number + 1) * 128
            ]

    take_matrix(w_ada, ADA, D, 18)
    take_matrix(w_qkv, QKV, D, 9)
    take_matrix(w_proj, PROJ, D, 3)
    take_matrix(w_up, UP, D, 12)
    take_matrix(w_down, DOWN, FF, 3)
    take_row(BADA, 18, 0)
    take_row(BQV, 3, 2304)
    bias[0:1, 2688:3072] = jnp.zeros((1, D), F32)
    take_row(BQV + 3, 3, 3072)
    take_row(BPROJ, 3, 3456)
    take_row(BUP, 12, 3840)
    take_row(BDOWN, 3, 5376)

    cond = cond_ref[...].astype(F32)
    silu[...] = jnp.zeros_like(silu)
    silu[0:LATENTS, :] = cond / (1.0 + jnp.exp(-cond))
    silu_low = silu[...].astype(BF16)
    mod[...] = dot(silu_low, w_ada[...]) + bias[0:1, 0:2304]
    d_mod[...] = jnp.zeros_like(d_mod)

    lane = lax.broadcasted_iota(jnp.int32, (SEQ, 128), 1)
    half = (lane < 64, lane >= 64)

    def masked(value, head):
        return jnp.where(half[head], value, jnp.zeros_like(value))

    load_tokens.wait()

    def forward_attention(latent, _):
        tokens = pl.ds(latent * SEQ, SEQ) if isinstance(latent, int) else pl.ds(pl.multiple_of(latent * SEQ, SEQ), SEQ)
        x = tokens_ref[tokens, :].astype(F32)
        shift = mod[pl.ds(latent, 1), 0:D]
        scale = mod[pl.ds(latent, 1), D : 2 * D]
        gate = mod[pl.ds(latent, 1), 2 * D : 3 * D]
        normed, inverse = normalize(x)
        h1[tokens, :] = normed
        inverse1[tokens, :] = inverse
        attn_in = (normed * (1.0 + scale) + shift).astype(BF16)
        attn_t[:, tokens] = attn_in.T
        projected = (dot(attn_in, w_qkv[...]) + bias[0:1, 2304:3456]).astype(BF16)
        qkv[tokens, :] = projected

        def tail(pair, weights):
            v_t = projected[:, 2 * D + pair * 128 : 2 * D + (pair + 1) * 128].T
            zz = jnp.zeros((64, SEQ), BF16)
            spread = jnp.concatenate([jnp.concatenate([v_t[:64], zz], axis=0), jnp.concatenate([zz, v_t[64:]], axis=0)], axis=1)
            mixed_t[pair * 128 : (pair + 1) * 128, tokens] = dot(spread, jnp.concatenate(weights, axis=0)).astype(BF16)

        def soft(pair, scores):
            top = jnp.max(scores, axis=0, keepdims=True)
            powers = jnp.exp(scores - top)
            low = (powers * (1.0 / column_sums(powers))).astype(BF16)
            both = [low[:, :SEQ], low[:, SEQ:]]
            for head in range(2):
                probs[latent * HEADS + pair * 2 + head] = both[head]
            return both

        def score(pair):
            q = projected[:, pair * 128 : (pair + 1) * 128] * jnp.asarray(0.125, BF16)
            k = projected[:, D + pair * 128 : D + (pair + 1) * 128]
            return dot_nt(k, jnp.concatenate([masked(q, 0), masked(q, 1)], axis=0))

        scores = [score(pair) for pair in range(3)]
        weights = [soft(pair, scores[pair]) for pair in range(3)]
        for pair in range(3):
            tail(pair, weights[pair])
        reached = dot_tn(mixed_t[:, tokens], w_proj[...]) + bias[0:1, 3456:3840]
        branch[tokens, :] = reached
        resid[tokens, :] = x + gate * reached
        return 0

    for latent in range(LATENTS):
        forward_attention(latent, 0)

    chunk = 512
    load_grad.wait()

    def mlp(latent, sums):
        sum_down, sum_up, sum_proj = sums
        tokens = pl.ds(latent * SEQ, SEQ) if isinstance(latent, int) else pl.ds(pl.multiple_of(latent * SEQ, SEQ), SEQ)
        row = pl.ds(latent, 1)
        gate1 = mod[row, 2 * D : 3 * D]
        shift = mod[row, 3 * D : 4 * D]
        scale = mod[row, 4 * D : 5 * D]
        gate = mod[row, 5 * D : 6 * D]
        kept = resid[tokens, :]
        normed, inverse = normalize(kept)
        mlp_in = (normed * (1.0 + scale) + shift).astype(BF16)
        mlp_t[:, tokens] = mlp_in.T
        for start in range(0, FF, chunk):
            here = slice(start, start + chunk)
            u = dot(mlp_in, w_up[:, here]) + bias[0:1, 3840 + start : 3840 + start + chunk]
            square = u * u
            inner = u * (0.7978845608028654 + (0.7978845608028654 * 0.044715) * square)
            tangent = jnp.tanh(inner)
            above = 0.5 + 0.5 * tangent
            hidden[tokens, here] = (u * above).astype(BF16)
            rise = 0.7978845608028654 + (3 * 0.7978845608028654 * 0.044715) * square
            slope[:, here] = above + (0.5 * u) * (1.0 - tangent * tangent) * rise
        mlp_out = dot(hidden[tokens, :], w_down[...]) + bias[0:1, 5376:5760]
        out_ref[tokens, :] = (kept + gate * mlp_out).astype(BF16)
        pltpu.make_async_copy(
            out_ref.at[tokens, :], out_hbm.at[tokens, :], store.at[0, latent]
        ).start()
        grad = grad_ref[tokens, :].astype(F32)
        d_mod[row, 5 * D : 6 * D] = column_sums(grad * mlp_out)
        grad_mlp = (grad * gate).astype(BF16)
        d_mlp[tokens, :] = grad_mlp
        sum_down = sum_down + column_sums(grad_mlp.astype(F32))
        ups = []
        for start in range(0, FF, chunk):
            here = slice(start, start + chunk)
            value = (slope[:, here] * dot_nt(grad_mlp, w_down[here, :])).astype(BF16)
            d_pre[tokens, here] = value
            ups.append(column_sums(value.astype(F32)))
        sum_up = sum_up + jnp.concatenate(ups, axis=1)
        d_in = dot_nt(d_pre[tokens, :], w_up[...])
        d_mod[row, 4 * D : 5 * D] = column_sums(d_in * normed)
        d_mod[row, 3 * D : 4 * D] = column_sums(d_in)
        back = grad + norm_back(d_in * (1.0 + scale), normed, inverse)
        resid[tokens, :] = back
        d_mod[row, 2 * D : 3 * D] = column_sums(back * branch[tokens, :])
        low = (back * gate1).astype(BF16)
        d_branch[tokens, :] = low
        sum_proj = sum_proj + column_sums(low.astype(F32))
        d_mixed[tokens, :] = dot_nt(low, w_proj[...]).astype(BF16)
        return sum_down, sum_up, sum_proj

    zeros = jnp.zeros((1, D), F32)
    sums = (zeros, jnp.zeros((1, FF), F32), zeros)
    for latent in range(LATENTS):
        sums = mlp(latent, sums)
    sum_down, sum_up, sum_proj = sums
    put_row(BDOWN, sum_down)
    put_row(BUP, sum_up)
    put_row(BPROJ, sum_proj)
    for start in range(0, FF, 256):
        here = slice(start, start + 256)
        put_block(UP, 12, start // 128, dot(mlp_t[...], d_pre[:, here]))
        put_block(DOWN + start * 3, 3, 0, dot_tn(hidden[:, here], d_mlp[...]))
    put_block(PROJ, 3, 0, dot(mixed_t[...], d_branch[...]))

    def backward_attention(latent, sums):
        tokens = pl.ds(latent * SEQ, SEQ) if isinstance(latent, int) else pl.ds(pl.multiple_of(latent * SEQ, SEQ), SEQ)
        row = pl.ds(latent, 1)
        scale = mod[row, D : 2 * D]
        projected = qkv[tokens, :]
        d_out = d_mixed[tokens, :]

        def columns(number, pair):
            return projected[:, number * D + pair * 128 : number * D + (pair + 1) * 128]

        def split(value):
            return jnp.concatenate([masked(value, 0), masked(value, 1)], axis=0)

        def weights_of(pair):
            return jnp.concatenate([probs[latent * HEADS + pair * 2 + head] for head in range(2)], axis=1)

        spread = [split(d_out[:, pair * 128 : (pair + 1) * 128]) for pair in range(3)]
        first = [dot_nt(columns(2, pair), spread[pair]) for pair in range(3)]
        scores = []
        for pair in range(3):
            wide = weights_of(pair).astype(F32)
            product = first[pair] * wide
            scores.append((product - wide * column_sums(product)).astype(BF16))
        for pair in range(3):
            here = slice(pair * 128, (pair + 1) * 128)
            grad_v = dot(weights_of(pair), spread[pair])
            qkv[tokens, 2 * D + pair * 128 : 2 * D + (pair + 1) * 128] = grad_v.astype(BF16)
            q = columns(0, pair) * jnp.asarray(0.125, BF16)
            grad_k = dot(scores[pair], split(q))
            qkv[tokens, D + pair * 128 : D + (pair + 1) * 128] = grad_k.astype(BF16)
            k_t = columns(1, pair).T
            zz = jnp.zeros((64, SEQ), BF16)
            lhs = jnp.concatenate([jnp.concatenate([k_t[:64], zz], axis=0), jnp.concatenate([zz, k_t[64:]], axis=0)], axis=1)
            rhs = jnp.concatenate([scores[pair][:, :SEQ], scores[pair][:, SEQ:]], axis=0)
            qkv[tokens, here] = (dot(lhs, rhs) * 0.125).astype(BF16).T
        low = qkv[tokens, :]
        normed = h1[tokens, :]
        d_in = dot_nt(low, w_qkv[...])
        d_mod[row, D : 2 * D] = column_sums(d_in * normed)
        d_mod[row, 0:D] = column_sums(d_in)
        h1[tokens, :] = resid[tokens, :] + norm_back(
            d_in * (1.0 + scale), normed, inverse1[tokens, :]
        )
        pltpu.make_async_copy(
            h1.at[tokens, :], d_tokens_hbm.at[tokens, :], store.at[1, latent]
        ).start()
        return sums + column_sums(low.astype(F32))

    sum_qkv = jnp.zeros((1, 3 * D), F32)
    for latent in range(LATENTS):
        sum_qkv = backward_attention(latent, sum_qkv)
    put_row(BQV, sum_qkv[:, :D])
    put_row(BQV + 3, sum_qkv[:, 2 * D :])
    for start in range(0, 3 * D, D):
        put_block(QKV, 9, start // 128, dot(attn_t[...], qkv[:, start : start + D]))
    d_mod_low = d_mod[...].astype(BF16)
    put_row(BADA, column_sums(d_mod_low.astype(F32)))
    for start in range(0, 6 * D, D):
        put_block(ADA, 18, start // 128, dot_tn(silu_low, d_mod_low[:, start : start + D]))
    d_silu = dot_nt(d_mod_low, w_ada[...])[0:LATENTS]
    gate = 1.0 / (1.0 + jnp.exp(-cond))
    d_cond_ref[...] = d_silu * (gate * (1.0 + cond * (1.0 - gate)))

    def slot_row(part, c, b, a, which):
        spot = [0, 0, 0]
        first, second, third = ORDERS[part]
        spot[third], spot[second], spot[first] = c, b, a
        start = first_row(device_at(*spot, which)[0])
        return pl.ds(pl.multiple_of(start + FIRST[part], 8), PARTS[part])

    def pack(part, value):
        def body(step, _):
            b, a = lax.div(step, 4), lax.rem(step, 4)
            slots[part][1 - core, value, b, a] = flat[
                slot_row(part, value, b, a, 1 - core), :
            ].astype(BF16)
            return 0

        lax.fori_loop(0, 16, body, 0, unroll=4)

    def meet(part, value):
        def body(step, _):
            b, a = lax.div(step, 4), lax.rem(step, 4)
            mine = flat[slot_row(part, value, b, a, core), :]
            slots[part][core, value, b, a] = (mine + sib[part][value, b, a].astype(F32)).astype(
                BF16
            )
            return 0

        lax.fori_loop(0, 16, body, 0, unroll=4)

    started = []
    spots = []
    for part in range(3):
        axis = ORDERS[part][2]
        spots.append(
            (axis, along(place, axis, 2), along(place, axis, -sign), along(place, axis, sign))
        )
    for kind in range(4):
        for part in range(3):
            axis = spots[part][0]
            value = place[axis] if kind == 3 else spots[part][(1, 3, 2)[kind]][axis]
            pack(part, value)
            copy = remote(
                slots[part].at[1 - core, value],
                sib[part].at[value],
                core_send.at[part, kind],
                core_recv.at[part, kind],
                sibling,
            )
            copy.start()
            started.append(copy)

    def send_sum(part, stage, kind, source, device):
        copy = remote(
            source,
            lands[stage][part].at[kind],
            send.at[part, stage, kind],
            recv.at[part, stage, kind],
            device,
        )
        copy.start()
        started.append(copy)

    def sum_arrived(part, stage, kind):
        ref = lands[stage][part].at[kind]
        remote(
            ref, ref, send.at[part, stage, kind], recv.at[part, stage, kind], sibling
        ).wait_recv()

    def add(target, *others):
        shape = target.shape

        def body(step, _):
            if len(shape) == 4:
                here = (lax.div(step, shape[1]), lax.rem(step, shape[1]))
            else:
                here = (step,)
            value = target[here].astype(F32)
            for other in others:
                value = value + other[here].astype(F32)
            target[here] = value.astype(BF16)
            return 0

        count = shape[0] * shape[1] if len(shape) == 4 else shape[0]
        lax.fori_loop(0, count, body, 0, unroll=4)

    for kind in range(4):
        for part in range(3):
            axis = spots[part][0]
            value = place[axis] if kind == 3 else spots[part][1 + kind][axis]
            ref = sib[part].at[value]
            mine = slots[part].at[core, value]
            remote(
                ref, ref, core_send.at[part, kind], core_recv.at[part, kind], sibling
            ).wait_recv()
            meet(part, value)
            if kind == 0:
                send_sum(part, 0, 0, mine, spots[part][3])
            if kind == 1:
                send_sum(part, 0, 1, mine, spots[part][2])
            if kind == 2:
                sum_arrived(part, 0, 0)
                add(mine, lands[0][part].at[0])
                send_sum(part, 0, 2, mine, spots[part][3])
    held = []
    for part in range(3):
        ref = slots[part].at[core, place[spots[part][0]]]
        sum_arrived(part, 0, 1)
        sum_arrived(part, 0, 2)
        add(ref, lands[0][part].at[1], lands[0][part].at[2])
        held.append(ref)
        axis = ORDERS[part][1]
        for kind in range(3):
            far = along(place, axis, kind + 1)
            send_sum(part, 1, kind, ref.at[far[axis]], far)
    for part in range(3):
        axis = ORDERS[part][1]
        ref = held[part].at[place[axis]]
        for kind in range(3):
            sum_arrived(part, 1, kind)
        add(ref, *[lands[1][part].at[kind] for kind in range(3)])
        held[part] = ref
        axis = ORDERS[part][0]
        for kind in range(3):
            far = along(place, axis, kind + 1)
            send_sum(part, 2, kind, ref.at[far[axis]], far)
    for part in range(3):
        axis = ORDERS[part][0]
        value = held[part][place[axis]].astype(F32)
        for kind in range(3):
            sum_arrived(part, 2, kind)
            value = value + lands[2][part][kind].astype(F32)
        total[FIRST[part] : FIRST[part] + PARTS[part], :] = value
    for copy in started:
        copy.wait_send()
    for latent in range(LATENTS):
        tokens = pl.ds(latent * SEQ, SEQ)
        pltpu.make_async_copy(
            out_ref.at[tokens, :], out_hbm.at[tokens, :], store.at[0, latent]
        ).wait()
        pltpu.make_async_copy(
            h1.at[tokens, :], d_tokens_hbm.at[tokens, :], store.at[1, latent]
        ).wait()
    summed = total[...]

    def product(left, right):
        return jnp.dot(left, right, preferred_element_type=F32, precision=lax.Precision.HIGHEST)

    low = product(summed, one_hot((128, 128), -lanes, F32))
    high = product(summed, one_hot((128, 128), 128 - lanes, F32))
    summed_ref[...] = product(one_hot(square, rows, F32), low) + product(
        one_hot(square, rows + 1, F32), high
    )


def transformer_block(piece, cond, tokens, d_out):
    vmem = pl.BlockSpec(memory_space=pltpu.VMEM)
    hbm = pl.BlockSpec(memory_space=pl.ANY)
    scratch = [((2, 4, 4, 4, rows, 128), BF16) for rows in PARTS]
    scratch += [((4, 4, 4, rows, 128), BF16) for rows in PARTS]
    scratch += [((3, 4, 4, rows, 128), BF16) for rows in PARTS]
    scratch += [((3, 4, rows, 128), BF16) for rows in PARTS]
    scratch += [((3, rows, 128), BF16) for rows in PARTS]
    scratch += [
        ((BLOCK, 128), F32),
        ((ROWS, D), BF16),
        ((ROWS, D), BF16),
        ((ROWS, D), BF16),
        ((FLAT_ROWS, 128), F32),
        ((D, 6 * D), BF16),
        ((D, 3 * D), BF16),
        ((D, D), BF16),
        ((D, FF), BF16),
        ((FF, D), BF16),
        ((8, 5760), F32),
        ((16, D), F32),
        ((16, 6 * D), F32),
        ((16, 6 * D), F32),
        ((ROWS, D), F32),
        ((ROWS, 1), F32),
        ((ROWS, 3 * D), BF16),
        ((LATENTS * HEADS, SEQ, SEQ), BF16),
        ((D, ROWS), BF16),
        ((D, ROWS), BF16),
        ((ROWS, D), F32),
        ((ROWS, D), F32),
        ((D, ROWS), BF16),
        ((ROWS, FF), BF16),
        ((SEQ, FF), F32),
        ((ROWS, D), BF16),
        ((ROWS, FF), BF16),
        ((ROWS, D), BF16),
        ((ROWS, D), BF16),
    ]
    sems = [(2,), (2, 4), (3, 3, 3), (3, 3, 3), (3, 4), (3, 4), (3, 4), (3, 4), (3, 3, 3), (3, 3, 3)]
    return pl.pallas_call(
        whole_kernel,
        out_shape=[
            jax.ShapeDtypeStruct((ROWS, D), BF16),
            jax.ShapeDtypeStruct((ROWS, D), F32),
            jax.ShapeDtypeStruct((LATENTS, D), F32),
            jax.ShapeDtypeStruct((BLOCK, 128), F32),
        ],
        in_specs=[vmem, vmem, hbm, hbm],
        out_specs=[hbm, hbm, vmem, vmem],
        scratch_shapes=[pltpu.VMEM(shape, dtype) for shape, dtype in scratch]
        + [pltpu.SemaphoreType.DMA(shape) for shape in sems],
        compiler_params=pltpu.CompilerParams(
            collective_id=0, has_side_effects=True, vmem_limit_bytes=58 * 1024 * 1024
        ),
        name="block",
    )(piece, cond, tokens, d_out)


def hand_over_kernel(*refs):
    sources, targets, middles, (into, out_of) = refs[:3], refs[3:6], refs[6:9], refs[9:]
    firsts, seconds = [], []
    for number, (source, middle, target) in enumerate(zip(sources, middles, targets)):
        pieces = 4 if source.shape[0] == ROWS else 1
        rows = source.shape[0] // pieces
        for piece in range(pieces):
            here = pl.ds(piece * rows, rows)
            firsts.append(
                pltpu.make_async_copy(source.at[here], middle.at[here], into.at[number, piece])
            )
            seconds.append(
                pltpu.make_async_copy(middle.at[here], target.at[here], out_of.at[number, piece])
            )
    for copy in firsts:
        copy.start()
    for first, second in zip(firsts, seconds):
        first.wait()
        second.start()
    for copy in seconds:
        copy.wait()


def hand_over(*results):
    hbm = pl.BlockSpec(memory_space=pl.ANY)
    return pl.pallas_call(
        hand_over_kernel,
        out_shape=[jax.ShapeDtypeStruct(result.shape, result.dtype) for result in results],
        in_specs=[hbm] * 3,
        out_specs=[hbm] * 3,
        scratch_shapes=[pltpu.VMEM(result.shape, result.dtype) for result in results]
        + [pltpu.SemaphoreType.DMA((3, 4))] * 2,
        compiler_params=pltpu.CompilerParams(vmem_limit_bytes=63 * 1024 * 1024),
        name="hand_over",
    )(*results)


def local(tokens, cond, params, d_out):
    piece = jnp.pad(params, (0, BLOCK * 128 - SHARD)).reshape(BLOCK, 128)
    out, d_tokens, d_cond, summed = transformer_block(piece, cond, tokens, d_out)
    out, d_tokens, d_cond = hand_over(out, d_tokens, d_cond)
    return out, d_tokens, d_cond, summed.reshape(-1)[:SHARD]


def solution(mesh):
    placed = (P("dev", None), P("dev", None), P("dev"), P("dev", None))
    return jax.shard_map(
        local,
        mesh=mesh,
        in_specs=placed,
        out_specs=(P("dev", None), P("dev", None), P("dev", None), P("dev")),
        check_vma=False,
    )
```

```python
import functools

import jax
import jax.numpy as jnp
from jax import lax
from jax.experimental import pallas as pl
from jax.experimental.pallas import tpu as pltpu
from jax.sharding import PartitionSpec as P

D = 384
FF = 1536
HEADS = 6
SEQ = 256
LATENTS = 4
ROWS = LATENTS * SEQ
SHARD = 20778
DEVICES = 128
BLOCK = 176
PARTS = (64, 64, 48)
FIRST = (0, 64, 128)
FLAT_ROWS = 20784

ADA, BADA = 0, 6912
QKV, BQV = 6930, 10386
PROJ, BPROJ = 10392, 11544
UP, BUP = 11547, 16155
DOWN, BDOWN = 16167, 20775

MESH = pl.DeviceIdType.MESH
BF16 = jnp.bfloat16
F32 = jnp.float32

ORDERS = ((2, 1, 0), (1, 0, 2), (0, 2, 1))


def coordinates():
    me = lax.axis_index("dev")
    return (
        lax.rem(lax.div(me, 32), 4),
        lax.rem(lax.div(me, 8), 4),
        lax.rem(lax.div(me, 2), 4),
        lax.rem(me, 2),
    )


def device_at(y, x, z, core):
    return (((y * 4 + x) * 4 + z) * 2 + core,)


def along(place, axis, step):
    moved = list(place)
    moved[axis] = lax.rem(place[axis] + step + 4, 4)
    return moved


def slot_at(part, index):
    place = (
        lax.rem(lax.div(index, 32), 4),
        lax.rem(lax.div(index, 8), 4),
        lax.rem(lax.div(index, 2), 4),
    )
    first, second, third = ORDERS[part]
    return lax.rem(index, 2), place[third], place[second], place[first]


def shift_parts():
    offset = lax.rem(lax.axis_index("dev") * SHARD, 1024)
    return lax.div(offset, 128), lax.rem(offset, 128)


def one_hot(shape, difference, dtype):
    rows = lax.broadcasted_iota(jnp.int32, shape, 0)
    columns = lax.broadcasted_iota(jnp.int32, shape, 1)
    return jnp.where(columns - rows == difference, 1.0, 0.0).astype(dtype)


def greet(place):
    barrier = pltpu.get_barrier_semaphore()
    partners = [along(place, axis, step) for axis in range(3) for step in (1, 2, 3)]
    partners.append([place[0], place[1], place[2], 1 - place[3]])
    for partner in partners:
        pl.semaphore_signal(barrier, inc=1, device_id=device_at(*partner), device_id_type=MESH)
    pl.semaphore_wait(barrier, len(partners))


def remote(source, target, send, recv, device):
    return pltpu.make_async_remote_copy(
        src_ref=source,
        dst_ref=target,
        send_sem=send,
        recv_sem=recv,
        device_id=device_at(*device),
        device_id_type=MESH,
    )


def dot(left, right):
    return jnp.dot(left, right, preferred_element_type=F32)


def dot_nt(left, right):
    return lax.dot_general(left, right, (((1,), (1,)), ((), ())), preferred_element_type=F32)


def dot_tn(left, right):
    return lax.dot_general(left, right, (((0,), (0,)), ((), ())), preferred_element_type=F32)


def normalize(values):
    centered = values - jnp.mean(values, axis=-1, keepdims=True)
    inverse = lax.rsqrt(jnp.mean(centered * centered, axis=-1, keepdims=True) + 1e-06)
    return centered * inverse, inverse


def norm_back(grad_norm, normed, inverse):
    return inverse * (
        grad_norm
        - jnp.mean(grad_norm, axis=-1, keepdims=True)
        - normed * jnp.mean(grad_norm * normed, axis=-1, keepdims=True)
    )


def column_sums(values):
    return jnp.sum(values, axis=0, keepdims=True)


def whole_kernel(
    piece_ref, cond_ref, tokens_hbm, grad_hbm,
    out_hbm, d_tokens_hbm, d_cond_ref, summed_ref,
    slots_a, slots_b, slots_c, sib_a, sib_b, sib_c,
    one_a, one_b, one_c, two_a, two_b, two_c, three_a, three_b, three_c, total,
    tokens_ref, grad_ref, out_ref,
    flat, w_ada, w_qkv, w_proj, w_up, w_down, bias,
    silu, mod, d_mod, h1, inverse1, qkv, probs, attn_t, mixed_t, branch, resid,
    mlp_t, hidden, slope, d_mlp, d_pre, d_branch, d_mixed,
    load, store, gather_send, gather_recv, meet_send, meet_recv,
    core_send, core_recv, send, recv,
):
    slots = (slots_a, slots_b, slots_c)
    sib = (sib_a, sib_b, sib_c)
    lands = ((one_a, one_b, one_c), (two_a, two_b, two_c), (three_a, three_b, three_c))
    place = coordinates()
    core = place[3]
    sign = 1 - 2 * core
    sibling = [place[0], place[1], place[2], 1 - core]
    load_tokens = pltpu.make_async_copy(tokens_hbm, tokens_ref, load.at[0])
    load_grad = pltpu.make_async_copy(grad_hbm, grad_ref, load.at[1])
    load_tokens.start()
    load_grad.start()

    rows, lanes = shift_parts()
    x = piece_ref[...]
    low = dot(x, one_hot((128, 128), lanes, BF16)).astype(BF16)
    high = dot(x, one_hot((128, 128), lanes - 128, BF16)).astype(BF16)
    square = (BLOCK, BLOCK)
    aligned = dot(one_hot(square, -rows, BF16), low) + dot(one_hot(square, -rows - 1, BF16), high)
    aligned = aligned.astype(BF16)
    for part, slot in enumerate(slots):
        first, second, third = ORDERS[part]
        slot[core, place[third], place[second], place[first]] = aligned[
            FIRST[part] : FIRST[part] + PARTS[part]
        ]
    greet(place)

    def block(part, stage, value):
        slot = slots[part]
        first, second, third = ORDERS[part]
        if stage == 0:
            return slot.at[core, place[third], place[second], value]
        if stage == 1:
            return slot.at[core, place[third], value]
        return slot.at[core, value]

    started = []

    def push(part, stage, kind, value, device):
        ref = block(part, stage, value)
        copy = remote(
            ref, ref, gather_send.at[part, stage, kind], gather_recv.at[part, stage, kind], device
        )
        copy.start()
        started.append(copy)

    def arrived(part, stage, kind, value):
        ref = block(part, stage, value)
        remote(
            ref,
            ref,
            gather_send.at[part, stage, kind],
            gather_recv.at[part, stage, kind],
            sibling,
        ).wait_recv()

    crossed = []

    def cross(part, kind, value):
        ref = block(part, 2, value)
        copy = remote(ref, ref, meet_send.at[part, kind], meet_recv.at[part, kind], sibling)
        copy.start()
        started.append(copy)
        mine = slots[part].at[1 - core, value]
        crossed.append(
            remote(mine, mine, meet_send.at[part, kind], meet_recv.at[part, kind], sibling)
        )

    for stage in range(3):
        spots = []
        for part in range(3):
            axis = ORDERS[part][stage]
            ahead, behind = along(place, axis, sign), along(place, axis, -sign)
            across = along(place, axis, 2)
            spots.append((axis, ahead, behind, across))
            push(part, stage, 0, place[axis], ahead)
            push(part, stage, 1, place[axis], behind)
            if stage < 2:
                push(part, stage, 2, place[axis], across)
        if stage == 2:
            for part in range(3):
                cross(part, 0, place[spots[part][0]])
        for part in range(3):
            axis, ahead, behind, across = spots[part]
            arrived(part, stage, 0, behind[axis])
            if stage == 2:
                push(part, stage, 2, behind[axis], ahead)
                cross(part, 1, behind[axis])
        for part in range(3):
            axis, ahead, behind, across = spots[part]
            arrived(part, stage, 1, ahead[axis])
            if stage == 2:
                cross(part, 2, ahead[axis])
        for part in range(3):
            axis, ahead, behind, across = spots[part]
            arrived(part, stage, 2, across[axis])
            if stage == 2:
                cross(part, 3, across[axis])
    for copy in crossed:
        copy.wait_recv()
    for copy in started:
        copy.wait_send()

    def first_row(index):
        return pl.multiple_of(lax.div(index * SHARD, 1024) * 8, 8)

    def unpack(index, _):
        start = first_row(index)
        before = lax.max(index - 1, 0)
        tail = slots[2][slot_at(2, before)][32:48].astype(F32)
        tail = jnp.where(start - first_row(before) == 160, tail[:8], tail[8:])
        tail = jnp.where(index == 0, jnp.zeros_like(tail), tail)
        for part in range(3):
            value = slots[part][slot_at(part, index)].astype(F32)
            if part == 0:
                flat[pl.ds(start, 8), :] = value[:8] + tail
                flat[pl.ds(start + 8, PARTS[0] - 8), :] = value[8:]
            else:
                flat[pl.ds(start + FIRST[part], PARTS[part]), :] = value
        return 0

    lax.fori_loop(0, DEVICES, unpack, 0, unroll=4)

    def take_matrix(target, base, height, width):
        for column in range(width):
            target[:, column * 128 : (column + 1) * 128] = flat[
                pl.ds(base + column, height, stride=width), :
            ].astype(BF16)

    def take_row(base, width, offset):
        for column in range(width):
            bias[0:1, offset + column * 128 : offset + (column + 1) * 128] = flat[
                base + column : base + column + 1, :
            ]

    def put_row(base, value):
        for column in range(value.shape[1] // 128):
            flat[base + column : base + column + 1, :] = value[
                :, column * 128 : (column + 1) * 128
            ]

    def put_block(base, width, column, value):
        for number in range(value.shape[1] // 128):
            flat[pl.ds(base + column + number, value.shape[0], stride=width), :] = value[
                :, number * 128 : (number + 1) * 128
            ]

    take_matrix(w_ada, ADA, D, 18)
    take_matrix(w_qkv, QKV, D, 9)
    take_matrix(w_proj, PROJ, D, 3)
    take_matrix(w_up, UP, D, 12)
    take_matrix(w_down, DOWN, FF, 3)
    take_row(BADA, 18, 0)
    take_row(BQV, 3, 2304)
    bias[0:1, 2688:3072] = jnp.zeros((1, D), F32)
    take_row(BQV + 3, 3, 3072)
    take_row(BPROJ, 3, 3456)
    take_row(BUP, 12, 3840)
    take_row(BDOWN, 3, 5376)

    cond = cond_ref[...].astype(F32)
    silu[...] = jnp.zeros_like(silu)
    silu[0:LATENTS, :] = cond / (1.0 + jnp.exp(-cond))
    silu_low = silu[...].astype(BF16)
    mod[...] = dot(silu_low, w_ada[...]) + bias[0:1, 0:2304]
    d_mod[...] = jnp.zeros_like(d_mod)

    lane = lax.broadcasted_iota(jnp.int32, (SEQ, 128), 1)
    half = (lane < 64, lane >= 64)

    def masked(value, head):
        return jnp.where(half[head], value, jnp.zeros_like(value))

    load_tokens.wait()

    def forward_attention(latent, _):
        tokens = pl.ds(latent * SEQ, SEQ)
        x = tokens_ref[tokens, :].astype(F32)
        shift = mod[pl.ds(latent, 1), 0:D]
        scale = mod[pl.ds(latent, 1), D : 2 * D]
        gate = mod[pl.ds(latent, 1), 2 * D : 3 * D]
        normed, inverse = normalize(x)
        h1[tokens, :] = normed
        inverse1[tokens, :] = inverse
        attn_in = (normed * (1.0 + scale) + shift).astype(BF16)
        attn_t[:, tokens] = attn_in.T
        projected = (dot(attn_in, w_qkv[...]) + bias[0:1, 2304:3456]).astype(BF16)
        qkv[tokens, :] = projected

        def tail(pair, weights):
            v_t = projected[:, 2 * D + pair * 128 : 2 * D + (pair + 1) * 128].T
            zz = jnp.zeros((64, SEQ), BF16)
            spread = jnp.concatenate([jnp.concatenate([v_t[:64], zz], axis=0), jnp.concatenate([zz, v_t[64:]], axis=0)], axis=1)
            mixed_t[pair * 128 : (pair + 1) * 128, tokens] = dot(spread, jnp.concatenate(weights, axis=0)).astype(BF16)

        def soft(pair, scores):
            top = jnp.max(scores, axis=0, keepdims=True)
            powers = jnp.exp(scores - top)
            low = (powers * (1.0 / column_sums(powers))).astype(BF16)
            both = [low[:, :SEQ], low[:, SEQ:]]
            for head in range(2):
                probs[latent * HEADS + pair * 2 + head] = both[head]
            return both

        def score(pair):
            q = projected[:, pair * 128 : (pair + 1) * 128] * jnp.asarray(0.125, BF16)
            k = projected[:, D + pair * 128 : D + (pair + 1) * 128]
            return dot_nt(k, jnp.concatenate([masked(q, 0), masked(q, 1)], axis=0))

        scores = [score(pair) for pair in range(3)]
        weights = [soft(pair, scores[pair]) for pair in range(3)]
        for pair in range(3):
            tail(pair, weights[pair])
        reached = dot_tn(mixed_t[:, tokens], w_proj[...]) + bias[0:1, 3456:3840]
        branch[tokens, :] = reached
        resid[tokens, :] = x + gate * reached
        return 0

    for latent in range(LATENTS):
        forward_attention(latent, 0)

    chunk = 512
    load_grad.wait()

    def mlp(both, sums):
        sum_down, sum_up, sum_proj = sums
        tokens = pl.ds(both * 2 * SEQ, 2 * SEQ)
        rows = [pl.ds(both * 2 + number, 1) for number in range(2)]

        def tall(number):
            wide = [mod[row, number * D : (number + 1) * D] for row in rows]
            return jnp.concatenate([jnp.broadcast_to(one, (SEQ, D)) for one in wide], axis=0)

        def keep_sums(number, value):
            for row, part in zip(rows, (value[:SEQ], value[SEQ:])):
                d_mod[row, number * D : (number + 1) * D] = column_sums(part)

        gate1, shift, scale, gate = tall(2), tall(3), tall(4), tall(5)
        kept = resid[tokens, :]
        normed, inverse = normalize(kept)
        mlp_in = (normed * (1.0 + scale) + shift).astype(BF16)
        mlp_t[:, tokens] = mlp_in.T
        for start in range(0, FF, chunk):
            here = slice(start, start + chunk)
            u = dot(mlp_in, w_up[:, here]) + bias[0:1, 3840 + start : 3840 + start + chunk]
            square = u * u
            inner = u * (0.7978845608028654 + (0.7978845608028654 * 0.044715) * square)
            tangent = jnp.tanh(inner)
            above = 0.5 + 0.5 * tangent
            hidden[tokens, here] = (u * above).astype(BF16)
            rise = 0.7978845608028654 + (3 * 0.7978845608028654 * 0.044715) * square
            slope[:, here] = above + (0.5 * u) * (1.0 - tangent * tangent) * rise
        mlp_out = dot(hidden[tokens, :], w_down[...]) + bias[0:1, 5376:5760]
        out_ref[tokens, :] = (kept + gate * mlp_out).astype(BF16)
        pltpu.make_async_copy(
            out_ref.at[tokens, :], out_hbm.at[tokens, :], store.at[0, both]
        ).start()
        grad = grad_ref[tokens, :].astype(F32)
        keep_sums(5, grad * mlp_out)
        grad_mlp = (grad * gate).astype(BF16)
        d_mlp[tokens, :] = grad_mlp
        sum_down = sum_down + column_sums(grad_mlp.astype(F32))
        ups = []
        for start in range(0, FF, chunk):
            here = slice(start, start + chunk)
            value = (slope[:, here] * dot_nt(grad_mlp, w_down[here, :])).astype(BF16)
            d_pre[tokens, here] = value
            ups.append(column_sums(value.astype(F32)))
        sum_up = sum_up + jnp.concatenate(ups, axis=1)
        d_in = dot_nt(d_pre[tokens, :], w_up[...])
        keep_sums(4, d_in * normed)
        keep_sums(3, d_in)
        back = grad + norm_back(d_in * (1.0 + scale), normed, inverse)
        resid[tokens, :] = back
        keep_sums(2, back * branch[tokens, :])
        low = (back * gate1).astype(BF16)
        d_branch[tokens, :] = low
        sum_proj = sum_proj + column_sums(low.astype(F32))
        d_mixed[tokens, :] = dot_nt(low, w_proj[...]).astype(BF16)
        return sum_down, sum_up, sum_proj

    zeros = jnp.zeros((1, D), F32)
    sums = (zeros, jnp.zeros((1, FF), F32), zeros)
    for both in range(LATENTS // 2):
        sums = mlp(both, sums)
    sum_down, sum_up, sum_proj = sums
    put_row(BDOWN, sum_down)
    put_row(BUP, sum_up)
    put_row(BPROJ, sum_proj)
    for start in range(0, FF, 256):
        here = slice(start, start + 256)
        put_block(UP, 12, start // 128, dot(mlp_t[...], d_pre[:, here]))
        put_block(DOWN + start * 3, 3, 0, dot_tn(hidden[:, here], d_mlp[...]))
    put_block(PROJ, 3, 0, dot(mixed_t[...], d_branch[...]))

    def backward_attention(latent, sums):
        tokens = pl.ds(latent * SEQ, SEQ)
        row = pl.ds(latent, 1)
        scale = mod[row, D : 2 * D]
        projected = qkv[tokens, :]
        d_out = d_mixed[tokens, :]

        def columns(number, pair):
            return projected[:, number * D + pair * 128 : number * D + (pair + 1) * 128]

        def split(value):
            return jnp.concatenate([masked(value, 0), masked(value, 1)], axis=0)

        def weights_of(pair):
            return jnp.concatenate([probs[latent * HEADS + pair * 2 + head] for head in range(2)], axis=1)

        spread = [split(d_out[:, pair * 128 : (pair + 1) * 128]) for pair in range(3)]
        first = [dot_nt(columns(2, pair), spread[pair]) for pair in range(3)]
        scores = []
        for pair in range(3):
            wide = weights_of(pair).astype(F32)
            product = first[pair] * wide
            scores.append((product - wide * column_sums(product)).astype(BF16))
        for pair in range(3):
            here = slice(pair * 128, (pair + 1) * 128)
            grad_v = dot(weights_of(pair), spread[pair])
            qkv[tokens, 2 * D + pair * 128 : 2 * D + (pair + 1) * 128] = grad_v.astype(BF16)
            q = columns(0, pair) * jnp.asarray(0.125, BF16)
            grad_k = dot(scores[pair], split(q))
            qkv[tokens, D + pair * 128 : D + (pair + 1) * 128] = grad_k.astype(BF16)
            k_t = columns(1, pair).T
            zz = jnp.zeros((64, SEQ), BF16)
            lhs = jnp.concatenate([jnp.concatenate([k_t[:64], zz], axis=0), jnp.concatenate([zz, k_t[64:]], axis=0)], axis=1)
            rhs = jnp.concatenate([scores[pair][:, :SEQ], scores[pair][:, SEQ:]], axis=0)
            qkv[tokens, here] = (dot(lhs, rhs) * 0.125).astype(BF16).T
        low = qkv[tokens, :]
        normed = h1[tokens, :]
        d_in = dot_nt(low, w_qkv[...])
        d_mod[row, D : 2 * D] = column_sums(d_in * normed)
        d_mod[row, 0:D] = column_sums(d_in)
        h1[tokens, :] = resid[tokens, :] + norm_back(
            d_in * (1.0 + scale), normed, inverse1[tokens, :]
        )
        pltpu.make_async_copy(
            h1.at[tokens, :], d_tokens_hbm.at[tokens, :], store.at[1, latent]
        ).start()
        return sums + column_sums(low.astype(F32))

    sum_qkv = jnp.zeros((1, 3 * D), F32)
    for latent in range(LATENTS):
        sum_qkv = backward_attention(latent, sum_qkv)
    put_row(BQV, sum_qkv[:, :D])
    put_row(BQV + 3, sum_qkv[:, 2 * D :])
    for start in range(0, 3 * D, D):
        put_block(QKV, 9, start // 128, dot(attn_t[...], qkv[:, start : start + D]))
    d_mod_low = d_mod[...].astype(BF16)
    put_row(BADA, column_sums(d_mod_low.astype(F32)))
    for start in range(0, 6 * D, D):
        put_block(ADA, 18, start // 128, dot_tn(silu_low, d_mod_low[:, start : start + D]))
    d_silu = dot_nt(d_mod_low, w_ada[...])[0:LATENTS]
    gate = 1.0 / (1.0 + jnp.exp(-cond))
    d_cond_ref[...] = d_silu * (gate * (1.0 + cond * (1.0 - gate)))

    def slot_row(part, c, b, a, which):
        spot = [0, 0, 0]
        first, second, third = ORDERS[part]
        spot[third], spot[second], spot[first] = c, b, a
        start = first_row(device_at(*spot, which)[0])
        return pl.ds(pl.multiple_of(start + FIRST[part], 8), PARTS[part])

    def pack(part, value):
        def body(step, _):
            b, a = lax.div(step, 4), lax.rem(step, 4)
            slots[part][1 - core, value, b, a] = flat[
                slot_row(part, value, b, a, 1 - core), :
            ].astype(BF16)
            return 0

        lax.fori_loop(0, 16, body, 0, unroll=8)

    def meet(part, value):
        def body(step, _):
            b, a = lax.div(step, 4), lax.rem(step, 4)
            mine = flat[slot_row(part, value, b, a, core), :]
            slots[part][core, value, b, a] = (mine + sib[part][value, b, a].astype(F32)).astype(
                BF16
            )
            return 0

        lax.fori_loop(0, 16, body, 0, unroll=8)

    started = []
    spots = []
    for part in range(3):
        axis = ORDERS[part][2]
        spots.append(
            (axis, along(place, axis, 2), along(place, axis, -sign), along(place, axis, sign))
        )
    for kind in range(4):
        for part in range(3):
            axis = spots[part][0]
            value = place[axis] if kind == 3 else spots[part][(1, 3, 2)[kind]][axis]
            pack(part, value)
            copy = remote(
                slots[part].at[1 - core, value],
                sib[part].at[value],
                core_send.at[part, kind],
                core_recv.at[part, kind],
                sibling,
            )
            copy.start()
            started.append(copy)

    def send_sum(part, stage, kind, source, device):
        copy = remote(
            source,
            lands[stage][part].at[kind],
            send.at[part, stage, kind],
            recv.at[part, stage, kind],
            device,
        )
        copy.start()
        started.append(copy)

    def sum_arrived(part, stage, kind):
        ref = lands[stage][part].at[kind]
        remote(
            ref, ref, send.at[part, stage, kind], recv.at[part, stage, kind], sibling
        ).wait_recv()

    def add(target, *others):
        shape = target.shape

        def body(step, _):
            if len(shape) == 4:
                here = (lax.div(step, shape[1]), lax.rem(step, shape[1]))
            else:
                here = (step,)
            value = target[here].astype(F32)
            for other in others:
                value = value + other[here].astype(F32)
            target[here] = value.astype(BF16)
            return 0

        count = shape[0] * shape[1] if len(shape) == 4 else shape[0]
        lax.fori_loop(0, count, body, 0, unroll=4)

    for kind in range(4):
        for part in range(3):
            axis = spots[part][0]
            value = place[axis] if kind == 3 else spots[part][1 + kind][axis]
            ref = sib[part].at[value]
            mine = slots[part].at[core, value]
            remote(
                ref, ref, core_send.at[part, kind], core_recv.at[part, kind], sibling
            ).wait_recv()
            meet(part, value)
            if kind == 0:
                send_sum(part, 0, 0, mine, spots[part][3])
            if kind == 1:
                send_sum(part, 0, 1, mine, spots[part][2])
            if kind == 2:
                sum_arrived(part, 0, 0)
                add(mine, lands[0][part].at[0])
                send_sum(part, 0, 2, mine, spots[part][3])
    held = []
    for part in range(3):
        ref = slots[part].at[core, place[spots[part][0]]]
        sum_arrived(part, 0, 1)
        sum_arrived(part, 0, 2)
        add(ref, lands[0][part].at[1], lands[0][part].at[2])
        held.append(ref)
        axis = ORDERS[part][1]
        for kind in range(3):
            far = along(place, axis, kind + 1)
            send_sum(part, 1, kind, ref.at[far[axis]], far)
    for part in range(3):
        axis = ORDERS[part][1]
        ref = held[part].at[place[axis]]
        for kind in range(3):
            sum_arrived(part, 1, kind)
        add(ref, *[lands[1][part].at[kind] for kind in range(3)])
        held[part] = ref
        axis = ORDERS[part][0]
        for kind in range(3):
            far = along(place, axis, kind + 1)
            send_sum(part, 2, kind, ref.at[far[axis]], far)
    for part in range(3):
        axis = ORDERS[part][0]
        value = held[part][place[axis]].astype(F32)
        for kind in range(3):
            sum_arrived(part, 2, kind)
            value = value + lands[2][part][kind].astype(F32)
        total[FIRST[part] : FIRST[part] + PARTS[part], :] = value
    for copy in started:
        copy.wait_send()
    for both in range(LATENTS // 2):
        tokens = pl.ds(both * 2 * SEQ, 2 * SEQ)
        pltpu.make_async_copy(
            out_ref.at[tokens, :], out_hbm.at[tokens, :], store.at[0, both]
        ).wait()
    for latent in range(LATENTS):
        tokens = pl.ds(latent * SEQ, SEQ)
        pltpu.make_async_copy(
            h1.at[tokens, :], d_tokens_hbm.at[tokens, :], store.at[1, latent]
        ).wait()
    summed = total[...]

    def product(left, right):
        return jnp.dot(left, right, preferred_element_type=F32, precision=lax.Precision.HIGHEST)

    low = product(summed, one_hot((128, 128), -lanes, F32))
    high = product(summed, one_hot((128, 128), 128 - lanes, F32))
    summed_ref[...] = product(one_hot(square, rows, F32), low) + product(
        one_hot(square, rows + 1, F32), high
    )


def transformer_block(piece, cond, tokens, d_out):
    vmem = pl.BlockSpec(memory_space=pltpu.VMEM)
    hbm = pl.BlockSpec(memory_space=pl.ANY)
    scratch = [((2, 4, 4, 4, rows, 128), BF16) for rows in PARTS]
    scratch += [((4, 4, 4, rows, 128), BF16) for rows in PARTS]
    scratch += [((3, 4, 4, rows, 128), BF16) for rows in PARTS]
    scratch += [((3, 4, rows, 128), BF16) for rows in PARTS]
    scratch += [((3, rows, 128), BF16) for rows in PARTS]
    scratch += [
        ((BLOCK, 128), F32),
        ((ROWS, D), BF16),
        ((ROWS, D), BF16),
        ((ROWS, D), BF16),
        ((FLAT_ROWS, 128), F32),
        ((D, 6 * D), BF16),
        ((D, 3 * D), BF16),
        ((D, D), BF16),
        ((D, FF), BF16),
        ((FF, D), BF16),
        ((8, 5760), F32),
        ((16, D), F32),
        ((16, 6 * D), F32),
        ((16, 6 * D), F32),
        ((ROWS, D), F32),
        ((ROWS, 1), F32),
        ((ROWS, 3 * D), BF16),
        ((LATENTS * HEADS, SEQ, SEQ), BF16),
        ((D, ROWS), BF16),
        ((D, ROWS), BF16),
        ((ROWS, D), F32),
        ((ROWS, D), F32),
        ((D, ROWS), BF16),
        ((ROWS, FF), BF16),
        ((2 * SEQ, FF), F32),
        ((ROWS, D), BF16),
        ((ROWS, FF), BF16),
        ((ROWS, D), BF16),
        ((ROWS, D), BF16),
    ]
    sems = [(2,), (2, 4), (3, 3, 3), (3, 3, 3), (3, 4), (3, 4), (3, 4), (3, 4), (3, 3, 3), (3, 3, 3)]
    return pl.pallas_call(
        whole_kernel,
        out_shape=[
            jax.ShapeDtypeStruct((ROWS, D), BF16),
            jax.ShapeDtypeStruct((ROWS, D), F32),
            jax.ShapeDtypeStruct((LATENTS, D), F32),
            jax.ShapeDtypeStruct((BLOCK, 128), F32),
        ],
        in_specs=[vmem, vmem, hbm, hbm],
        out_specs=[hbm, hbm, vmem, vmem],
        scratch_shapes=[pltpu.VMEM(shape, dtype) for shape, dtype in scratch]
        + [pltpu.SemaphoreType.DMA(shape) for shape in sems],
        compiler_params=pltpu.CompilerParams(
            collective_id=0, has_side_effects=True, vmem_limit_bytes=61 * 1024 * 1024
        ),
        name="block",
    )(piece, cond, tokens, d_out)


def hand_over_kernel(*refs):
    sources, targets, middles, (into, out_of) = refs[:3], refs[3:6], refs[6:9], refs[9:]
    firsts, seconds = [], []
    for number, (source, middle, target) in enumerate(zip(sources, middles, targets)):
        pieces = 4 if source.shape[0] == ROWS else 1
        rows = source.shape[0] // pieces
        for piece in range(pieces):
            here = pl.ds(piece * rows, rows)
            firsts.append(
                pltpu.make_async_copy(source.at[here], middle.at[here], into.at[number, piece])
            )
            seconds.append(
                pltpu.make_async_copy(middle.at[here], target.at[here], out_of.at[number, piece])
            )
    for copy in firsts:
        copy.start()
    for first, second in zip(firsts, seconds):
        first.wait()
        second.start()
    for copy in seconds:
        copy.wait()


def hand_over(*results):
    hbm = pl.BlockSpec(memory_space=pl.ANY)
    return pl.pallas_call(
        hand_over_kernel,
        out_shape=[jax.ShapeDtypeStruct(result.shape, result.dtype) for result in results],
        in_specs=[hbm] * 3,
        out_specs=[hbm] * 3,
        scratch_shapes=[pltpu.VMEM(result.shape, result.dtype) for result in results]
        + [pltpu.SemaphoreType.DMA((3, 4))] * 2,
        compiler_params=pltpu.CompilerParams(vmem_limit_bytes=63 * 1024 * 1024),
        name="hand_over",
    )(*results)


def local(tokens, cond, params, d_out):
    piece = jnp.pad(params, (0, BLOCK * 128 - SHARD)).reshape(BLOCK, 128)
    out, d_tokens, d_cond, summed = transformer_block(piece, cond, tokens, d_out)
    out, d_tokens, d_cond = hand_over(out, d_tokens, d_cond)
    return out, d_tokens, d_cond, summed.reshape(-1)[:SHARD]


def solution(mesh):
    placed = (P("dev", None), P("dev", None), P("dev"), P("dev", None))
    return jax.shard_map(
        local,
        mesh=mesh,
        in_specs=placed,
        out_specs=(P("dev", None), P("dev", None), P("dev", None), P("dev")),
        check_vma=False,
    )
```

```python
import functools

import jax
import jax.numpy as jnp
from jax import lax
from jax.experimental import pallas as pl
from jax.experimental.pallas import tpu as pltpu
from jax.sharding import PartitionSpec as P

D = 384
FF = 1536
HEADS = 6
SEQ = 256
LATENTS = 4
ROWS = LATENTS * SEQ
SHARD = 20778
DEVICES = 128
BLOCK = 176
PARTS = (64, 64, 48)
FIRST = (0, 64, 128)
FLAT_ROWS = 20784

ADA, BADA = 0, 6912
QKV, BQV = 6930, 10386
PROJ, BPROJ = 10392, 11544
UP, BUP = 11547, 16155
DOWN, BDOWN = 16167, 20775

MESH = pl.DeviceIdType.MESH
BF16 = jnp.bfloat16
F32 = jnp.float32

ORDERS = ((2, 1, 0), (1, 0, 2), (0, 2, 1))


def coordinates():
    me = lax.axis_index("dev")
    return (
        lax.rem(lax.div(me, 32), 4),
        lax.rem(lax.div(me, 8), 4),
        lax.rem(lax.div(me, 2), 4),
        lax.rem(me, 2),
    )


def device_at(y, x, z, core):
    return (((y * 4 + x) * 4 + z) * 2 + core,)


def along(place, axis, step):
    moved = list(place)
    moved[axis] = lax.rem(place[axis] + step + 4, 4)
    return moved


def slot_at(part, index):
    place = (
        lax.rem(lax.div(index, 32), 4),
        lax.rem(lax.div(index, 8), 4),
        lax.rem(lax.div(index, 2), 4),
    )
    first, second, third = ORDERS[part]
    return lax.rem(index, 2), place[third], place[second], place[first]


def shift_parts():
    offset = lax.rem(lax.axis_index("dev") * SHARD, 1024)
    return lax.div(offset, 128), lax.rem(offset, 128)


def one_hot(shape, difference, dtype):
    rows = lax.broadcasted_iota(jnp.int32, shape, 0)
    columns = lax.broadcasted_iota(jnp.int32, shape, 1)
    return jnp.where(columns - rows == difference, 1.0, 0.0).astype(dtype)


def greet(place):
    barrier = pltpu.get_barrier_semaphore()
    partners = [along(place, axis, step) for axis in range(3) for step in (1, 2, 3)]
    partners.append([place[0], place[1], place[2], 1 - place[3]])
    for partner in partners:
        pl.semaphore_signal(barrier, inc=1, device_id=device_at(*partner), device_id_type=MESH)
    pl.semaphore_wait(barrier, len(partners))


def remote(source, target, send, recv, device):
    return pltpu.make_async_remote_copy(
        src_ref=source,
        dst_ref=target,
        send_sem=send,
        recv_sem=recv,
        device_id=device_at(*device),
        device_id_type=MESH,
    )


def dot(left, right):
    return jnp.dot(left, right, preferred_element_type=F32)


def dot_nt(left, right):
    return lax.dot_general(left, right, (((1,), (1,)), ((), ())), preferred_element_type=F32)


def dot_tn(left, right):
    return lax.dot_general(left, right, (((0,), (0,)), ((), ())), preferred_element_type=F32)


def normalize(values):
    centered = values - jnp.mean(values, axis=-1, keepdims=True)
    inverse = lax.rsqrt(jnp.mean(centered * centered, axis=-1, keepdims=True) + 1e-06)
    return centered * inverse, inverse


def norm_back(grad_norm, normed, inverse):
    return inverse * (
        grad_norm
        - jnp.mean(grad_norm, axis=-1, keepdims=True)
        - normed * jnp.mean(grad_norm * normed, axis=-1, keepdims=True)
    )


def column_sums(values):
    return jnp.sum(values, axis=0, keepdims=True)


def whole_kernel(
    piece_ref, cond_ref, tokens_hbm, grad_hbm,
    out_hbm, d_tokens_hbm, d_cond_ref, summed_ref,
    slots_a, slots_b, slots_c, sib_a, sib_b, sib_c,
    one_a, one_b, one_c, two_a, two_b, two_c, three_a, three_b, three_c, total,
    tokens_ref, grad_ref, out_ref,
    flat, w_ada, w_qkv, w_proj, w_up, w_down, bias,
    silu, mod, d_mod, h1, inverse1, qkv, probs, attn_t, mixed_t, branch, resid,
    mlp_t, hidden, slope, d_mlp, d_pre, d_branch, d_mixed,
    load, store, gather_send, gather_recv, meet_send, meet_recv,
    core_send, core_recv, send, recv,
):
    slots = (slots_a, slots_b, slots_c)
    sib = (sib_a, sib_b, sib_c)
    lands = ((one_a, one_b, one_c), (two_a, two_b, two_c), (three_a, three_b, three_c))
    place = coordinates()
    core = place[3]
    sign = 1 - 2 * core
    sibling = [place[0], place[1], place[2], 1 - core]
    load_tokens = pltpu.make_async_copy(tokens_hbm, tokens_ref, load.at[0])
    load_grad = pltpu.make_async_copy(grad_hbm, grad_ref, load.at[1])
    load_tokens.start()
    load_grad.start()

    rows, lanes = shift_parts()
    x = piece_ref[...]
    low = dot(x, one_hot((128, 128), lanes, BF16)).astype(BF16)
    high = dot(x, one_hot((128, 128), lanes - 128, BF16)).astype(BF16)
    square = (BLOCK, BLOCK)
    aligned = dot(one_hot(square, -rows, BF16), low) + dot(one_hot(square, -rows - 1, BF16), high)
    aligned = aligned.astype(BF16)
    for part, slot in enumerate(slots):
        first, second, third = ORDERS[part]
        slot[core, place[third], place[second], place[first]] = aligned[
            FIRST[part] : FIRST[part] + PARTS[part]
        ]
    greet(place)

    def block(part, stage, value):
        slot = slots[part]
        first, second, third = ORDERS[part]
        if stage == 0:
            return slot.at[core, place[third], place[second], value]
        if stage == 1:
            return slot.at[core, place[third], value]
        return slot.at[core, value]

    started = []

    def push(part, stage, kind, value, device):
        ref = block(part, stage, value)
        copy = remote(
            ref, ref, gather_send.at[part, stage, kind], gather_recv.at[part, stage, kind], device
        )
        copy.start()
        started.append(copy)

    def arrived(part, stage, kind, value):
        ref = block(part, stage, value)
        remote(
            ref,
            ref,
            gather_send.at[part, stage, kind],
            gather_recv.at[part, stage, kind],
            sibling,
        ).wait_recv()

    crossed = []

    def cross(part, kind, value):
        ref = block(part, 2, value)
        copy = remote(ref, ref, meet_send.at[part, kind], meet_recv.at[part, kind], sibling)
        copy.start()
        started.append(copy)
        mine = slots[part].at[1 - core, value]
        crossed.append(
            remote(mine, mine, meet_send.at[part, kind], meet_recv.at[part, kind], sibling)
        )

    for stage in range(3):
        spots = []
        for part in range(3):
            axis = ORDERS[part][stage]
            ahead, behind = along(place, axis, sign), along(place, axis, -sign)
            across = along(place, axis, 2)
            spots.append((axis, ahead, behind, across))
            push(part, stage, 0, place[axis], ahead)
            push(part, stage, 1, place[axis], behind)
            if stage < 2:
                push(part, stage, 2, place[axis], across)
        if stage == 2:
            for part in range(3):
                cross(part, 0, place[spots[part][0]])
        for part in range(3):
            axis, ahead, behind, across = spots[part]
            arrived(part, stage, 0, behind[axis])
            if stage == 2:
                push(part, stage, 2, behind[axis], ahead)
                cross(part, 1, behind[axis])
        for part in range(3):
            axis, ahead, behind, across = spots[part]
            arrived(part, stage, 1, ahead[axis])
            if stage == 2:
                cross(part, 2, ahead[axis])
        for part in range(3):
            axis, ahead, behind, across = spots[part]
            arrived(part, stage, 2, across[axis])
            if stage == 2:
                cross(part, 3, across[axis])
    for copy in crossed:
        copy.wait_recv()
    for copy in started:
        copy.wait_send()

    def first_row(index):
        return pl.multiple_of(lax.div(index * SHARD, 1024) * 8, 8)

    def unpack(index, _):
        start = first_row(index)
        before = lax.max(index - 1, 0)
        tail = slots[2][slot_at(2, before)][32:48].astype(F32)
        tail = jnp.where(start - first_row(before) == 160, tail[:8], tail[8:])
        tail = jnp.where(index == 0, jnp.zeros_like(tail), tail)
        for part in range(3):
            value = slots[part][slot_at(part, index)].astype(F32)
            if part == 0:
                flat[pl.ds(start, 8), :] = value[:8] + tail
                flat[pl.ds(start + 8, PARTS[0] - 8), :] = value[8:]
            else:
                flat[pl.ds(start + FIRST[part], PARTS[part]), :] = value
        return 0

    lax.fori_loop(0, DEVICES, unpack, 0, unroll=4)

    def take_matrix(target, base, height, width):
        for column in range(width):
            target[:, column * 128 : (column + 1) * 128] = flat[
                pl.ds(base + column, height, stride=width), :
            ].astype(BF16)

    def take_row(base, width, offset):
        for column in range(width):
            bias[0:1, offset + column * 128 : offset + (column + 1) * 128] = flat[
                base + column : base + column + 1, :
            ]

    def put_row(base, value):
        for column in range(value.shape[1] // 128):
            flat[base + column : base + column + 1, :] = value[
                :, column * 128 : (column + 1) * 128
            ]

    def put_block(base, width, column, value):
        for number in range(value.shape[1] // 128):
            flat[pl.ds(base + column + number, value.shape[0], stride=width), :] = value[
                :, number * 128 : (number + 1) * 128
            ]

    take_matrix(w_ada, ADA, D, 18)
    take_matrix(w_qkv, QKV, D, 9)
    take_matrix(w_proj, PROJ, D, 3)
    take_matrix(w_up, UP, D, 12)
    take_matrix(w_down, DOWN, FF, 3)
    take_row(BADA, 18, 0)
    take_row(BQV, 3, 2304)
    bias[0:1, 2688:3072] = jnp.zeros((1, D), F32)
    take_row(BQV + 3, 3, 3072)
    take_row(BPROJ, 3, 3456)
    take_row(BUP, 12, 3840)
    take_row(BDOWN, 3, 5376)

    cond = cond_ref[...].astype(F32)
    silu[...] = jnp.zeros_like(silu)
    silu[0:LATENTS, :] = cond / (1.0 + jnp.exp(-cond))
    silu_low = silu[...].astype(BF16)
    mod[...] = dot(silu_low, w_ada[...]) + bias[0:1, 0:2304]
    d_mod[...] = jnp.zeros_like(d_mod)

    lane = lax.broadcasted_iota(jnp.int32, (SEQ, 128), 1)
    half = (lane < 64, lane >= 64)

    def masked(value, head):
        return jnp.where(half[head], value, jnp.zeros_like(value))

    load_tokens.wait()

    def forward_attention(latent, _):
        tokens = pl.ds(latent * SEQ, SEQ)
        x = tokens_ref[tokens, :].astype(F32)
        shift = mod[pl.ds(latent, 1), 0:D]
        scale = mod[pl.ds(latent, 1), D : 2 * D]
        gate = mod[pl.ds(latent, 1), 2 * D : 3 * D]
        normed, inverse = normalize(x)
        h1[tokens, :] = normed
        inverse1[tokens, :] = inverse
        attn_in = (normed * (1.0 + scale) + shift).astype(BF16)
        attn_t[:, tokens] = attn_in.T
        projected = (dot(attn_in, w_qkv[...]) + bias[0:1, 2304:3456]).astype(BF16)
        qkv[tokens, :] = projected

        def tail(pair, weights):
            v_t = projected[:, 2 * D + pair * 128 : 2 * D + (pair + 1) * 128].T
            zz = jnp.zeros((64, SEQ), BF16)
            spread = jnp.concatenate([jnp.concatenate([v_t[:64], zz], axis=0), jnp.concatenate([zz, v_t[64:]], axis=0)], axis=1)
            mixed_t[pair * 128 : (pair + 1) * 128, tokens] = dot(spread, jnp.concatenate(weights, axis=0)).astype(BF16)

        def soft(pair, scores):
            top = jnp.max(scores, axis=0, keepdims=True)
            powers = jnp.exp(scores - top)
            low = (powers * (1.0 / column_sums(powers))).astype(BF16)
            both = [low[:, :SEQ], low[:, SEQ:]]
            for head in range(2):
                probs[latent * HEADS + pair * 2 + head] = both[head]
            return both

        def score(pair):
            q = projected[:, pair * 128 : (pair + 1) * 128] * jnp.asarray(0.125, BF16)
            k = projected[:, D + pair * 128 : D + (pair + 1) * 128]
            return dot_nt(k, jnp.concatenate([masked(q, 0), masked(q, 1)], axis=0))

        scores = [score(pair) for pair in range(3)]
        weights = [soft(pair, scores[pair]) for pair in range(3)]
        for pair in range(3):
            tail(pair, weights[pair])
        reached = dot_tn(mixed_t[:, tokens], w_proj[...]) + bias[0:1, 3456:3840]
        branch[tokens, :] = reached
        resid[tokens, :] = x + gate * reached
        return 0

    for latent in range(LATENTS):
        forward_attention(latent, 0)

    chunk = 512
    load_grad.wait()

    def mlp(both, sums):
        sum_down, sum_up, sum_proj = sums
        tokens = pl.ds(both * 2 * SEQ, 2 * SEQ)
        rows = [pl.ds(both * 2 + number, 1) for number in range(2)]

        def tall(number):
            wide = [mod[row, number * D : (number + 1) * D] for row in rows]
            return jnp.concatenate([jnp.broadcast_to(one, (SEQ, D)) for one in wide], axis=0)

        def keep_sums(number, value):
            for row, part in zip(rows, (value[:SEQ], value[SEQ:])):
                d_mod[row, number * D : (number + 1) * D] = column_sums(part)

        gate1, shift, scale, gate = tall(2), tall(3), tall(4), tall(5)
        kept = resid[tokens, :]
        normed, inverse = normalize(kept)
        mlp_in = (normed * (1.0 + scale) + shift).astype(BF16)
        mlp_t[:, tokens] = mlp_in.T
        for start in range(0, FF, chunk):
            here = slice(start, start + chunk)
            u = dot(mlp_in, w_up[:, here]) + bias[0:1, 3840 + start : 3840 + start + chunk]
            square = u * u
            inner = u * (0.7978845608028654 + (0.7978845608028654 * 0.044715) * square)
            tangent = jnp.tanh(inner)
            above = 0.5 + 0.5 * tangent
            hidden[tokens, here] = (u * above).astype(BF16)
            rise = 0.7978845608028654 + (3 * 0.7978845608028654 * 0.044715) * square
            slope[:, here] = above + (0.5 * u) * (1.0 - tangent * tangent) * rise
        mlp_out = dot(hidden[tokens, :], w_down[...]) + bias[0:1, 5376:5760]
        out_ref[tokens, :] = (kept + gate * mlp_out).astype(BF16)
        pltpu.make_async_copy(
            out_ref.at[tokens, :], out_hbm.at[tokens, :], store.at[0, both]
        ).start()
        grad = grad_ref[tokens, :].astype(F32)
        keep_sums(5, grad * mlp_out)
        grad_mlp = (grad * gate).astype(BF16)
        d_mlp[tokens, :] = grad_mlp
        sum_down = sum_down + column_sums(grad_mlp.astype(F32))
        ups = []
        for start in range(0, FF, chunk):
            here = slice(start, start + chunk)
            value = (slope[:, here] * dot_nt(grad_mlp, w_down[here, :])).astype(BF16)
            d_pre[tokens, here] = value
            ups.append(column_sums(value.astype(F32)))
        sum_up = sum_up + jnp.concatenate(ups, axis=1)
        d_in = dot_nt(d_pre[tokens, :], w_up[...])
        keep_sums(4, d_in * normed)
        keep_sums(3, d_in)
        back = grad + norm_back(d_in * (1.0 + scale), normed, inverse)
        resid[tokens, :] = back
        keep_sums(2, back * branch[tokens, :])
        low = (back * gate1).astype(BF16)
        d_branch[tokens, :] = low
        sum_proj = sum_proj + column_sums(low.astype(F32))
        d_mixed[tokens, :] = dot_nt(low, w_proj[...]).astype(BF16)
        return sum_down, sum_up, sum_proj

    zeros = jnp.zeros((1, D), F32)
    sums = (zeros, jnp.zeros((1, FF), F32), zeros)
    for both in range(LATENTS // 2):
        sums = mlp(both, sums)
    sum_down, sum_up, sum_proj = sums
    put_row(BDOWN, sum_down)
    put_row(BUP, sum_up)
    put_row(BPROJ, sum_proj)
    for start in range(0, FF, 256):
        here = slice(start, start + 256)
        put_block(UP, 12, start // 128, dot(mlp_t[...], d_pre[:, here]))
        put_block(DOWN + start * 3, 3, 0, dot_tn(hidden[:, here], d_mlp[...]))
    put_block(PROJ, 3, 0, dot(mixed_t[...], d_branch[...]))

    def backward_attention(latent, sums):
        tokens = pl.ds(latent * SEQ, SEQ)
        row = pl.ds(latent, 1)
        scale = mod[row, D : 2 * D]
        projected = qkv[tokens, :]
        d_out = d_mixed[tokens, :]

        def columns(number, pair):
            return projected[:, number * D + pair * 128 : number * D + (pair + 1) * 128]

        def split(value):
            return jnp.concatenate([masked(value, 0), masked(value, 1)], axis=0)

        def weights_of(pair):
            return jnp.concatenate([probs[latent * HEADS + pair * 2 + head] for head in range(2)], axis=1)

        spread = [split(d_out[:, pair * 128 : (pair + 1) * 128]) for pair in range(3)]
        first = [dot_nt(columns(2, pair), spread[pair]) for pair in range(3)]
        scores = []
        for pair in range(3):
            wide = weights_of(pair).astype(F32)
            product = first[pair] * wide
            scores.append((product - wide * column_sums(product)).astype(BF16))
        for pair in range(3):
            here = slice(pair * 128, (pair + 1) * 128)
            grad_v = dot(weights_of(pair), spread[pair])
            qkv[tokens, 2 * D + pair * 128 : 2 * D + (pair + 1) * 128] = grad_v.astype(BF16)
            q = columns(0, pair) * jnp.asarray(0.125, BF16)
            grad_k = dot(scores[pair], split(q))
            qkv[tokens, D + pair * 128 : D + (pair + 1) * 128] = grad_k.astype(BF16)
            k_t = columns(1, pair).T
            zz = jnp.zeros((64, SEQ), BF16)
            lhs = jnp.concatenate([jnp.concatenate([k_t[:64], zz], axis=0), jnp.concatenate([zz, k_t[64:]], axis=0)], axis=1)
            rhs = jnp.concatenate([scores[pair][:, :SEQ], scores[pair][:, SEQ:]], axis=0)
            qkv[tokens, here] = (dot(lhs, rhs) * 0.125).astype(BF16).T
        low = qkv[tokens, :]
        normed = h1[tokens, :]
        d_in = dot_nt(low, w_qkv[...])
        d_mod[row, D : 2 * D] = column_sums(d_in * normed)
        d_mod[row, 0:D] = column_sums(d_in)
        h1[tokens, :] = resid[tokens, :] + norm_back(
            d_in * (1.0 + scale), normed, inverse1[tokens, :]
        )
        pltpu.make_async_copy(
            h1.at[tokens, :], d_tokens_hbm.at[tokens, :], store.at[1, latent]
        ).start()
        return sums + column_sums(low.astype(F32))

    sum_qkv = jnp.zeros((1, 3 * D), F32)
    for latent in range(LATENTS):
        sum_qkv = backward_attention(latent, sum_qkv)
    put_row(BQV, sum_qkv[:, :D])
    put_row(BQV + 3, sum_qkv[:, 2 * D :])
    for start in range(0, 3 * D, D):
        put_block(QKV, 9, start // 128, dot(attn_t[...], qkv[:, start : start + D]))
    d_mod_low = d_mod[...].astype(BF16)
    put_row(BADA, column_sums(d_mod_low.astype(F32)))
    for start in range(0, 6 * D, D):
        put_block(ADA, 18, start // 128, dot_tn(silu_low, d_mod_low[:, start : start + D]))
    d_silu = dot_nt(d_mod_low, w_ada[...])[0:LATENTS]
    gate = 1.0 / (1.0 + jnp.exp(-cond))
    d_cond_ref[...] = d_silu * (gate * (1.0 + cond * (1.0 - gate)))

    def slot_row(part, c, b, a, which):
        spot = [0, 0, 0]
        first, second, third = ORDERS[part]
        spot[third], spot[second], spot[first] = c, b, a
        start = first_row(device_at(*spot, which)[0])
        return pl.ds(pl.multiple_of(start + FIRST[part], 8), PARTS[part])

    def pack(part, value):
        def body(step, _):
            b, a = lax.div(step, 4), lax.rem(step, 4)
            slots[part][1 - core, value, b, a] = flat[
                slot_row(part, value, b, a, 1 - core), :
            ].astype(BF16)
            return 0

        lax.fori_loop(0, 16, body, 0, unroll=8)

    def meet(part, value):
        def body(step, _):
            b, a = lax.div(step, 4), lax.rem(step, 4)
            mine = flat[slot_row(part, value, b, a, core), :]
            slots[part][core, value, b, a] = (mine + sib[part][value, b, a].astype(F32)).astype(
                BF16
            )
            return 0

        lax.fori_loop(0, 16, body, 0, unroll=8)

    started = []
    spots = []
    for part in range(3):
        axis = ORDERS[part][2]
        spots.append(
            (axis, along(place, axis, 2), along(place, axis, -sign), along(place, axis, sign))
        )
    for kind in range(4):
        for part in range(3):
            axis = spots[part][0]
            value = place[axis] if kind == 3 else spots[part][(1, 3, 2)[kind]][axis]
            pack(part, value)
            copy = remote(
                slots[part].at[1 - core, value],
                sib[part].at[value],
                core_send.at[part, kind],
                core_recv.at[part, kind],
                sibling,
            )
            copy.start()
            started.append(copy)

    def send_sum(part, stage, kind, source, device):
        copy = remote(
            source,
            lands[stage][part].at[kind],
            send.at[part, stage, kind],
            recv.at[part, stage, kind],
            device,
        )
        copy.start()
        started.append(copy)

    def sum_arrived(part, stage, kind):
        ref = lands[stage][part].at[kind]
        remote(
            ref, ref, send.at[part, stage, kind], recv.at[part, stage, kind], sibling
        ).wait_recv()

    def add(target, *others):
        shape = target.shape

        def body(step, _):
            if len(shape) == 4:
                here = (lax.div(step, shape[1]), lax.rem(step, shape[1]))
            else:
                here = (step,)
            value = target[here].astype(F32)
            for other in others:
                value = value + other[here].astype(F32)
            target[here] = value.astype(BF16)
            return 0

        count = shape[0] * shape[1] if len(shape) == 4 else shape[0]
        lax.fori_loop(0, count, body, 0, unroll=4)

    for kind in range(4):
        for part in range(3):
            axis = spots[part][0]
            value = place[axis] if kind == 3 else spots[part][1 + kind][axis]
            ref = sib[part].at[value]
            mine = slots[part].at[core, value]
            remote(
                ref, ref, core_send.at[part, kind], core_recv.at[part, kind], sibling
            ).wait_recv()
            meet(part, value)
            if kind == 0:
                send_sum(part, 0, 0, mine, spots[part][3])
            if kind == 1:
                send_sum(part, 0, 1, mine, spots[part][2])
            if kind == 2:
                sum_arrived(part, 0, 0)
                add(mine, lands[0][part].at[0])
                send_sum(part, 0, 2, mine, spots[part][3])
    held = []
    for part in range(3):
        ref = slots[part].at[core, place[spots[part][0]]]
        sum_arrived(part, 0, 1)
        sum_arrived(part, 0, 2)
        add(ref, lands[0][part].at[1], lands[0][part].at[2])
        held.append(ref)
        axis = ORDERS[part][1]
        for kind in range(3):
            far = along(place, axis, kind + 1)
            send_sum(part, 1, kind, ref.at[far[axis]], far)
    for part in range(3):
        axis = ORDERS[part][1]
        ref = held[part].at[place[axis]]
        for kind in range(3):
            sum_arrived(part, 1, kind)
        add(ref, *[lands[1][part].at[kind] for kind in range(3)])
        held[part] = ref
        axis = ORDERS[part][0]
        for kind in range(3):
            far = along(place, axis, kind + 1)
            send_sum(part, 2, kind, ref.at[far[axis]], far)
    for part in range(3):
        axis = ORDERS[part][0]
        value = held[part][place[axis]].astype(F32)
        for kind in range(3):
            sum_arrived(part, 2, kind)
            value = value + lands[2][part][kind].astype(F32)
        total[FIRST[part] : FIRST[part] + PARTS[part], :] = value
    for copy in started:
        copy.wait_send()
    for both in range(LATENTS // 2):
        tokens = pl.ds(both * 2 * SEQ, 2 * SEQ)
        pltpu.make_async_copy(
            out_ref.at[tokens, :], out_hbm.at[tokens, :], store.at[0, both]
        ).wait()
    for latent in range(LATENTS):
        tokens = pl.ds(latent * SEQ, SEQ)
        pltpu.make_async_copy(
            h1.at[tokens, :], d_tokens_hbm.at[tokens, :], store.at[1, latent]
        ).wait()
    count = BLOCK - 8
    place_in_row = lax.broadcasted_iota(jnp.int32, (count, 128), 1)
    back = lax.rem(128 - lanes, 128)
    here = pltpu.roll(total[pl.ds(rows, count), :], back, axis=1)
    below = pltpu.roll(total[pl.ds(rows + 1, count), :], back, axis=1)
    summed_ref[0:count, :] = jnp.where(place_in_row < 128 - lanes, here, below)
    summed_ref[count:BLOCK, :] = jnp.zeros((8, 128), F32)


def transformer_block(piece, cond, tokens, d_out):
    vmem = pl.BlockSpec(memory_space=pltpu.VMEM)
    hbm = pl.BlockSpec(memory_space=pl.ANY)
    scratch = [((2, 4, 4, 4, rows, 128), BF16) for rows in PARTS]
    scratch += [((4, 4, 4, rows, 128), BF16) for rows in PARTS]
    scratch += [((3, 4, 4, rows, 128), BF16) for rows in PARTS]
    scratch += [((3, 4, rows, 128), BF16) for rows in PARTS]
    scratch += [((3, rows, 128), BF16) for rows in PARTS]
    scratch += [
        ((BLOCK, 128), F32),
        ((ROWS, D), BF16),
        ((ROWS, D), BF16),
        ((ROWS, D), BF16),
        ((FLAT_ROWS, 128), F32),
        ((D, 6 * D), BF16),
        ((D, 3 * D), BF16),
        ((D, D), BF16),
        ((D, FF), BF16),
        ((FF, D), BF16),
        ((8, 5760), F32),
        ((16, D), F32),
        ((16, 6 * D), F32),
        ((16, 6 * D), F32),
        ((ROWS, D), F32),
        ((ROWS, 1), F32),
        ((ROWS, 3 * D), BF16),
        ((LATENTS * HEADS, SEQ, SEQ), BF16),
        ((D, ROWS), BF16),
        ((D, ROWS), BF16),
        ((ROWS, D), F32),
        ((ROWS, D), F32),
        ((D, ROWS), BF16),
        ((ROWS, FF), BF16),
        ((2 * SEQ, FF), F32),
        ((ROWS, D), BF16),
        ((ROWS, FF), BF16),
        ((ROWS, D), BF16),
        ((ROWS, D), BF16),
    ]
    sems = [(2,), (2, 4), (3, 3, 3), (3, 3, 3), (3, 4), (3, 4), (3, 4), (3, 4), (3, 3, 3), (3, 3, 3)]
    return pl.pallas_call(
        whole_kernel,
        out_shape=[
            jax.ShapeDtypeStruct((ROWS, D), BF16),
            jax.ShapeDtypeStruct((ROWS, D), F32),
            jax.ShapeDtypeStruct((LATENTS, D), F32),
            jax.ShapeDtypeStruct((BLOCK, 128), F32),
        ],
        in_specs=[vmem, vmem, hbm, hbm],
        out_specs=[hbm, hbm, vmem, vmem],
        scratch_shapes=[pltpu.VMEM(shape, dtype) for shape, dtype in scratch]
        + [pltpu.SemaphoreType.DMA(shape) for shape in sems],
        compiler_params=pltpu.CompilerParams(
            collective_id=0, has_side_effects=True, vmem_limit_bytes=61 * 1024 * 1024
        ),
        name="block",
    )(piece, cond, tokens, d_out)


def hand_over_kernel(*refs):
    sources, targets, middles, (into, out_of) = refs[:3], refs[3:6], refs[6:9], refs[9:]
    firsts, seconds = [], []
    for number, (source, middle, target) in enumerate(zip(sources, middles, targets)):
        pieces = 4 if source.shape[0] == ROWS else 1
        rows = source.shape[0] // pieces
        for piece in range(pieces):
            here = pl.ds(piece * rows, rows)
            firsts.append(
                pltpu.make_async_copy(source.at[here], middle.at[here], into.at[number, piece])
            )
            seconds.append(
                pltpu.make_async_copy(middle.at[here], target.at[here], out_of.at[number, piece])
            )
    for copy in firsts:
        copy.start()
    for first, second in zip(firsts, seconds):
        first.wait()
        second.start()
    for copy in seconds:
        copy.wait()


def hand_over(*results):
    hbm = pl.BlockSpec(memory_space=pl.ANY)
    return pl.pallas_call(
        hand_over_kernel,
        out_shape=[jax.ShapeDtypeStruct(result.shape, result.dtype) for result in results],
        in_specs=[hbm] * 3,
        out_specs=[hbm] * 3,
        scratch_shapes=[pltpu.VMEM(result.shape, result.dtype) for result in results]
        + [pltpu.SemaphoreType.DMA((3, 4))] * 2,
        compiler_params=pltpu.CompilerParams(vmem_limit_bytes=63 * 1024 * 1024),
        name="hand_over",
    )(*results)


def local(tokens, cond, params, d_out):
    piece = jnp.pad(params, (0, BLOCK * 128 - SHARD)).reshape(BLOCK, 128)
    out, d_tokens, d_cond, summed = transformer_block(piece, cond, tokens, d_out)
    out, d_tokens, d_cond = hand_over(out, d_tokens, d_cond)
    return out, d_tokens, d_cond, summed.reshape(-1)[:SHARD]


def solution(mesh):
    placed = (P("dev", None), P("dev", None), P("dev"), P("dev", None))
    return jax.shard_map(
        local,
        mesh=mesh,
        in_specs=placed,
        out_specs=(P("dev", None), P("dev", None), P("dev", None), P("dev")),
        check_vma=False,
    )
```
